512 devices in a mesh: clip: 16 (over x, y), seq: 32 (over z, core).
Axes of the slice: x: 4, y: 4, z: 16, core: 2. Of those that a mesh axis runs over, the one named last changes fastest.
Arguments:
- clip_in: bfloat16 [16, 64, 64, 8, 128], P('clip', 'seq'), may hold values from -6 to 6
- first_plane: bfloat16 [3, 3, 128, 128], replicated, may hold values from -0.1875 to 0.1875
- first_time: bfloat16 [3, 128, 128], replicated, may hold values from -0.3125 to 0.3125
- down_plane: bfloat16 [3, 3, 128, 256], replicated, may hold values from -0.1875 to 0.1875
- down_time: bfloat16 [3, 256, 256], replicated, may hold values from -0.21875 to 0.21875
- last_time: bfloat16 [3, 256, 256], replicated, may hold values from -0.21875 to 0.21875
- cotan_out: bfloat16 [16, 32, 32, 4, 256], P('clip', None, 'seq'), may hold values from -6 to 6
Outputs:
- output: bfloat16 [16, 32, 32, 4, 256], P('clip', None, 'seq')
- grad_first_plane: bfloat16 [3, 3, 128, 128], replicated
- grad_first_time: bfloat16 [3, 128, 128], replicated
- grad_down_plane: bfloat16 [3, 3, 128, 256], replicated
- grad_down_time: bfloat16 [3, 256, 256], replicated
- grad_last_time: bfloat16 [3, 256, 256], replicated
The draws below stay inside these ranges and needn't reach their ends.
All inputs are finite; a program needn't handle non-finite values.
Results may differ from the reference program's by a relative error of at most 0.014.
Values may be sent and summed in bfloat16 or wider, within the bound.
No kernel may reach another device: no remote copies, remote signals or barrier semaphores. Data moves between devices by JAX's collectives and lax.ppermute only.
A program may use at most 64 MiB of HBM per device.

```python
import jax
import jax.numpy as jnp
from jax import lax

CH_IN = 128
CH_OUT = 256
WIDTH_CELLS = 8
CLIPS = 16
FRAMES = 64
HEIGHT = 64


def steps_of(own_key, extent, split, least, top_value):
    def one(axis_at, parts):
        heights = jax.random.uniform(jax.random.fold_in(jax.random.fold_in(own_key, 6), axis_at), (parts,), jnp.float32, least / len(split), top_value / len(split))
        return jnp.repeat(jnp.exp(heights), extent[axis_at] // parts).reshape((-1,) + (1,) * (len(extent) - axis_at - 1))

    loudness = one(*split[0])
    for cut in split[1:]:
        loudness = loudness * one(*cut)
    return loudness


def scatter_about(stream_key, extent, width, most, split=(), kind=jnp.bfloat16):
    array = jax.random.normal(stream_key, extent, jnp.float32) * width
    if len(split) > 0:
        array = steps_of(stream_key, extent, split, -0.22, 0.18) * array
    return jnp.clip(array, min=-most, max=most).astype(kind)


def setup_inputs(seed: int = 0) -> dict:
    keys = jax.random.split(jax.random.key(seed), 8)
    clip_in = scatter_about(keys[0], (CLIPS, FRAMES, HEIGHT, WIDTH_CELLS, CH_IN), 1.0, 6.0, ((0, 16), (1, 32)))
    first_plane = scatter_about(keys[1], (3, 3, CH_IN, CH_IN), (9 * CH_IN) ** -0.5, 0.1875)
    first_time = scatter_about(keys[2], (3, CH_IN, CH_IN), (3 * CH_IN) ** -0.5, 0.3125)
    down_plane = scatter_about(keys[3], (3, 3, CH_IN, CH_OUT), (9 * CH_IN) ** -0.5, 0.1875)
    down_time = scatter_about(keys[4], (3, CH_OUT, CH_OUT), (3 * CH_OUT) ** -0.5, 0.21875)
    last_time = scatter_about(keys[5], (3, CH_OUT, CH_OUT), (3 * CH_OUT) ** -0.5, 0.21875)
    cotan_out = scatter_about(keys[6], (CLIPS, FRAMES // 2, HEIGHT // 2, WIDTH_CELLS // 2, CH_OUT), 1.0, 6.0, ((0, 16), (2, 32)))
    return dict(clip_in=clip_in, first_plane=first_plane, first_time=first_time, down_plane=down_plane, down_time=down_time, last_time=last_time, cotan_out=cotan_out)


def plane_conv(source, kernel, stride):
    num_frames, num_rows, num_cols, num_chans = source.shape
    padded = jnp.pad(source, ((0, 0), (1, 1), (1, 1), (0, 0)))
    out_rows = num_rows // stride
    out_cols = num_cols // stride
    summed = jnp.zeros((num_frames * out_rows * out_cols, kernel.shape[3]), jnp.float32)
    for row_tap in range(3):
        for col_tap in range(3):
            window = padded[:, row_tap:row_tap + num_rows:stride, col_tap:col_tap + num_cols:stride, :]
            summed = summed + jnp.dot(window.reshape(-1, num_chans), kernel[row_tap, col_tap], preferred_element_type=jnp.float32)
    return summed.reshape(num_frames, out_rows, out_cols, kernel.shape[3])

def plane_conv_grad(source, cotan, stride):
    num_frames, num_rows, num_cols, num_chans = source.shape
    padded = jnp.pad(source, ((0, 0), (1, 1), (1, 1), (0, 0)))
    flat_cotan = cotan.reshape(-1, cotan.shape[3])
    result = []
    for row_tap in range(3):
        row_list = []
        for col_tap in range(3):
            window = padded[:, row_tap:row_tap + num_rows:stride, col_tap:col_tap + num_cols:stride, :]
            row_list.append(jnp.dot(window.reshape(-1, num_chans).T, flat_cotan, preferred_element_type=jnp.float32))
        result.append(jnp.stack(row_list, axis=0))
    return jnp.stack(result, axis=0)

def plane_back_strided(cotan, kernel):
    num_frames, half_rows, half_cols, num_chans = cotan.shape
    padded = jnp.pad(cotan, ((0, 0), (0, 1), (0, 1), (0, 0)))
    taps_by_parity = (((1, 0),), ((0, 1), (2, 0)))
    blocks = []
    for row_par in range(2):
        row_blocks = []
        for col_par in range(2):
            summed = jnp.zeros((num_frames * half_rows * half_cols, kernel.shape[2]), jnp.float32)
            for row_tap, row_off in taps_by_parity[row_par]:
                for col_tap, col_off in taps_by_parity[col_par]:
                    window = padded[:, row_off:row_off + half_rows, col_off:col_off + half_cols, :]
                    summed = summed + jnp.dot(window.reshape(-1, num_chans), kernel[row_tap, col_tap].T, preferred_element_type=jnp.float32)
            row_blocks.append(summed.reshape(num_frames, half_rows, half_cols, kernel.shape[2]))
        blocks.append(jnp.stack(row_blocks, axis=3))
    stacked = jnp.stack(blocks, axis=2)
    return stacked.reshape(num_frames, 2 * half_rows, 2 * half_cols, kernel.shape[2])

def time_conv(extended, kernel, stride):
    num_out = (extended.shape[0] - 2) // stride
    num_chans = extended.shape[-1]
    summed = jnp.zeros((num_out * extended.shape[1] * extended.shape[2], kernel.shape[2]), jnp.float32)
    for tap_index in range(3):
        taps = extended[tap_index:tap_index + stride * num_out:stride]
        summed = summed + jnp.dot(taps.reshape(-1, num_chans), kernel[tap_index], preferred_element_type=jnp.float32)
    return summed.reshape(num_out, extended.shape[1], extended.shape[2], kernel.shape[2])

def time_conv_grad(extended, cotan, stride):
    num_out = cotan.shape[0]
    flat_cotan = cotan.reshape(-1, cotan.shape[3])
    result = []
    for tap_index in range(3):
        taps = extended[tap_index:tap_index + stride * num_out:stride]
        result.append(jnp.dot(taps.reshape(-1, extended.shape[3]).T, flat_cotan, preferred_element_type=jnp.float32))
    return jnp.stack(result, axis=0)

def time_back_one(ahead, kernel):
    num_frames = ahead.shape[0] - 2
    summed = jnp.zeros((num_frames * ahead.shape[1] * ahead.shape[2], kernel.shape[1]), jnp.float32)
    for tap_index in range(3):
        taps = ahead[2 - tap_index:2 - tap_index + num_frames]
        summed = summed + jnp.dot(taps.reshape(-1, ahead.shape[3]), kernel[tap_index].T, preferred_element_type=jnp.float32)
    return summed.reshape(num_frames, ahead.shape[1], ahead.shape[2], kernel.shape[1])

def time_back_two(ahead, kernel):
    num_frames = ahead.shape[0] - 1
    num_chans = ahead.shape[3]
    current = ahead[:num_frames].reshape(-1, num_chans)
    following = ahead[1:].reshape(-1, num_chans)
    even_part = jnp.dot(current, kernel[2].T, preferred_element_type=jnp.float32) + jnp.dot(following, kernel[0].T, preferred_element_type=jnp.float32)
    odd_part = jnp.dot(following, kernel[1].T, preferred_element_type=jnp.float32)
    shape_one = (num_frames, ahead.shape[1], ahead.shape[2], kernel.shape[1])
    stacked = jnp.stack([even_part.reshape(shape_one), odd_part.reshape(shape_one)], axis=1)
    return stacked.reshape(2 * num_frames, ahead.shape[1], ahead.shape[2], kernel.shape[1])

def silu_slope(preact):
    sigma = jax.nn.sigmoid(preact)
    return sigma * (1.0 + preact * (1.0 - sigma))

def zero_frames(count, like):
    return jnp.zeros((count,) + like.shape[1:], like.dtype)

def one_clip(source, cotan, first_plane, first_time, down_plane, down_time, last_time):
    pre_first = plane_conv(source, first_plane, 1)
    hidden = jax.nn.silu(pre_first).astype(jnp.bfloat16)
    hidden_ext = jnp.concatenate([zero_frames(2, hidden), hidden], axis=0)
    mixed = (source.astype(jnp.float32) + time_conv(hidden_ext, first_time, 1)).astype(jnp.bfloat16)
    strided = plane_conv(mixed, down_plane, 2).astype(jnp.bfloat16)
    strided_ext = jnp.concatenate([zero_frames(2, strided), strided], axis=0)
    pre_down = time_conv(strided_ext, down_time, 2)
    lowered = jax.nn.silu(pre_down).astype(jnp.bfloat16)
    lowered_ext = jnp.concatenate([zero_frames(2, lowered), lowered], axis=0)
    output = (lowered.astype(jnp.float32) + time_conv(lowered_ext, last_time, 1)).astype(jnp.bfloat16)
    grad_last = time_conv_grad(lowered_ext, cotan, 1)
    cotan_ext = jnp.concatenate([cotan, zero_frames(2, cotan)], axis=0)
    grad_lowered = (cotan.astype(jnp.float32) + time_back_one(cotan_ext, last_time)).astype(jnp.bfloat16)
    grad_pre = (grad_lowered.astype(jnp.float32) * silu_slope(pre_down)).astype(jnp.bfloat16)
    grad_down_time = time_conv_grad(strided_ext, grad_pre, 2)
    pre_ext = jnp.concatenate([grad_pre, zero_frames(1, grad_pre)], axis=0)
    grad_strided = time_back_two(pre_ext, down_time).astype(jnp.bfloat16)
    grad_down_plane = plane_conv_grad(mixed, grad_strided, 2)
    grad_mixed = plane_back_strided(grad_strided, down_plane).astype(jnp.bfloat16)
    grad_first_time = time_conv_grad(hidden_ext, grad_mixed, 1)
    mixed_ext = jnp.concatenate([grad_mixed, zero_frames(2, grad_mixed)], axis=0)
    grad_hidden = time_back_one(mixed_ext, first_time)
    grad_first_pre = (grad_hidden * silu_slope(pre_first)).astype(jnp.bfloat16)
    grad_first_plane = plane_conv_grad(source, grad_first_pre, 1)
    return (output, (grad_first_plane, grad_first_time, grad_down_plane, grad_down_time, grad_last))

def reference(clip_in, first_plane, first_time, down_plane, down_time, last_time, cotan_out):

    def one_step(carry, pair):
        output, grads = one_clip(pair[0], pair[1], first_plane, first_time, down_plane, down_time, last_time)
        return (tuple((left + right for left, right in zip(carry, grads))), output)
    start = (jnp.zeros(first_plane.shape, jnp.float32), jnp.zeros(first_time.shape, jnp.float32), jnp.zeros(down_plane.shape, jnp.float32), jnp.zeros(down_time.shape, jnp.float32), jnp.zeros(last_time.shape, jnp.float32))
    sums, outputs = lax.scan(one_step, start, (clip_in, cotan_out))
    return (outputs, sums[0].astype(jnp.bfloat16), sums[1].astype(jnp.bfloat16), sums[2].astype(jnp.bfloat16), sums[3].astype(jnp.bfloat16), sums[4].astype(jnp.bfloat16))
```

```python
import jax
import jax.numpy as jnp
from jax import lax
from jax.sharding import PartitionSpec as P


def from_behind(block, axis, distance):
    devices = range(lax.axis_size(axis))
    route = [(i - distance, i) for i in devices if i - distance in devices]
    return lax.ppermute(block, axis, route)


def plane_conv(source, kernel, stride):
    num_frames, num_rows, num_cols, num_chans = source.shape
    padded = jnp.pad(source, ((0, 0), (1, 1), (1, 1), (0, 0)))
    out_rows = num_rows // stride
    out_cols = num_cols // stride
    summed = jnp.zeros((num_frames * out_rows * out_cols, kernel.shape[3]), jnp.float32)
    for row_tap in range(3):
        for col_tap in range(3):
            window = padded[
                :, row_tap : row_tap + num_rows : stride, col_tap : col_tap + num_cols : stride, :
            ]
            summed = summed + jnp.dot(
                window.reshape(-1, num_chans),
                kernel[row_tap, col_tap],
                preferred_element_type=jnp.float32,
            )
    return summed.reshape(num_frames, out_rows, out_cols, kernel.shape[3])


def plane_conv_grad(source, cotan, stride):
    num_frames, num_rows, num_cols, num_chans = source.shape
    padded = jnp.pad(source, ((0, 0), (1, 1), (1, 1), (0, 0)))
    flat_cotan = cotan.reshape(-1, cotan.shape[3])
    result = []
    for row_tap in range(3):
        row_list = []
        for col_tap in range(3):
            window = padded[
                :, row_tap : row_tap + num_rows : stride, col_tap : col_tap + num_cols : stride, :
            ]
            row_list.append(
                jnp.dot(
                    window.reshape(-1, num_chans).T, flat_cotan, preferred_element_type=jnp.float32
                )
            )
        result.append(jnp.stack(row_list, axis=0))
    return jnp.stack(result, axis=0)


def plane_back_strided(cotan, kernel):
    num_frames, half_rows, half_cols, num_chans = cotan.shape
    padded = jnp.pad(cotan, ((0, 0), (0, 1), (0, 1), (0, 0)))
    taps_by_parity = (((1, 0),), ((0, 1), (2, 0)))
    blocks = []
    for row_par in range(2):
        row_blocks = []
        for col_par in range(2):
            summed = jnp.zeros((num_frames * half_rows * half_cols, kernel.shape[2]), jnp.float32)
            for row_tap, row_off in taps_by_parity[row_par]:
                for col_tap, col_off in taps_by_parity[col_par]:
                    window = padded[
                        :, row_off : row_off + half_rows, col_off : col_off + half_cols, :
                    ]
                    summed = summed + jnp.dot(
                        window.reshape(-1, num_chans),
                        kernel[row_tap, col_tap].T,
                        preferred_element_type=jnp.float32,
                    )
            row_blocks.append(summed.reshape(num_frames, half_rows, half_cols, kernel.shape[2]))
        blocks.append(jnp.stack(row_blocks, axis=3))
    stacked = jnp.stack(blocks, axis=2)
    return stacked.reshape(num_frames, 2 * half_rows, 2 * half_cols, kernel.shape[2])


def time_conv(extended, kernel, stride):
    num_out = (extended.shape[0] - 2) // stride
    num_chans = extended.shape[-1]
    summed = jnp.zeros(
        (num_out * extended.shape[1] * extended.shape[2], kernel.shape[2]), jnp.float32
    )
    for tap_index in range(3):
        taps = extended[tap_index : tap_index + stride * num_out : stride]
        summed = summed + jnp.dot(
            taps.reshape(-1, num_chans), kernel[tap_index], preferred_element_type=jnp.float32
        )
    return summed.reshape(num_out, extended.shape[1], extended.shape[2], kernel.shape[2])


def time_conv_grad(extended, cotan, stride):
    num_out = cotan.shape[0]
    flat_cotan = cotan.reshape(-1, cotan.shape[3])
    result = []
    for tap_index in range(3):
        taps = extended[tap_index : tap_index + stride * num_out : stride]
        result.append(
            jnp.dot(
                taps.reshape(-1, extended.shape[3]).T,
                flat_cotan,
                preferred_element_type=jnp.float32,
            )
        )
    return jnp.stack(result, axis=0)


def time_back_one(ahead, kernel):
    num_frames = ahead.shape[0] - 2
    summed = jnp.zeros((num_frames * ahead.shape[1] * ahead.shape[2], kernel.shape[1]), jnp.float32)
    for tap_index in range(3):
        taps = ahead[2 - tap_index : 2 - tap_index + num_frames]
        summed = summed + jnp.dot(
            taps.reshape(-1, ahead.shape[3]),
            kernel[tap_index].T,
            preferred_element_type=jnp.float32,
        )
    return summed.reshape(num_frames, ahead.shape[1], ahead.shape[2], kernel.shape[1])


def time_back_two(ahead, kernel):
    num_frames = ahead.shape[0] - 1
    num_chans = ahead.shape[3]
    current = ahead[:num_frames].reshape(-1, num_chans)
    following = ahead[1:].reshape(-1, num_chans)
    even_part = jnp.dot(current, kernel[2].T, preferred_element_type=jnp.float32) + jnp.dot(
        following, kernel[0].T, preferred_element_type=jnp.float32
    )
    odd_part = jnp.dot(following, kernel[1].T, preferred_element_type=jnp.float32)
    shape_one = (num_frames, ahead.shape[1], ahead.shape[2], kernel.shape[1])
    stacked = jnp.stack([even_part.reshape(shape_one), odd_part.reshape(shape_one)], axis=1)
    return stacked.reshape(2 * num_frames, ahead.shape[1], ahead.shape[2], kernel.shape[1])


def silu_slope(preact):
    sigma = jax.nn.sigmoid(preact)
    return sigma * (1.0 + preact * (1.0 - sigma))


def zero_frames(count, like):
    return jnp.zeros((count,) + like.shape[1:], like.dtype)


def last_section(lowered, cotan, last_time):
    lowered_ext = jnp.concatenate([zero_frames(2, lowered), lowered], axis=0)
    output = (lowered.astype(jnp.float32) + time_conv(lowered_ext, last_time, 1)).astype(
        jnp.bfloat16
    )
    grad_last = time_conv_grad(lowered_ext, cotan, 1)
    cotan_ext = jnp.concatenate([cotan, zero_frames(2, cotan)], axis=0)
    grad_lowered = (cotan.astype(jnp.float32) + time_back_one(cotan_ext, last_time)).astype(
        jnp.bfloat16
    )
    return (output, grad_last, grad_lowered)


def swap_cores(block):
    count = lax.axis_size("seq")
    return lax.ppermute(block, "seq", [(i, i ^ 1) for i in range(count)])


def exchange_clip(blocks):
    return lax.all_to_all(blocks, "clip", split_axis=0, concat_axis=0, tiled=True)


def exchange_depth(blocks):
    count = lax.axis_size("seq")
    groups = [list(range(core, count, 2)) for core in range(2)]
    return lax.all_to_all(
        blocks, "seq", split_axis=0, concat_axis=0, axis_index_groups=groups, tiled=True
    )


def sum_blocks(blocks):
    return jnp.sum(blocks.astype(jnp.float32), axis=0)


def sum_everywhere(grads):
    clips = lax.axis_size("clip")
    chips = lax.axis_size("seq") // 2
    core = lax.axis_index("seq") % 2
    flat = jnp.concatenate([grad.reshape(-1, 128) for grad in grads], axis=0)
    num_rows = flat.shape[0]
    halves = flat.reshape(2, num_rows // 2, 128)
    mine = lax.dynamic_index_in_dim(halves, core, 0, keepdims=False)
    other = lax.dynamic_index_in_dim(halves, 1 - core, 0, keepdims=False)
    other = swap_cores(other.astype(jnp.bfloat16))
    half = (mine + other.astype(jnp.float32)).astype(jnp.bfloat16)
    part = sum_blocks(exchange_clip(half.reshape(clips, -1, 128)))
    part_rows = part.shape[0]
    chunk = 16 * (-(-part_rows // (16 * chips)))
    part = jnp.pad(part, ((0, chunk * chips - part_rows), (0, 0))).astype(jnp.bfloat16)
    piece = sum_blocks(exchange_depth(part.reshape(chips, chunk, 128))).astype(jnp.bfloat16)
    part = exchange_depth(jnp.broadcast_to(piece[None], (chips, chunk, 128)))
    part = part.reshape(-1, 128)[:part_rows]
    half = exchange_clip(jnp.broadcast_to(part[None], (clips, part_rows, 128)))
    half = half.reshape(-1, 128)
    other = swap_cores(half)
    first = jnp.where(core == 0, half, other)
    second = jnp.where(core == 0, other, half)
    whole = jnp.concatenate([first, second], axis=0)
    result = []
    start = 0
    for grad in grads:
        rows = grad.size // 128
        result.append(whole[start : start + rows].reshape(grad.shape))
        start += rows
    return tuple(result)


def local(clip_in, first_plane, first_time, down_plane, down_time, last_time, cotan_out):
    source = clip_in[0]
    cotan = cotan_out[0]
    pre_first = plane_conv(source, first_plane, 1)
    hidden = jax.nn.silu(pre_first).astype(jnp.bfloat16)
    hidden_prior = from_behind(hidden, "seq", 1)
    hidden_ext = jnp.concatenate([hidden_prior, hidden], axis=0)
    mixed = (source.astype(jnp.float32) + time_conv(hidden_ext, first_time, 1)).astype(jnp.bfloat16)
    strided = plane_conv(mixed, down_plane, 2).astype(jnp.bfloat16)
    strided_prior = from_behind(strided, "seq", 1)
    strided_ext = jnp.concatenate([strided_prior, strided], axis=0)
    pre_down = time_conv(strided_ext, down_time, 2)
    lowered = jax.nn.silu(pre_down).astype(jnp.bfloat16)
    lowered_rows = lax.all_to_all(lowered, "seq", split_axis=1, concat_axis=0, tiled=True)
    output, grad_last, grad_rows = last_section(lowered_rows, cotan, last_time)
    grad_lowered = lax.all_to_all(grad_rows, "seq", split_axis=0, concat_axis=1, tiled=True)
    grad_pre = (grad_lowered.astype(jnp.float32) * silu_slope(pre_down)).astype(jnp.bfloat16)
    grad_down_time = time_conv_grad(strided_ext, grad_pre, 2)
    pre_next = from_behind(grad_pre, "seq", -1)
    pre_ext = jnp.concatenate([grad_pre, pre_next], axis=0)
    grad_strided = time_back_two(pre_ext, down_time).astype(jnp.bfloat16)
    grad_down_plane = plane_conv_grad(mixed, grad_strided, 2)
    grad_mixed = plane_back_strided(grad_strided, down_plane).astype(jnp.bfloat16)
    grad_first_time = time_conv_grad(hidden_ext, grad_mixed, 1)
    mixed_next = from_behind(grad_mixed, "seq", -1)
    mixed_ext = jnp.concatenate([grad_mixed, mixed_next], axis=0)
    grad_hidden = time_back_one(mixed_ext, first_time)
    grad_first_pre = (grad_hidden * silu_slope(pre_first)).astype(jnp.bfloat16)
    grad_first_plane = plane_conv_grad(source, grad_first_pre, 1)
    sums = sum_everywhere(
        (grad_first_plane, grad_first_time, grad_down_plane, grad_down_time, grad_last)
    )
    return (output[None],) + sums


def solution(mesh):
    placed = (
        P("clip", "seq", None, None, None),
        P(),
        P(),
        P(),
        P(),
        P(),
        P("clip", None, "seq", None, None),
    )
    return jax.shard_map(
        local,
        mesh=mesh,
        in_specs=placed,
        out_specs=(P("clip", None, "seq", None, None), P(), P(), P(), P(), P()),
        check_vma=False,
    )
```

```python
import functools

import jax
import jax.numpy as jnp
from jax import lax
from jax.experimental import pallas as pl
from jax.experimental.pallas import tpu as pltpu
from jax.sharding import PartitionSpec as P


F32 = jnp.float32
BF16 = jnp.bfloat16
COLS = 8
HALF = 32
CELLS = COLS * HALF
DOWN = CELLS // 2
CH = 128
WIDE = 256


def dot(left, right):
    return lax.dot_general(left, right, (((1,), (0,)), ((), ())), preferred_element_type=F32)


def dot_nt(left, right):
    return lax.dot_general(left, right, (((1,), (1,)), ((), ())), preferred_element_type=F32)


def dot_tn(left, right):
    return lax.dot_general(left, right, (((0,), (0,)), ((), ())), preferred_element_type=F32)


def call(body, outs, scratch, *args, smem=0, flops=0):
    spaces = [pltpu.SMEM] * smem + [pltpu.VMEM] * (len(args) - smem)
    return pl.pallas_call(
        body,
        out_shape=[jax.ShapeDtypeStruct(shape, kind) for shape, kind in outs],
        in_specs=[pl.BlockSpec(memory_space=space) for space in spaces],
        out_specs=[pl.BlockSpec(memory_space=pltpu.VMEM) for _ in outs],
        scratch_shapes=[pltpu.VMEM(shape, kind) for shape, kind in scratch],
        compiler_params=pltpu.CompilerParams(vmem_limit_bytes=40 * 1024 * 1024),
        cost_estimate=pl.CostEstimate(flops=flops, bytes_accessed=4000000, transcendentals=0),
    )(*args)


def row_before(planes):
    wide = planes.astype(F32)
    rolled = pltpu.roll(wide, 1, 1)
    at = lax.broadcasted_iota(jnp.int32, wide.shape, 1)
    return jnp.where(at == 0, 0.0, rolled).astype(BF16)


def row_after(planes):
    wide = planes.astype(F32)
    rolled = pltpu.roll(wide, HALF - 1, 1)
    at = lax.broadcasted_iota(jnp.int32, wide.shape, 1)
    return jnp.where(at == HALF - 1, 0.0, rolled).astype(BF16)


def fill_windows(windows, at, even, odd):
    by_row = (row_before(odd), even, odd, row_after(even))
    edge = jnp.zeros((HALF, CH), BF16)
    for row, planes in enumerate(by_row):
        flat = planes.reshape(CELLS, CH)
        for tap in range(3):
            lanes = pl.ds((tap * 4 + row) * CH, CH)
            if tap == 0:
                windows[pl.ds(at, HALF), lanes] = edge
                windows[pl.ds(at + HALF, CELLS - HALF), lanes] = flat[: CELLS - HALF]
            elif tap == 1:
                windows[pl.ds(at, CELLS), lanes] = flat
            else:
                windows[pl.ds(at, CELLS - HALF), lanes] = flat[HALF:]
                windows[pl.ds(at + CELLS - HALF, HALF), lanes] = edge


def silu_slope(preact):
    sigma = jax.nn.sigmoid(preact)
    return sigma * (1.0 + preact * (1.0 - sigma))


def first_body(
    prior, own, first_plane, first_time, down_plane,
    pre_out, hidden_out, cells_out, strided_out,
    windows, both,
):
    both[...] = jnp.zeros_like(both)
    for tap in range(3):
        for row in range(4):
            rows = pl.ds((tap * 4 + row) * CH, CH)
            if row < 3:
                both[rows, pl.ds(0, CH)] = first_plane[row, tap]
            if row > 0:
                both[rows, pl.ds(CH, CH)] = first_plane[row - 1, tap]
    for frame in range(4):
        source = prior if frame < 2 else own
        fill_windows(windows, frame * CELLS, source[frame % 2, 0], source[frame % 2, 1])
    for frame in range(4):
        pre = dot(windows[pl.ds(frame * CELLS, CELLS), :], both[...])
        hid = (pre * jax.nn.sigmoid(pre)).astype(BF16)
        for par in range(2):
            hidden_out[frame, par] = hid[:, par * CH : (par + 1) * CH]
            if frame >= 2:
                pre_out[frame - 2, par] = pre[:, par * CH : (par + 1) * CH]
    times = first_time[...].reshape(3 * CH, CH)
    for frame in range(2):
        mixed = []
        for par in range(2):
            taps = jnp.concatenate([hidden_out[frame + k, par] for k in range(3)], axis=1)
            here = own[frame, par].reshape(CELLS, CH).astype(F32) + dot(taps, times)
            mixed.append(here.astype(BF16).reshape(COLS, HALF, CH))
        by_row = (row_before(mixed[1]), mixed[0], mixed[1])
        for row in range(3):
            for tap in range(3):
                lanes = pl.ds((row * 3 + tap) * CH, CH)
                for col in range(COLS // 2):
                    rows = pl.ds(frame * DOWN + col * HALF, HALF)
                    where = 2 * col + tap - 1
                    if where < 0:
                        cells_out[rows, lanes] = jnp.zeros((HALF, CH), BF16)
                    else:
                        cells_out[rows, lanes] = by_row[row][where]
    kernel = down_plane[...].reshape(9 * CH, WIDE)
    strided_out[...] = dot(cells_out[...], kernel).astype(BF16).reshape(2, DOWN, WIDE)


def middle_body(
    prior, own, cotans, down_time, last_time,
    lowered_out, grad_pre_out, grad_down_time_out, grad_last_out,
    spread, turned,
):
    spread[...] = cotans[...].reshape(HALF * 24, CH).astype(F32)
    cot = []
    for ahead in range(3):
        parts = []
        for col in range(4):
            halves = [
                spread[pl.ds(ahead * 8 + col * 2 + half, HALF, stride=24), :] for half in range(2)
            ]
            parts.append(jnp.concatenate(halves, axis=1))
        cot.append(jnp.concatenate(parts, axis=0).astype(BF16))
    grad_lowered = cot[0].astype(F32)
    for k in range(3):
        grad_lowered = grad_lowered + dot_nt(cot[2 - k], last_time[k])
    grad_lowered = grad_lowered.astype(BF16)
    taps = (prior[0], prior[1], own[0])
    pre = dot(taps[0], down_time[0]) + dot(taps[1], down_time[1]) + dot(taps[2], down_time[2])
    lowered = (pre * jax.nn.sigmoid(pre)).astype(BF16)
    grad_pre = (grad_lowered.astype(F32) * silu_slope(pre)).astype(BF16)
    grad_pre_out[...] = grad_pre
    wide = lowered.astype(F32)
    for col in range(4):
        for half in range(2):
            turned[pl.ds(col * 2 + half, HALF, stride=8), :] = wide[
                col * HALF : (col + 1) * HALF, half * CH : (half + 1) * CH
            ]
    lowered_out[...] = turned[...].astype(BF16).reshape(HALF, 8, CH)
    for k in range(3):
        down = dot_tn(taps[k], grad_pre)
        last = dot_tn(lowered, cot[2 - k])
        for half in range(2):
            lanes = slice(half * CH, (half + 1) * CH)
            grad_down_time_out[half, pl.ds(k * WIDE, WIDE), :] = down[:, lanes]
            grad_last_out[half, pl.ds(k * WIDE, WIDE), :] = last[:, lanes]


BACK = (
    (0, 0, 0, 0, 1, 1),
    (0, 1, 0, 1, 1, 0),
    (0, 1, 0, 0, 1, 2),
    (1, 0, 1, 0, 0, 1),
    (1, 0, 0, 0, 2, 1),
    (1, 1, 1, 1, 0, 0),
    (1, 1, 1, 0, 0, 2),
    (1, 1, 0, 1, 2, 0),
    (1, 1, 0, 0, 2, 2),
)


def back_body(
    own, ahead, down_time, down_plane, cells, hidden,
    grad_mixed_out, grad_first_time_out, grad_down_plane_out,
    shifted, kernels,
):
    current, following = own[...], ahead[...]
    even = dot_nt(current, down_time[2]) + dot_nt(following, down_time[0])
    odd = dot_nt(following, down_time[1])
    strided = [even.astype(BF16), odd.astype(BF16)]
    kernels[...] = jnp.zeros_like(kernels)
    for row_par, col_par, row_off, col_off, row, tap in BACK:
        rows = pl.ds((row_par * 2 + col_par) * CH, CH)
        lanes = pl.ds((row_off * 2 + col_off) * WIDE, WIDE)
        kernels[rows, lanes] = down_plane[row, tap]
    for frame in range(2):
        planes = strided[frame].reshape(4, HALF, WIDE)
        for row_off, rows in ((0, planes), (1, row_after(planes))):
            flat = rows.reshape(DOWN, WIDE)
            here = pl.ds((row_off * 2) * WIDE, WIDE)
            after = pl.ds((row_off * 2 + 1) * WIDE, WIDE)
            shifted[pl.ds(frame * DOWN, DOWN), here] = flat
            shifted[pl.ds(frame * DOWN, DOWN - HALF), after] = flat[HALF:]
            shifted[pl.ds(frame * DOWN + DOWN - HALF, HALF), after] = jnp.zeros((HALF, WIDE), BF16)
    mixed = dot_nt(shifted[...], kernels[...]).astype(BF16)
    for frame in range(2):
        for par in range(2):
            for col_par in range(2):
                lanes = slice((par * 2 + col_par) * CH, (par * 2 + col_par + 1) * CH)
                for col in range(4):
                    rows = slice(frame * DOWN + col * HALF, frame * DOWN + (col + 1) * HALF)
                    grad_mixed_out[frame, par, 2 * col + col_par] = mixed[rows, lanes]
    both = jnp.concatenate(strided, axis=0)
    down = dot_tn(cells[...], both)
    for half in range(2):
        grad_down_plane_out[half] = down[:, half * CH : (half + 1) * CH]
    cotan = grad_mixed_out[...].reshape(4 * CELLS, CH)
    for k in range(3):
        taps = hidden[pl.ds(k, 2)].reshape(4 * CELLS, CH)
        grad_first_time_out[pl.ds(k * CH, CH), :] = dot_tn(taps, cotan)


def last_body(
    core, own, ahead, first_time, pre, source, grad_first_time, grad_down_plane, grad_down_time, grad_last,
    mine_out, other_out,
    windows, flat,
):
    frames = [own[0], own[1], ahead[0], ahead[1]]
    kernels = jnp.concatenate([first_time[k] for k in range(3)], axis=1)
    cotans = []
    for frame in range(2):
        fill_windows(windows, frame * CELLS, source[frame, 0], source[frame, 1])
        parts = []
        for par in range(2):
            taps = [frames[frame + 2 - k][par].reshape(CELLS, CH) for k in range(3)]
            grad_hidden = dot_nt(jnp.concatenate(taps, axis=1), kernels)
            parts.append((grad_hidden * silu_slope(pre[frame, par])).astype(BF16))
        cotans.append(jnp.concatenate(parts, axis=1))
    product = dot_tn(windows[...], jnp.concatenate(cotans, axis=0))
    for row in range(3):
        for tap in range(3):
            at = (tap * 4 + row) * CH
            flat[pl.ds((row * 3 + tap) * CH, CH), :] = (
                product[at : at + CH, :CH] + product[at + CH : at + 2 * CH, CH:]
            )
    start = 9 * CH
    for grad in (grad_first_time, grad_down_plane, grad_down_time, grad_last):
        rows = grad.size // CH
        flat[pl.ds(start, rows), :] = grad[...].reshape(rows, CH)
        start += rows
    half = start // 2
    here = core[0]
    mine_out[...] = flat[pl.ds(pl.multiple_of(here * half, 16), half), :]
    other_out[...] = flat[pl.ds(pl.multiple_of((1 - here) * half, 16), half), :].astype(BF16)


def output_body(lowered, last_time, output, spread, padded):
    spread[...] = lowered[...].reshape(HALF * 8, CH).astype(F32)
    padded[pl.ds(0, 8), :] = jnp.zeros((8, WIDE), F32)
    for half in range(2):
        padded[pl.ds(8, DOWN), pl.ds(half * CH, CH)] = spread[pl.ds(half, DOWN, stride=2), :]
    total = padded[pl.ds(8, DOWN), :]
    for k in range(3):
        taps = padded[pl.ds(4 * k, DOWN), :].astype(BF16)
        total = total + dot(taps, last_time[k])
    output[...] = total.astype(BF16)


def from_behind(block, distance):
    devices = range(lax.axis_size("seq"))
    route = [(i - distance, i) for i in devices if i - distance in devices]
    return lax.ppermute(block, "seq", route)


def swap_cores(block):
    count = lax.axis_size("seq")
    return lax.ppermute(block, "seq", [(i, i ^ 1) for i in range(count)])


def exchange_clip(blocks):
    return lax.all_to_all(blocks, "clip", split_axis=0, concat_axis=0, tiled=True)


def exchange_seq(blocks):
    return lax.all_to_all(blocks, "seq", split_axis=0, concat_axis=0, tiled=True)


def exchange_depth(blocks):
    count = lax.axis_size("seq")
    groups = [list(range(core, count, 2)) for core in range(2)]
    return lax.all_to_all(
        blocks, "seq", split_axis=0, concat_axis=0, axis_index_groups=groups, tiled=True
    )


def sum_blocks(blocks):
    return jnp.sum(blocks.astype(F32), axis=0)


def sum_everywhere(mine, other):
    clips = lax.axis_size("clip")
    chips = lax.axis_size("seq") // 2
    core = lax.axis_index("seq") % 2
    other = swap_cores(other)
    half = (mine + other.astype(F32)).astype(BF16)
    part = sum_blocks(exchange_clip(half.reshape(clips, -1, CH)))
    part_rows = part.shape[0]
    chunk = 16 * (-(-part_rows // (16 * chips)))
    part = jnp.pad(part, ((0, chunk * chips - part_rows), (0, 0))).astype(BF16)
    piece = sum_blocks(exchange_depth(part.reshape(chips, chunk, CH))).astype(BF16)
    part = exchange_depth(jnp.broadcast_to(piece[None], (chips, chunk, CH)))
    part = part.reshape(-1, CH)[:part_rows]
    half = exchange_clip(jnp.broadcast_to(part[None], (clips, part_rows, CH)))
    half = half.reshape(-1, CH)
    other = swap_cores(half)
    first = jnp.where(core == 0, half, other)
    second = jnp.where(core == 0, other, half)
    return jnp.concatenate([first, second], axis=0)


def local(clip_in, first_plane, first_time, down_plane, down_time, last_time, cotan_out):
    source = clip_in[0].reshape(2, HALF, 2, COLS, CH).transpose(0, 2, 3, 1, 4)
    prior = from_behind(source, 1)
    rows = cotan_out[0].reshape(HALF, 8, CH)
    rows_ahead = jnp.pad(rows, ((0, 2), (0, 0), (0, 0)))
    cotans = jnp.concatenate([rows, rows_ahead[1 : HALF + 1], rows_ahead[2:]], axis=1)
    cotans = exchange_seq(cotans)
    pre_first, hidden, cells, strided = call(
        first_body,
        [
            ((2, 2, CELLS, CH), F32),
            ((4, 2, CELLS, CH), BF16),
            ((2 * DOWN, 9 * CH), BF16),
            ((2, DOWN, WIDE), BF16),
        ],
        [((4 * CELLS, 12 * CH), BF16), ((12 * CH, WIDE), BF16)],
        prior, source, first_plane, first_time, down_plane,
        flops=2000000000,
    )
    strided_prior = from_behind(strided, 1)
    lowered, grad_pre, grad_down_time, grad_last = call(
        middle_body,
        [
            ((HALF, 8, CH), BF16),
            ((DOWN, WIDE), BF16),
            ((2, 3 * WIDE, CH), F32),
            ((2, 3 * WIDE, CH), F32),
        ],
        [((HALF * 24, CH), F32), ((HALF * 8, CH), F32)],
        strided_prior, strided, cotans, down_time, last_time,
        flops=200000000,
    )
    grad_pre_next = from_behind(grad_pre, -1)
    grad_mixed, grad_first_time, grad_down_plane = call(
        back_body,
        [
            ((2, 2, COLS, HALF, CH), BF16),
            ((3 * CH, CH), F32),
            ((2, 9 * CH, CH), F32),
        ],
        [((2 * DOWN, 4 * WIDE), BF16), ((4 * CH, 4 * WIDE), BF16)],
        grad_pre, grad_pre_next, down_time, down_plane, cells, hidden,
        flops=600000000,
    )
    grad_mixed_next = from_behind(grad_mixed, -1)
    core = (lax.axis_index("seq") % 2).astype(jnp.int32).reshape(1)
    num_rows = (9 + 3 + 18 + 12 + 12) * CH
    mine, other = call(
        last_body,
        [((num_rows // 2, CH), F32), ((num_rows // 2, CH), BF16)],
        [((2 * CELLS, 12 * CH), BF16), ((num_rows, CH), F32)],
        core, grad_mixed, grad_mixed_next, first_time, pre_first, source,
        grad_first_time, grad_down_plane, grad_down_time, grad_last,
        smem=1,
        flops=800000000,
    )
    whole = sum_everywhere(mine, other)
    lowered_rows = exchange_seq(lowered)
    (output,) = call(
        output_body,
        [((DOWN, WIDE), BF16)],
        [((HALF * 8, CH), F32), ((DOWN + 8, WIDE), F32)],
        lowered_rows, last_time,
        flops=60000000,
    )

    result = [output.reshape(1, HALF, 1, 4, WIDE)]
    start = 0
    for shape in ((3, 3, CH, CH), (3, CH, CH), (3, 3, CH, WIDE), (3, WIDE, WIDE), (3, WIDE, WIDE)):
        rows = functools.reduce(lambda a, b: a * b, shape) // CH
        block = whole[start : start + rows]
        if shape[-1] == WIDE:
            block = jnp.concatenate([block[: rows // 2], block[rows // 2 :]], axis=1)
        result.append(block.reshape(shape))
        start += rows
    return tuple(result)


def solution(mesh):
    placed = (
        P("clip", "seq", None, None, None),
        P(),
        P(),
        P(),
        P(),
        P(),
        P("clip", None, "seq", None, None),
    )
    return jax.shard_map(
        local,
        mesh=mesh,
        in_specs=placed,
        out_specs=(P("clip", None, "seq", None, None), P(), P(), P(), P(), P()),
        check_vma=False,
    )
```

```python
import jax
import jax.numpy as jnp
from jax import lax
from jax.experimental import pallas as pl
from jax.experimental.pallas import tpu as pltpu
from jax.sharding import PartitionSpec as P


F32 = jnp.float32
BF16 = jnp.bfloat16
COLS = 8
HALF = 32
CELLS = COLS * HALF
DOWN = CELLS // 2
CH = 128
WIDE = 256


def dot(left, right):
    return lax.dot_general(left, right, (((1,), (0,)), ((), ())), preferred_element_type=F32)


def dot_nt(left, right):
    return lax.dot_general(left, right, (((1,), (1,)), ((), ())), preferred_element_type=F32)


def dot_tn(left, right):
    return lax.dot_general(left, right, (((0,), (0,)), ((), ())), preferred_element_type=F32)


def call(body, outs, scratch, *args, smem=0, flops=0):
    spaces = [pltpu.SMEM] * smem + [pltpu.VMEM] * (len(args) - smem)
    return pl.pallas_call(
        body,
        out_shape=[jax.ShapeDtypeStruct(shape, kind) for shape, kind in outs],
        in_specs=[pl.BlockSpec(memory_space=space) for space in spaces],
        out_specs=[pl.BlockSpec(memory_space=pltpu.VMEM) for _ in outs],
        scratch_shapes=[pltpu.VMEM(shape, kind) for shape, kind in scratch],
        compiler_params=pltpu.CompilerParams(vmem_limit_bytes=24 * 1024 * 1024),
        cost_estimate=pl.CostEstimate(flops=flops, bytes_accessed=4000000, transcendentals=0),
    )(*args)


def row_before(planes):
    wide = planes.astype(F32)
    rolled = pltpu.roll(wide, 1, 1)
    at = lax.broadcasted_iota(jnp.int32, wide.shape, 1)
    return jnp.where(at == 0, 0.0, rolled).astype(BF16)


def row_after(planes):
    wide = planes.astype(F32)
    rolled = pltpu.roll(wide, HALF - 1, 1)
    at = lax.broadcasted_iota(jnp.int32, wide.shape, 1)
    return jnp.where(at == HALF - 1, 0.0, rolled).astype(BF16)


def fill_windows(windows, at, even, odd):
    by_row = (row_before(odd), even, odd, row_after(even))
    edge = jnp.zeros((HALF, CH), BF16)
    for row, planes in enumerate(by_row):
        flat = planes.reshape(CELLS, CH)
        for tap in range(3):
            lanes = pl.ds((tap * 4 + row) * CH, CH)
            if tap == 0:
                windows[pl.ds(at, HALF), lanes] = edge
                windows[pl.ds(at + HALF, CELLS - HALF), lanes] = flat[: CELLS - HALF]
            elif tap == 1:
                windows[pl.ds(at, CELLS), lanes] = flat
            else:
                windows[pl.ds(at, CELLS - HALF), lanes] = flat[HALF:]
                windows[pl.ds(at + CELLS - HALF, HALF), lanes] = edge


def silu_slope(preact):
    sigma = jax.nn.sigmoid(preact)
    return sigma * (1.0 + preact * (1.0 - sigma))


def first_body(
    prior, own, first_plane, first_time, down_plane,
    pre_out, hidden_out, cells_out, strided_out, source_out,
    spread, windows, both,
):
    both[...] = jnp.zeros_like(both)
    for tap in range(3):
        for row in range(4):
            rows = pl.ds((tap * 4 + row) * CH, CH)
            if row < 3:
                both[rows, pl.ds(0, CH)] = first_plane[row, tap]
            if row > 0:
                both[rows, pl.ds(CH, CH)] = first_plane[row - 1, tap]
    for frame in range(4):
        source = prior if frame < 2 else own
        spread[...] = source[frame % 2].astype(F32).reshape(2 * CELLS, CH)
        planes = []
        for par in range(2):
            cols = [
                spread[pl.ds(par * COLS + col, HALF, stride=2 * COLS), :] for col in range(COLS)
            ]
            planes.append(jnp.stack(cols, axis=0).astype(BF16))
            if frame >= 2:
                source_out[frame - 2, par] = planes[par]
        fill_windows(windows, frame * CELLS, planes[0], planes[1])
    for frame in range(4):
        pre = dot(windows[pl.ds(frame * CELLS, CELLS), :], both[...])
        hid = (pre * jax.nn.sigmoid(pre)).astype(BF16)
        for par in range(2):
            hidden_out[frame, par] = hid[:, par * CH : (par + 1) * CH]
            if frame >= 2:
                pre_out[frame - 2, par] = pre[:, par * CH : (par + 1) * CH]
    times = first_time[...].reshape(3 * CH, CH)
    for frame in range(2):
        mixed = []
        for par in range(2):
            taps = jnp.concatenate([hidden_out[frame + k, par] for k in range(3)], axis=1)
            here = source_out[frame, par].reshape(CELLS, CH).astype(F32) + dot(taps, times)
            mixed.append(here.astype(BF16).reshape(COLS, HALF, CH))
        by_row = (row_before(mixed[1]), mixed[0], mixed[1])
        for row in range(3):
            for tap in range(3):
                lanes = pl.ds((row * 3 + tap) * CH, CH)
                for col in range(COLS // 2):
                    rows = pl.ds(frame * DOWN + col * HALF, HALF)
                    where = 2 * col + tap - 1
                    if where < 0:
                        cells_out[rows, lanes] = jnp.zeros((HALF, CH), BF16)
                    else:
                        cells_out[rows, lanes] = by_row[row][where]
    kernel = down_plane[...].reshape(9 * CH, WIDE)
    strided_out[...] = dot(cells_out[...], kernel).astype(BF16).reshape(2, DOWN, WIDE)


def middle_body(
    prior, own, cotans, down_time, last_time,
    lowered_out, grad_pre_out, grad_down_time_out, grad_last_out,
    spread, turned,
):
    spread[...] = cotans[...].reshape(HALF * 24, CH).astype(F32)
    cot = []
    for ahead in range(3):
        parts = []
        for col in range(4):
            halves = [
                spread[pl.ds(ahead * 8 + col * 2 + half, HALF, stride=24), :] for half in range(2)
            ]
            parts.append(jnp.concatenate(halves, axis=1))
        cot.append(jnp.concatenate(parts, axis=0).astype(BF16))
    grad_lowered = cot[0].astype(F32)
    for k in range(3):
        grad_lowered = grad_lowered + dot_nt(cot[2 - k], last_time[k])
    grad_lowered = grad_lowered.astype(BF16)
    taps = (prior[0], prior[1], own[0])
    pre = dot(taps[0], down_time[0]) + dot(taps[1], down_time[1]) + dot(taps[2], down_time[2])
    lowered = (pre * jax.nn.sigmoid(pre)).astype(BF16)
    grad_pre = (grad_lowered.astype(F32) * silu_slope(pre)).astype(BF16)
    grad_pre_out[...] = grad_pre
    wide = lowered.astype(F32)
    for col in range(4):
        for half in range(2):
            turned[pl.ds(col * 2 + half, HALF, stride=8), :] = wide[
                col * HALF : (col + 1) * HALF, half * CH : (half + 1) * CH
            ]
    lowered_out[...] = turned[...].reshape(HALF // 2, 2, 8, CH).astype(BF16)
    for k in range(3):
        down = dot_tn(taps[k], grad_pre)
        last = dot_tn(lowered, cot[2 - k])
        for half in range(2):
            lanes = slice(half * CH, (half + 1) * CH)
            grad_down_time_out[half, pl.ds(k * WIDE, WIDE), :] = down[:, lanes]
            grad_last_out[half, pl.ds(k * WIDE, WIDE), :] = last[:, lanes]


BACK = (
    (0, 0, 0, 0, 1, 1),
    (0, 1, 0, 1, 1, 0),
    (0, 1, 0, 0, 1, 2),
    (1, 0, 1, 0, 0, 1),
    (1, 0, 0, 0, 2, 1),
    (1, 1, 1, 1, 0, 0),
    (1, 1, 1, 0, 0, 2),
    (1, 1, 0, 1, 2, 0),
    (1, 1, 0, 0, 2, 2),
)


def back_body(
    own, ahead, down_time, down_plane, cells, hidden,
    grad_mixed_out, grad_first_time_out, grad_down_plane_out,
    shifted, kernels,
):
    current, following = own[...], ahead[...]
    even = dot_nt(current, down_time[2]) + dot_nt(following, down_time[0])
    odd = dot_nt(following, down_time[1])
    strided = [even.astype(BF16), odd.astype(BF16)]
    kernels[...] = jnp.zeros_like(kernels)
    for row_par, col_par, row_off, col_off, row, tap in BACK:
        rows = pl.ds((row_par * 2 + col_par) * CH, CH)
        lanes = pl.ds((row_off * 2 + col_off) * WIDE, WIDE)
        kernels[rows, lanes] = down_plane[row, tap]
    for frame in range(2):
        planes = strided[frame].reshape(4, HALF, WIDE)
        for row_off, rows in ((0, planes), (1, row_after(planes))):
            flat = rows.reshape(DOWN, WIDE)
            here = pl.ds((row_off * 2) * WIDE, WIDE)
            after = pl.ds((row_off * 2 + 1) * WIDE, WIDE)
            shifted[pl.ds(frame * DOWN, DOWN), here] = flat
            shifted[pl.ds(frame * DOWN, DOWN - HALF), after] = flat[HALF:]
            shifted[pl.ds(frame * DOWN + DOWN - HALF, HALF), after] = jnp.zeros((HALF, WIDE), BF16)
    mixed = dot_nt(shifted[...], kernels[...]).astype(BF16)
    for frame in range(2):
        for par in range(2):
            for col_par in range(2):
                lanes = slice((par * 2 + col_par) * CH, (par * 2 + col_par + 1) * CH)
                for col in range(4):
                    rows = slice(frame * DOWN + col * HALF, frame * DOWN + (col + 1) * HALF)
                    grad_mixed_out[frame, par, 2 * col + col_par] = mixed[rows, lanes]
    both = jnp.concatenate(strided, axis=0)
    down = dot_tn(cells[...], both)
    for half in range(2):
        grad_down_plane_out[half] = down[:, half * CH : (half + 1) * CH]
    cotan = grad_mixed_out[...].reshape(4 * CELLS, CH)
    for k in range(3):
        taps = hidden[pl.ds(k, 2)].reshape(4 * CELLS, CH)
        grad_first_time_out[pl.ds(k * CH, CH), :] = dot_tn(taps, cotan)


def last_body(
    core, own, ahead, first_time, pre, source, lowered,
    grad_first_time, grad_down_plane, grad_down_time, grad_last,
    mine_out, other_out,
    windows, flat,
):
    frames = [own[0], own[1], ahead[0], ahead[1]]
    kernels = jnp.concatenate([first_time[k] for k in range(3)], axis=1)
    cotans = []
    for frame in range(2):
        fill_windows(windows, frame * CELLS, source[frame, 0], source[frame, 1])
        parts = []
        for par in range(2):
            taps = [frames[frame + 2 - k][par].reshape(CELLS, CH) for k in range(3)]
            grad_hidden = dot_nt(jnp.concatenate(taps, axis=1), kernels)
            parts.append((grad_hidden * silu_slope(pre[frame, par])).astype(BF16))
        cotans.append(jnp.concatenate(parts, axis=1))
    product = dot_tn(windows[...], jnp.concatenate(cotans, axis=0))
    for row in range(3):
        for tap in range(3):
            at = (tap * 4 + row) * CH
            flat[pl.ds((row * 3 + tap) * CH, CH), :] = (
                product[at : at + CH, :CH] + product[at + CH : at + 2 * CH, CH:]
            )
    start = 9 * CH
    for grad in (grad_first_time, grad_down_plane, grad_down_time, grad_last):
        rows = grad.size // CH
        flat[pl.ds(start, rows), :] = grad[...].reshape(rows, CH)
        start += rows
    half = start // 2
    here = core[0]
    mine_out[...] = flat[pl.ds(pl.multiple_of(here * half, 16), half), :]
    other_out[pl.ds(0, half), :] = flat[
        pl.ds(pl.multiple_of((1 - here) * half, 16), half), :
    ].astype(BF16)
    away = lowered[:, pl.ds(1 - here, 1)].astype(F32).reshape(DOWN, CH)
    other_out[pl.ds(half, DOWN), :] = away.astype(BF16)


def sum_body(core, blocks, own, other, sent_out, padded):
    rows = blocks.shape[1]
    total = blocks[0].astype(F32)
    for block in range(1, blocks.shape[0]):
        total = total + blocks[block].astype(F32)
    padded[...] = jnp.zeros_like(padded)
    padded[pl.ds(0, rows), :] = total
    chips = sent_out.shape[0]
    sent_out[:, pl.ds(0, 16), :] = padded[...].reshape(chips, 16, CH).astype(BF16)
    here = core[0]
    mine = own[:, pl.ds(here, 1)].astype(F32).reshape(chips, 8, CH)
    theirs = other[...].astype(F32).reshape(chips, 8, CH)
    frames = [jnp.where(here == 0, mine, theirs), jnp.where(here == 0, theirs, mine)]
    sent_out[:, pl.ds(16, 16), :] = jnp.concatenate(frames, axis=1).astype(BF16)


def piece_body(received, piece_out):
    chips = received.shape[0]
    total = received[0, pl.ds(0, 16), :].astype(F32)
    for chip in range(1, chips):
        total = total + received[chip, pl.ds(0, 16), :].astype(F32)
    piece = total.astype(BF16)
    for chip in range(chips):
        piece_out[chip] = piece


def spread_body(pieces, part_out):
    flat = pieces[...].reshape(-1, CH).astype(F32)
    part = flat[: part_out.shape[1]].astype(BF16)
    for block in range(part_out.shape[0]):
        part_out[block] = part


def results_body(core, mine, other, *rest):
    outs, whole = rest[:-1], rest[-1]
    here = core[0]
    half = mine.shape[0]
    whole[pl.ds(pl.multiple_of(here * half, 16), half), :] = mine[...]
    whole[pl.ds(pl.multiple_of((1 - here) * half, 16), half), :] = other[...]
    start = 0
    for out in outs:
        rows, lanes = out.shape
        for part in range(lanes // CH):
            out[:, pl.ds(part * CH, CH)] = whole[pl.ds(start, rows), :]
            start += rows


def output_body(received, last_time, output, spread, padded):
    frames = received[:, pl.ds(16, 16), :]
    spread[...] = frames.astype(F32).reshape(HALF * 8, CH)
    padded[pl.ds(0, 8), :] = jnp.zeros((8, WIDE), F32)
    for half in range(2):
        padded[pl.ds(8, DOWN), pl.ds(half * CH, CH)] = spread[pl.ds(half, DOWN, stride=2), :]
    total = padded[pl.ds(8, DOWN), :]
    for k in range(3):
        taps = padded[pl.ds(4 * k, DOWN), :].astype(BF16)
        total = total + dot(taps, last_time[k])
    output[...] = total.astype(BF16)


def from_behind(block, distance):
    devices = range(lax.axis_size("seq"))
    route = [(i - distance, i) for i in devices if i - distance in devices]
    return lax.ppermute(block, "seq", route)


def swap_cores(block):
    count = lax.axis_size("seq")
    return lax.ppermute(block, "seq", [(i, i ^ 1) for i in range(count)])


def exchange_clip(blocks):
    return lax.all_to_all(blocks, "clip", split_axis=0, concat_axis=0, tiled=True)


def exchange_seq(blocks):
    return lax.all_to_all(blocks, "seq", split_axis=0, concat_axis=0, tiled=True)


def exchange_depth(blocks):
    count = lax.axis_size("seq")
    groups = [list(range(core, count, 2)) for core in range(2)]
    return lax.all_to_all(
        blocks, "seq", split_axis=0, concat_axis=0, axis_index_groups=groups, tiled=True
    )


def local(clip_in, first_plane, first_time, down_plane, down_time, last_time, cotan_out):
    prior = from_behind(clip_in[0], 1)
    rows = cotan_out[0].reshape(HALF, 8, CH)
    rows_ahead = jnp.pad(rows, ((0, 2), (0, 0), (0, 0)))
    cotans = jnp.concatenate([rows, rows_ahead[1 : HALF + 1], rows_ahead[2:]], axis=1)
    cotans = exchange_seq(cotans)
    pre_first, hidden, cells, strided, source = call(
        first_body,
        [
            ((2, 2, CELLS, CH), F32),
            ((4, 2, CELLS, CH), BF16),
            ((2 * DOWN, 9 * CH), BF16),
            ((2, DOWN, WIDE), BF16),
            ((2, 2, COLS, HALF, CH), BF16),
        ],
        [((2 * CELLS, CH), F32), ((4 * CELLS, 12 * CH), BF16), ((12 * CH, WIDE), BF16)],
        prior, clip_in[0], first_plane, first_time, down_plane,
        flops=2000000000,
    )
    strided_prior = from_behind(strided, 1)
    lowered, grad_pre, grad_down_time, grad_last = call(
        middle_body,
        [
            ((HALF // 2, 2, 8, CH), BF16),
            ((DOWN, WIDE), BF16),
            ((2, 3 * WIDE, CH), F32),
            ((2, 3 * WIDE, CH), F32),
        ],
        [((HALF * 24, CH), F32), ((HALF * 8, CH), F32)],
        strided_prior, strided, cotans, down_time, last_time,
        flops=200000000,
    )
    grad_pre_next = from_behind(grad_pre, -1)
    grad_mixed, grad_first_time, grad_down_plane = call(
        back_body,
        [
            ((2, 2, COLS, HALF, CH), BF16),
            ((3 * CH, CH), F32),
            ((2, 9 * CH, CH), F32),
        ],
        [((2 * DOWN, 4 * WIDE), BF16), ((4 * CH, 4 * WIDE), BF16)],
        grad_pre, grad_pre_next, down_time, down_plane, cells, hidden,
        flops=600000000,
    )
    grad_mixed_next = from_behind(grad_mixed, -1)
    core = (lax.axis_index("seq") % 2).astype(jnp.int32).reshape(1)
    half_rows = (9 + 3 + 18 + 12 + 12) * CH // 2
    mine, other = call(
        last_body,
        [((half_rows, CH), F32), ((half_rows + DOWN, CH), BF16)],
        [((2 * CELLS, 12 * CH), BF16), ((2 * half_rows, CH), F32)],
        core, grad_mixed, grad_mixed_next, first_time, pre_first, source, lowered,
        grad_first_time, grad_down_plane, grad_down_time, grad_last,
        smem=1,
        flops=800000000,
    )

    clips = lax.axis_size("clip")
    chips = lax.axis_size("seq") // 2
    other = swap_cores(other)
    half = (mine + other[:half_rows].astype(F32)).astype(BF16)
    part_rows = half_rows // clips
    blocks = exchange_clip(half.reshape(clips, part_rows, CH))
    (sent,) = call(
        sum_body,
        [((chips, 32, CH), BF16)],
        [((16 * chips, CH), F32)],
        core, blocks, lowered, other[half_rows:],
        smem=1,
    )
    received = exchange_depth(sent)
    (pieces,) = call(piece_body, [((chips, 16, CH), BF16)], [], received)
    pieces = exchange_depth(pieces)
    (output,) = call(
        output_body,
        [((DOWN, WIDE), BF16)],
        [((HALF * 8, CH), F32), ((DOWN + 8, WIDE), F32)],
        received, last_time,
        flops=60000000,
    )
    (parts,) = call(spread_body, [((clips, part_rows, CH), BF16)], [], pieces)
    half = exchange_clip(parts).reshape(half_rows, CH)
    other = swap_cores(half)
    grads = call(
        results_body,
        [
            ((9 * CH, CH), BF16),
            ((3 * CH, CH), BF16),
            ((9 * CH, WIDE), BF16),
            ((3 * WIDE, WIDE), BF16),
            ((3 * WIDE, WIDE), BF16),
        ],
        [((2 * half_rows, CH), BF16)],
        core, half, other,
        smem=1,
    )
    shapes = ((3, 3, CH, CH), (3, CH, CH), (3, 3, CH, WIDE), (3, WIDE, WIDE), (3, WIDE, WIDE))
    grads = [grad.reshape(shape) for grad, shape in zip(grads, shapes)]
    return (output.reshape(1, HALF, 1, 4, WIDE), *grads)


def solution(mesh):
    placed = (
        P("clip", "seq", None, None, None),
        P(),
        P(),
        P(),
        P(),
        P(),
        P("clip", None, "seq", None, None),
    )
    return jax.shard_map(
        local,
        mesh=mesh,
        in_specs=placed,
        out_specs=(P("clip", None, "seq", None, None), P(), P(), P(), P(), P()),
        check_vma=False,
    )
```

```python
import jax
import jax.numpy as jnp
from jax import lax
from jax.experimental import pallas as pl
from jax.experimental.pallas import tpu as pltpu
from jax.sharding import PartitionSpec as P


F32 = jnp.float32
BF16 = jnp.bfloat16
COLS = 8
HALF = 32
CELLS = COLS * HALF
DOWN = CELLS // 2
CH = 128
WIDE = 256


def dot(left, right):
    return lax.dot_general(left, right, (((1,), (0,)), ((), ())), preferred_element_type=F32)


def dot_nt(left, right):
    return lax.dot_general(left, right, (((1,), (1,)), ((), ())), preferred_element_type=F32)


def dot_tn(left, right):
    return lax.dot_general(left, right, (((0,), (0,)), ((), ())), preferred_element_type=F32)


V, H, S = pltpu.VMEM, pltpu.HBM, pltpu.SMEM


def call(body, ins, outs, scratch=(), copies=0, flops=0):
    scratch = [pltpu.VMEM(shape, kind) for shape, kind in scratch]
    if copies:
        scratch.append(pltpu.SemaphoreType.DMA((copies,)))
    return pl.pallas_call(
        body,
        out_shape=[jax.ShapeDtypeStruct(shape, kind) for _, shape, kind in outs],
        in_specs=[pl.BlockSpec(memory_space=space) for space, _ in ins],
        out_specs=[pl.BlockSpec(memory_space=space) for space, _, _ in outs],
        scratch_shapes=scratch,
        compiler_params=pltpu.CompilerParams(vmem_limit_bytes=24 * 1024 * 1024),
        cost_estimate=pl.CostEstimate(flops=flops, bytes_accessed=2000000, transcendentals=0),
    )(*[array for _, array in ins])


def start(sems, *pairs):
    copies = [
        pltpu.make_async_copy(source, target, sems.at[at]) for at, source, target in pairs
    ]
    for copy in copies:
        copy.start()
    return copies


def row_before(planes):
    wide = planes.astype(F32)
    rolled = pltpu.roll(wide, 1, 1)
    at = lax.broadcasted_iota(jnp.int32, wide.shape, 1)
    return jnp.where(at == 0, 0.0, rolled).astype(BF16)


def row_after(planes):
    wide = planes.astype(F32)
    rolled = pltpu.roll(wide, HALF - 1, 1)
    at = lax.broadcasted_iota(jnp.int32, wide.shape, 1)
    return jnp.where(at == HALF - 1, 0.0, rolled).astype(BF16)


def fill_windows(windows, at, even, odd):
    by_row = (row_before(odd), even, odd, row_after(even))
    edge = jnp.zeros((HALF, CH), BF16)
    for row, planes in enumerate(by_row):
        flat = planes.reshape(CELLS, CH)
        for tap in range(3):
            lanes = pl.ds((tap * 4 + row) * CH, CH)
            if tap == 0:
                windows[pl.ds(at, HALF), lanes] = edge
                windows[pl.ds(at + HALF, CELLS - HALF), lanes] = flat[: CELLS - HALF]
            elif tap == 1:
                windows[pl.ds(at, CELLS), lanes] = flat
            else:
                windows[pl.ds(at, CELLS - HALF), lanes] = flat[HALF:]
                windows[pl.ds(at + CELLS - HALF, HALF), lanes] = edge


def silu_slope(preact):
    sigma = jax.nn.sigmoid(preact)
    return sigma * (1.0 + preact * (1.0 - sigma))


def first_body(
    prior, own_far, plane_far, time_far, down_far,
    pre_far, hidden_far, cells_far, source_far, strided_out,
    own, first_plane, first_time, down_plane, pre_out, hidden_out, cells_out, source_out,
    spread, windows, both, sems,
):
    loads = start(
        sems,
        (0, own_far, own),
        (1, plane_far, first_plane),
        (2, time_far, first_time),
        (3, down_far, down_plane),
    )
    both[...] = jnp.zeros_like(both)
    for frame in range(4):
        if frame == 2:
            loads[0].wait()
        source = prior if frame < 2 else own
        spread[...] = source[pl.ds(frame % 2 * 2 * CELLS, 2 * CELLS), :].astype(F32)
        planes = []
        for par in range(2):
            cols = [
                spread[pl.ds(par * COLS + col, HALF, stride=2 * COLS), :] for col in range(COLS)
            ]
            planes.append(jnp.stack(cols, axis=0).astype(BF16))
            if frame >= 2:
                source_out[frame - 2, par] = planes[par]
        fill_windows(windows, frame * CELLS, planes[0], planes[1])
    stores = start(sems, (4, source_out, source_far))
    loads[1].wait()
    for tap in range(3):
        for row in range(4):
            rows = pl.ds((tap * 4 + row) * CH, CH)
            if row < 3:
                both[rows, pl.ds(0, CH)] = first_plane[row, tap]
            if row > 0:
                both[rows, pl.ds(CH, CH)] = first_plane[row - 1, tap]
    for frame in range(4):
        pre = dot(windows[pl.ds(frame * CELLS, CELLS), :], both[...])
        hid = (pre * jax.nn.sigmoid(pre)).astype(BF16)
        for par in range(2):
            hidden_out[frame, par] = hid[:, par * CH : (par + 1) * CH]
            if frame >= 2:
                pre_out[frame - 2, par] = pre[:, par * CH : (par + 1) * CH]
    stores += start(sems, (5, pre_out, pre_far), (6, hidden_out, hidden_far))
    loads[2].wait()
    times = first_time[...].reshape(3 * CH, CH)
    for frame in range(2):
        mixed = []
        for par in range(2):
            taps = jnp.concatenate([hidden_out[frame + k, par] for k in range(3)], axis=1)
            here = source_out[frame, par].reshape(CELLS, CH).astype(F32) + dot(taps, times)
            mixed.append(here.astype(BF16).reshape(COLS, HALF, CH))
        by_row = (row_before(mixed[1]), mixed[0], mixed[1])
        for row in range(3):
            for tap in range(3):
                lanes = pl.ds((row * 3 + tap) * CH, CH)
                for col in range(COLS // 2):
                    rows = pl.ds(frame * DOWN + col * HALF, HALF)
                    where = 2 * col + tap - 1
                    if where < 0:
                        cells_out[rows, lanes] = jnp.zeros((HALF, CH), BF16)
                    else:
                        cells_out[rows, lanes] = by_row[row][where]
    stores += start(sems, (7, cells_out, cells_far))
    loads[3].wait()
    kernel = down_plane[...].reshape(9 * CH, WIDE)
    strided_out[...] = dot(cells_out[...], kernel).astype(BF16).reshape(2, DOWN, WIDE)
    for store in stores:
        store.wait()


def cotan_body(
    own, cotans, down_far, last_far,
    cot_out, grad_lowered_out, part_out, times_out,
    last_time, down_time, spread, sems,
):
    loads = start(sems, (0, last_far, last_time), (1, down_far, down_time))
    spread[...] = cotans[...].astype(F32).reshape(HALF * 24, CH)
    cot = []
    for ahead in range(3):
        parts = []
        for col in range(4):
            halves = [
                spread[pl.ds(ahead * 8 + col * 2 + half, HALF, stride=24), :] for half in range(2)
            ]
            parts.append(jnp.concatenate(halves, axis=1))
        cot.append(jnp.concatenate(parts, axis=0).astype(BF16))
        cot_out[ahead] = cot[ahead]
    loads[0].wait()
    grad_lowered = cot[0].astype(F32)
    for k in range(3):
        grad_lowered = grad_lowered + dot_nt(cot[2 - k], last_time[k])
    grad_lowered_out[...] = grad_lowered.astype(BF16)
    loads[1].wait()
    part_out[...] = dot(own[0], down_time[2])
    times_out[...] = down_time[pl.ds(0, 2)]


def middle_body(prior, part, times, grad_lowered, lowered_out, grad_pre_out):
    pre = dot(prior[0], times[0]) + dot(prior[1], times[1]) + part[...]
    lowered_out[...] = (pre * jax.nn.sigmoid(pre)).astype(BF16)
    grad_pre_out[...] = (grad_lowered[...].astype(F32) * silu_slope(pre)).astype(BF16)


BACK = (
    (0, 0, 0, 0, 1, 1),
    (0, 1, 0, 1, 1, 0),
    (0, 1, 0, 0, 1, 2),
    (1, 0, 1, 0, 0, 1),
    (1, 0, 0, 0, 2, 1),
    (1, 1, 1, 1, 0, 0),
    (1, 1, 1, 0, 0, 2),
    (1, 1, 0, 1, 2, 0),
    (1, 1, 0, 0, 2, 2),
)


def time_grads_body(
    grad_pre, lowered, cot, prior, own, down_far, plane_far,
    part_out, times_out, kernels_out, grad_down_time_out, grad_last_out, lowered_out,
    down_time, down_plane, turned, sems,
):
    loads = start(sems, (0, down_far, down_time), (1, plane_far, down_plane))
    kernels_out[...] = jnp.zeros_like(kernels_out)
    wide = lowered[...].astype(F32)
    for col in range(4):
        for half in range(2):
            turned[pl.ds(col * 2 + half, HALF, stride=8), :] = wide[
                col * HALF : (col + 1) * HALF, half * CH : (half + 1) * CH
            ]
    lowered_out[...] = turned[...].reshape(HALF // 2, 2, 8, CH).astype(BF16)
    taps = (prior[0], prior[1], own[0])
    for k in range(3):
        down = dot_tn(taps[k], grad_pre[...])
        last = dot_tn(lowered[...], cot[2 - k])
        for half in range(2):
            lanes = slice(half * CH, (half + 1) * CH)
            grad_down_time_out[half, pl.ds(k * WIDE, WIDE), :] = down[:, lanes]
            grad_last_out[half, pl.ds(k * WIDE, WIDE), :] = last[:, lanes]
    for load in loads:
        load.wait()
    part_out[...] = dot_nt(grad_pre[...], down_time[2])
    times_out[...] = down_time[pl.ds(0, 2)]
    for row_par, col_par, row_off, col_off, row, tap in BACK:
        rows = pl.ds((row_par * 2 + col_par) * CH, CH)
        lanes = pl.ds((row_off * 2 + col_off) * WIDE, WIDE)
        kernels_out[rows, lanes] = down_plane[row, tap]


def back_body(ahead, part, times, kernels, grad_strided_out, grad_mixed_out, shifted):
    following = ahead[...]
    even = part[...] + dot_nt(following, times[0])
    odd = dot_nt(following, times[1])
    for frame, strided in ((0, even.astype(BF16)), (1, odd.astype(BF16))):
        grad_strided_out[pl.ds(frame * DOWN, DOWN), :] = strided
        planes = strided.reshape(4, HALF, WIDE)
        for row_off, rows in ((0, planes), (1, row_after(planes))):
            flat = rows.reshape(DOWN, WIDE)
            here = pl.ds((row_off * 2) * WIDE, WIDE)
            after = pl.ds((row_off * 2 + 1) * WIDE, WIDE)
            shifted[pl.ds(frame * DOWN, DOWN), here] = flat
            shifted[pl.ds(frame * DOWN, DOWN - HALF), after] = flat[HALF:]
            shifted[pl.ds(frame * DOWN + DOWN - HALF, HALF), after] = jnp.zeros((HALF, WIDE), BF16)
    mixed = dot_nt(shifted[...], kernels[...]).astype(BF16)
    for frame in range(2):
        for par in range(2):
            for col_par in range(2):
                lanes = slice((par * 2 + col_par) * CH, (par * 2 + col_par + 1) * CH)
                for col in range(4):
                    rows = slice(frame * DOWN + col * HALF, frame * DOWN + (col + 1) * HALF)
                    grad_mixed_out[frame, par, 2 * col + col_par] = mixed[rows, lanes]


def plane_grads_body(
    core, grad_strided, grad_mixed, cells_far, hidden_far, source_far, pre_far, time_far,
    grad_down_time, grad_last, lowered,
    mine_out, other_out, windows_out, slope_out, part_out, time_out,
    cells, hidden, source, pre, flat, sems,
):
    loads = start(
        sems,
        (0, cells_far, cells),
        (1, hidden_far, hidden),
        (2, source_far, source),
        (3, pre_far, pre),
        (4, time_far, time_out),
    )
    rows = 2 * 3 * WIDE
    base = 3 * CH + 18 * CH
    flat[pl.ds(base, rows), :] = grad_down_time[...].reshape(rows, CH)
    flat[pl.ds(base + rows, rows), :] = grad_last[...].reshape(rows, CH)
    loads[0].wait()
    down = dot_tn(cells[...], grad_strided[...])
    for half in range(2):
        at = 3 * CH + half * 9 * CH
        flat[pl.ds(at, 9 * CH), :] = down[:, half * CH : (half + 1) * CH]
    cotan = grad_mixed[...].reshape(4 * CELLS, CH)
    loads[1].wait()
    for k in range(3):
        taps = hidden[pl.ds(k, 2)].reshape(4 * CELLS, CH)
        flat[pl.ds(k * CH, CH), :] = dot_tn(taps, cotan)
    here = core[0]
    half = mine_out.shape[0]
    mine_out[...] = flat[pl.ds(pl.multiple_of(here * half, 16), half), :]
    other_out[pl.ds(0, half), :] = flat[
        pl.ds(pl.multiple_of((1 - here) * half, 16), half), :
    ].astype(BF16)
    away = lowered[:, pl.ds(1 - here, 1)].astype(F32).reshape(DOWN, CH)
    other_out[pl.ds(half, DOWN), :] = away.astype(BF16)
    for load in loads[2:]:
        load.wait()
    for frame in range(2):
        fill_windows(windows_out, frame * CELLS, source[frame, 0], source[frame, 1])
    slope_out[...] = silu_slope(pre[...])
    for par in range(2):
        first, second = [grad_mixed[frame, par].reshape(CELLS, CH) for frame in range(2)]
        part_out[0, par] = dot_nt(first, time_out[2]) + dot_nt(second, time_out[1])
        part_out[1, par] = dot_nt(second, time_out[2])


def last_body(
    core, ahead, windows, slope, part, first_time,
    mine_out, other_out,
    flat,
):
    cotans = [[], []]
    for par in range(2):
        first, second = [ahead[frame, par].reshape(CELLS, CH) for frame in range(2)]
        hidden = (
            part[0, par] + dot_nt(first, first_time[0]),
            part[1, par] + dot_nt(first, first_time[1]) + dot_nt(second, first_time[0]),
        )
        for frame in range(2):
            cotans[frame].append((hidden[frame] * slope[frame, par]).astype(BF16))
    cotan = jnp.concatenate([jnp.concatenate(parts, axis=1) for parts in cotans], axis=0)
    product = dot_tn(windows[...], cotan)
    for row in range(3):
        for tap in range(3):
            at = (tap * 4 + row) * CH
            flat[pl.ds((row * 3 + tap) * CH, CH), :] = (
                product[at : at + CH, :CH] + product[at + CH : at + 2 * CH, CH:]
            )
    here = core[0]
    half = mine_out.shape[0]
    mine_out[...] = flat[pl.ds(pl.multiple_of(here * half, 16), half), :]
    other_out[...] = flat[pl.ds(pl.multiple_of((1 - here) * half, 16), half), :].astype(BF16)


def halves_body(early, early_other, late, late_other, half_out):
    rows, more = early.shape[0], late.shape[0]
    half_out[pl.ds(0, rows), :] = (
        early[...] + early_other[pl.ds(0, rows), :].astype(F32)
    ).astype(BF16)
    half_out[pl.ds(rows, more), :] = (late[...] + late_other[...].astype(F32)).astype(BF16)


def sum_body(core, blocks, own, other, sent_out, padded):
    rows = blocks.shape[1]
    total = blocks[0].astype(F32)
    for block in range(1, blocks.shape[0]):
        total = total + blocks[block].astype(F32)
    padded[...] = jnp.zeros_like(padded)
    padded[pl.ds(0, rows), :] = total
    chips = sent_out.shape[0]
    sent_out[:, pl.ds(0, 16), :] = padded[...].reshape(chips, 16, CH).astype(BF16)
    here = core[0]
    mine = own[:, pl.ds(here, 1)].astype(F32).reshape(chips, 8, CH)
    theirs = other[pl.ds(other.shape[0] - DOWN, DOWN), :].astype(F32).reshape(chips, 8, CH)
    frames = [jnp.where(here == 0, mine, theirs), jnp.where(here == 0, theirs, mine)]
    sent_out[:, pl.ds(16, 16), :] = jnp.concatenate(frames, axis=1).astype(BF16)


def piece_body(received, piece_out):
    chips = received.shape[0]
    total = received[0, pl.ds(0, 16), :].astype(F32)
    for chip in range(1, chips):
        total = total + received[chip, pl.ds(0, 16), :].astype(F32)
    piece = total.astype(BF16)
    for chip in range(chips):
        piece_out[chip] = piece


def spread_body(pieces, part_out):
    flat = pieces[...].reshape(-1, CH).astype(F32)
    part = flat[: part_out.shape[1]].astype(BF16)
    for block in range(part_out.shape[0]):
        part_out[block] = part


def results_body(core, mine, other, first_plane_out, *rest):
    outs, early, late = rest[:-2], rest[-2], rest[-1]
    here = core[0]
    rows, more = early.shape[0] // 2, late.shape[0] // 2
    for half, at in ((mine, here), (other, 1 - here)):
        early[pl.ds(pl.multiple_of(at * rows, 16), rows), :] = half[pl.ds(0, rows), :]
        late[pl.ds(pl.multiple_of(at * more, 16), more), :] = half[pl.ds(rows, more), :]
    first_plane_out[...] = late[...]
    first = 0
    for out in outs:
        count, lanes = out.shape
        for part in range(lanes // CH):
            out[:, pl.ds(part * CH, CH)] = early[pl.ds(first, count), :]
            first += count


def output_body(received, last_time, output, spread, padded):
    frames = received[:, pl.ds(16, 16), :]
    spread[...] = frames.astype(F32).reshape(HALF * 8, CH)
    padded[pl.ds(0, 8), :] = jnp.zeros((8, WIDE), F32)
    for half in range(2):
        padded[pl.ds(8, DOWN), pl.ds(half * CH, CH)] = spread[pl.ds(half, DOWN, stride=2), :]
    total = padded[pl.ds(8, DOWN), :]
    for k in range(3):
        taps = padded[pl.ds(4 * k, DOWN), :].astype(BF16)
        total = total + dot(taps, last_time[k])
    output[...] = total.astype(BF16)


def from_behind(block, distance):
    devices = range(lax.axis_size("seq"))
    route = [(i - distance, i) for i in devices if i - distance in devices]
    return lax.ppermute(block, "seq", route)


def swap_cores(block):
    count = lax.axis_size("seq")
    return lax.ppermute(block, "seq", [(i, i ^ 1) for i in range(count)])


def exchange_clip(blocks):
    return lax.all_to_all(blocks, "clip", split_axis=0, concat_axis=0, tiled=True)


def exchange_seq(blocks):
    return lax.all_to_all(blocks, "seq", split_axis=0, concat_axis=0, tiled=True)


def exchange_depth(blocks):
    count = lax.axis_size("seq")
    groups = [list(range(core, count, 2)) for core in range(2)]
    return lax.all_to_all(
        blocks, "seq", split_axis=0, concat_axis=0, axis_index_groups=groups, tiled=True
    )


def local(clip_in, first_plane, first_time, down_plane, down_time, last_time, cotan_out):
    own = clip_in.reshape(4 * CELLS, CH)
    prior = from_behind(own, 1)
    rows = cotan_out[0].reshape(HALF, 8, CH)
    rows_ahead = jnp.pad(rows, ((0, 2), (0, 0), (0, 0)))
    cotans = jnp.concatenate([rows, rows_ahead[1 : HALF + 1], rows_ahead[2:]], axis=1)
    cotans, prior = lax.optimization_barrier((cotans, prior))
    cotans = exchange_seq(cotans)
    frames = (2, 2, COLS, HALF, CH)
    flat_frames = (2, 2, CELLS, CH)
    far = [
        (H, flat_frames, F32),
        (H, (4, 2, CELLS, CH), BF16),
        (H, (2 * DOWN, 9 * CH), BF16),
        (H, frames, BF16),
    ]
    pre_first, hidden, cells, source, strided = call(
        first_body,
        [(V, prior), (H, own), (H, first_plane), (H, first_time), (H, down_plane)],
        [*far, (V, (2, DOWN, WIDE), BF16)],
        [
            ((4 * CELLS, CH), BF16),
            ((3, 3, CH, CH), BF16),
            ((3, CH, CH), BF16),
            ((3, 3, CH, WIDE), BF16),
            *[(shape, kind) for _, shape, kind in far],
            ((2 * CELLS, CH), F32),
            ((4 * CELLS, 12 * CH), BF16),
            ((12 * CH, WIDE), BF16),
        ],
        copies=8,
        flops=2000000000,
    )
    strided_prior = from_behind(strided, 1)
    times = (V, (2, WIDE, WIDE), BF16)
    cot, grad_lowered, part, near_times = call(
        cotan_body,
        [(V, strided), (V, cotans), (H, down_time), (H, last_time)],
        [(V, (3, DOWN, WIDE), BF16), (V, (DOWN, WIDE), BF16), (V, (DOWN, WIDE), F32), times],
        [((3, WIDE, WIDE), BF16), ((3, WIDE, WIDE), BF16), ((HALF * 24, CH), F32)],
        copies=2,
        flops=100000000,
    )
    lowered, grad_pre = call(
        middle_body,
        [(V, strided_prior), (V, part), (V, near_times), (V, grad_lowered)],
        [(V, (DOWN, WIDE), BF16), (V, (DOWN, WIDE), BF16)],
        flops=60000000,
    )
    grad_pre_next = from_behind(grad_pre, -1)
    part, near_times, kernels, grad_down_time, grad_last, lowered = call(
        time_grads_body,
        [
            (V, grad_pre), (V, lowered), (V, cot), (V, strided_prior), (V, strided),
            (H, down_time), (H, down_plane),
        ],
        [
            (V, (DOWN, WIDE), F32),
            times,
            (V, (4 * CH, 4 * WIDE), BF16),
            (V, (2, 3 * WIDE, CH), F32),
            (V, (2, 3 * WIDE, CH), F32),
            (V, (HALF // 2, 2, 8, CH), BF16),
        ],
        [((3, WIDE, WIDE), BF16), ((3, 3, CH, WIDE), BF16), ((HALF * 8, CH), F32)],
        copies=2,
        flops=120000000,
    )
    grad_strided, grad_mixed = call(
        back_body,
        [(V, grad_pre_next), (V, part), (V, near_times), (V, kernels)],
        [(V, (2 * DOWN, WIDE), BF16), (V, frames, BF16)],
        [((2 * DOWN, 4 * WIDE), BF16)],
        flops=300000000,
    )
    grad_mixed_next = from_behind(grad_mixed, -1)
    core = (lax.axis_index("seq") % 2).astype(jnp.int32).reshape(1)
    early_rows = (3 + 18 + 12 + 12) * CH
    late_rows = 9 * CH
    early, early_other, windows, slope, part, near_time = call(
        plane_grads_body,
        [
            (S, core), (V, grad_strided), (V, grad_mixed),
            (H, cells), (H, hidden), (H, source), (H, pre_first), (H, first_time),
            (V, grad_down_time), (V, grad_last), (V, lowered),
        ],
        [
            (V, (early_rows // 2, CH), F32),
            (V, (early_rows // 2 + DOWN, CH), BF16),
            (V, (2 * CELLS, 12 * CH), BF16),
            (V, flat_frames, F32),
            (V, flat_frames, F32),
            (V, (3, CH, CH), BF16),
        ],
        [
            ((2 * DOWN, 9 * CH), BF16),
            ((4, 2, CELLS, CH), BF16),
            (frames, BF16),
            (flat_frames, F32),
            ((early_rows, CH), F32),
        ],
        copies=5,
        flops=500000000,
    )
    early_other = swap_cores(early_other)
    late, late_other = call(
        last_body,
        [(S, core), (V, grad_mixed_next), (V, windows), (V, slope), (V, part), (V, near_time)],
        [(V, (late_rows // 2, CH), F32), (V, (late_rows // 2, CH), BF16)],
        [((late_rows, CH), F32)],
        flops=600000000,
    )
    late_other = swap_cores(late_other)

    clips = lax.axis_size("clip")
    chips = lax.axis_size("seq") // 2
    half_rows = (early_rows + late_rows) // 2
    part_rows = half_rows // clips
    (half,) = call(
        halves_body,
        [(V, early), (V, early_other), (V, late), (V, late_other)],
        [(V, (half_rows, CH), BF16)],
    )
    blocks = exchange_clip(half.reshape(clips, part_rows, CH))
    (sent,) = call(
        sum_body,
        [(S, core), (V, blocks), (V, lowered), (V, early_other)],
        [(V, (chips, 32, CH), BF16)],
        [((16 * chips, CH), F32)],
    )
    received = exchange_depth(sent)
    (pieces,) = call(piece_body, [(V, received)], [(V, (chips, 16, CH), BF16)])
    pieces = exchange_depth(pieces)
    (output,) = call(
        output_body,
        [(V, received), (V, last_time)],
        [(V, (DOWN, WIDE), BF16)],
        [((HALF * 8, CH), F32), ((DOWN + 8, WIDE), F32)],
        flops=60000000,
    )
    (parts,) = call(spread_body, [(V, pieces)], [(V, (clips, part_rows, CH), BF16)])
    half = exchange_clip(parts).reshape(half_rows, CH)
    other = swap_cores(half)
    grads = call(
        results_body,
        [(S, core), (V, half), (V, other)],
        [
            (V, (9 * CH, CH), BF16),
            (V, (3 * CH, CH), BF16),
            (V, (9 * CH, WIDE), BF16),
            (V, (3 * WIDE, WIDE), BF16),
            (V, (3 * WIDE, WIDE), BF16),
        ],
        [((early_rows, CH), BF16), ((late_rows, CH), BF16)],
    )
    shapes = ((3, 3, CH, CH), (3, CH, CH), (3, 3, CH, WIDE), (3, WIDE, WIDE), (3, WIDE, WIDE))
    grads = [grad.reshape(shape) for grad, shape in zip(grads, shapes)]
    return (output.reshape(1, HALF, 1, 4, WIDE), *grads)


def solution(mesh):
    placed = (
        P("clip", "seq", None, None, None),
        P(),
        P(),
        P(),
        P(),
        P(),
        P("clip", None, "seq", None, None),
    )
    return jax.shard_map(
        local,
        mesh=mesh,
        in_specs=placed,
        out_specs=(P("clip", None, "seq", None, None), P(), P(), P(), P(), P()),
        check_vma=False,
    )
```

```python
import jax
import jax.numpy as jnp
from jax import lax
from jax.experimental import pallas as pl
from jax.experimental.pallas import tpu as pltpu
from jax.sharding import PartitionSpec as P


F32 = jnp.float32
BF16 = jnp.bfloat16
COLS = 8
HALF = 32
CELLS = COLS * HALF
DOWN = CELLS // 2
CH = 128
WIDE = 256
EARLY = (3 + 18 + 12 + 8) * CH
LATE = (9 + 4) * CH


def dot(left, right):
    return lax.dot_general(left, right, (((1,), (0,)), ((), ())), preferred_element_type=F32)


def dot_nt(left, right):
    return lax.dot_general(left, right, (((1,), (1,)), ((), ())), preferred_element_type=F32)


def dot_tn(left, right):
    return lax.dot_general(left, right, (((0,), (0,)), ((), ())), preferred_element_type=F32)


V, P_, H, S = "vmem", "pinned", "hbm", "smem"
SPACES = {V: pltpu.VMEM, P_: pltpu.VMEM, H: pltpu.HBM, S: pltpu.SMEM}


def placed_input(space, array):
    if space in (P_, H):
        return pltpu.with_memory_space_constraint(array, SPACES[space])
    return array


def placed_output(space, shape, kind):
    if space in (P_, H):
        return SPACES[space](shape, kind)
    return jax.ShapeDtypeStruct(shape, kind)


def call(body, ins, outs, scratch=(), copies=0, flops=0):
    scratch = [pltpu.VMEM(shape, kind) for shape, kind in scratch]
    if copies:
        scratch.append(pltpu.SemaphoreType.DMA((copies,)))
    return pl.pallas_call(
        body,
        out_shape=[placed_output(*out) for out in outs],
        in_specs=[pl.BlockSpec(memory_space=SPACES[space]) for space, _ in ins],
        out_specs=[pl.BlockSpec(memory_space=SPACES[space]) for space, _, _ in outs],
        scratch_shapes=scratch,
        compiler_params=pltpu.CompilerParams(vmem_limit_bytes=24 * 1024 * 1024),
        cost_estimate=pl.CostEstimate(flops=flops, bytes_accessed=2000000, transcendentals=0),
    )(*[placed_input(*given) for given in ins])


def start(sems, *pairs):
    copies = [
        pltpu.make_async_copy(source, target, sems.at[at]) for at, source, target in pairs
    ]
    for copy in copies:
        copy.start()
    return copies


def row_before(planes):
    wide = planes.astype(F32)
    rolled = pltpu.roll(wide, 1, 1)
    at = lax.broadcasted_iota(jnp.int32, wide.shape, 1)
    return jnp.where(at == 0, 0.0, rolled).astype(BF16)


def row_after(planes):
    wide = planes.astype(F32)
    rolled = pltpu.roll(wide, HALF - 1, 1)
    at = lax.broadcasted_iota(jnp.int32, wide.shape, 1)
    return jnp.where(at == HALF - 1, 0.0, rolled).astype(BF16)


def fill_windows(windows, at, even, odd):
    by_row = (row_before(odd), even, odd, row_after(even))
    edge = jnp.zeros((HALF, CH), BF16)
    for row, planes in enumerate(by_row):
        flat = planes.reshape(CELLS, CH)
        for tap in range(3):
            lanes = pl.ds((tap * 4 + row) * CH, CH)
            if tap == 0:
                windows[pl.ds(at, HALF), lanes] = edge
                windows[pl.ds(at + HALF, CELLS - HALF), lanes] = flat[: CELLS - HALF]
            elif tap == 1:
                windows[pl.ds(at, CELLS), lanes] = flat
            else:
                windows[pl.ds(at, CELLS - HALF), lanes] = flat[HALF:]
                windows[pl.ds(at + CELLS - HALF, HALF), lanes] = edge


def silu_slope(preact):
    sigma = jax.nn.sigmoid(preact)
    return sigma * (1.0 + preact * (1.0 - sigma))


def first_body(
    prior, own_far, plane_far, time_far, down_far,
    pre_out, hidden_out, cells_out, source_out, strided_out,
    own, first_plane, first_time, down_plane, spread, windows, both, sems,
):
    loads = start(
        sems,
        (0, own_far, own),
        (1, plane_far, first_plane),
        (2, time_far, first_time),
        (3, down_far, down_plane),
    )
    both[...] = jnp.zeros_like(both)
    for frame in range(4):
        if frame == 2:
            loads[0].wait()
        source = prior if frame < 2 else own
        spread[...] = source[pl.ds(frame % 2 * 2 * CELLS, 2 * CELLS), :].astype(F32)
        planes = []
        for par in range(2):
            cols = [
                spread[pl.ds(par * COLS + col, HALF, stride=2 * COLS), :] for col in range(COLS)
            ]
            planes.append(jnp.stack(cols, axis=0).astype(BF16))
            if frame >= 2:
                source_out[frame - 2, par] = planes[par]
        fill_windows(windows, frame * CELLS, planes[0], planes[1])
    loads[1].wait()
    for tap in range(3):
        for row in range(4):
            rows = pl.ds((tap * 4 + row) * CH, CH)
            if row < 3:
                both[rows, pl.ds(0, CH)] = first_plane[row, tap]
            if row > 0:
                both[rows, pl.ds(CH, CH)] = first_plane[row - 1, tap]
    for frame in range(4):
        pre = dot(windows[pl.ds(frame * CELLS, CELLS), :], both[...])
        hid = (pre * jax.nn.sigmoid(pre)).astype(BF16)
        for par in range(2):
            hidden_out[frame, par] = hid[:, par * CH : (par + 1) * CH]
            if frame >= 2:
                pre_out[frame - 2, par] = pre[:, par * CH : (par + 1) * CH]
    loads[2].wait()
    times = first_time[...].reshape(3 * CH, CH)
    for frame in range(2):
        mixed = []
        for par in range(2):
            taps = jnp.concatenate([hidden_out[frame + k, par] for k in range(3)], axis=1)
            here = source_out[frame, par].reshape(CELLS, CH).astype(F32) + dot(taps, times)
            mixed.append(here.astype(BF16).reshape(COLS, HALF, CH))
        by_row = (row_before(mixed[1]), mixed[0], mixed[1])
        for row in range(3):
            for tap in range(3):
                lanes = pl.ds((row * 3 + tap) * CH, CH)
                for col in range(COLS // 2):
                    rows = pl.ds(frame * DOWN + col * HALF, HALF)
                    where = 2 * col + tap - 1
                    if where < 0:
                        cells_out[rows, lanes] = jnp.zeros((HALF, CH), BF16)
                    else:
                        cells_out[rows, lanes] = by_row[row][where]
    loads[3].wait()
    kernel = down_plane[...].reshape(9 * CH, WIDE)
    strided_out[...] = dot(cells_out[...], kernel).astype(BF16).reshape(2, DOWN, WIDE)


def rows_body(rows, last_far, sent_out, last_time, spread, padded, turned, sems):
    loads = start(sems, (0, last_far, last_time))
    cotan = rows[...].astype(F32)
    spread[...] = cotan.reshape(HALF * 8, CH)
    for half in range(2):
        padded[pl.ds(0, DOWN), pl.ds(half * CH, CH)] = spread[pl.ds(half, DOWN, stride=2), :]
    padded[pl.ds(DOWN, 8), :] = jnp.zeros((8, WIDE), F32)
    loads[0].wait()
    total = padded[pl.ds(0, DOWN), :]
    for k in range(3):
        taps = padded[pl.ds(4 * (2 - k), DOWN), :].astype(BF16)
        total = total + dot_nt(taps, last_time[k])
    for half in range(2):
        turned[pl.ds(half, DOWN, stride=2), :] = total[:, half * CH : (half + 1) * CH]
    both = jnp.concatenate([turned[...].reshape(HALF, 8, CH), cotan], axis=1)
    sent_out[...] = both.astype(BF16)


def cotan_body(
    own, received, down_far,
    grad_lowered_out, cot_out, part_out, times_out,
    down_time, spread, sems,
):
    loads = start(sems, (0, down_far, down_time))
    spread[...] = received[...].astype(F32).reshape(HALF * 16, CH)
    for at, out in ((0, grad_lowered_out), (8, cot_out)):
        parts = []
        for col in range(4):
            halves = [
                spread[pl.ds(at + col * 2 + half, HALF, stride=16), :] for half in range(2)
            ]
            parts.append(jnp.concatenate(halves, axis=1))
        out[...] = jnp.concatenate(parts, axis=0).astype(BF16)
    loads[0].wait()
    part_out[...] = dot(own[0], down_time[2])
    times_out[...] = down_time[pl.ds(0, 2)]


def middle_body(prior, part, times, grad_lowered, cot, lowered_out, sent_out):
    pre = dot(prior[0], times[0]) + dot(prior[1], times[1]) + part[...]
    lowered_out[...] = (pre * jax.nn.sigmoid(pre)).astype(BF16)
    sent_out[pl.ds(0, DOWN), :] = (grad_lowered[...].astype(F32) * silu_slope(pre)).astype(BF16)
    sent_out[pl.ds(DOWN, DOWN), :] = cot[...]


BACK = (
    (0, 0, 0, 0, 1, 1),
    (0, 1, 0, 1, 1, 0),
    (0, 1, 0, 0, 1, 2),
    (1, 0, 1, 0, 0, 1),
    (1, 0, 0, 0, 2, 1),
    (1, 1, 1, 1, 0, 0),
    (1, 1, 1, 0, 0, 2),
    (1, 1, 0, 1, 2, 0),
    (1, 1, 0, 0, 2, 2),
)


def time_grads_body(
    sent, lowered, prior, own, down_far, plane_far,
    part_out, times_out, kernels_out, grad_down_time_out, grad_last_out, lowered_out,
    down_time, down_plane, turned, sems,
):
    loads = start(sems, (0, down_far, down_time), (1, plane_far, down_plane))
    kernels_out[...] = jnp.zeros_like(kernels_out)
    wide = lowered[...].astype(F32)
    for col in range(4):
        for half in range(2):
            turned[pl.ds(col * 2 + half, HALF, stride=8), :] = wide[
                col * HALF : (col + 1) * HALF, half * CH : (half + 1) * CH
            ]
    lowered_out[...] = turned[...].reshape(HALF // 2, 2, 8, CH).astype(BF16)
    taps = (prior[0], prior[1], own[0])
    grad_pre = sent[pl.ds(0, DOWN), :]
    for k in range(3):
        down = dot_tn(taps[k], grad_pre)
        for half in range(2):
            lanes = slice(half * CH, (half + 1) * CH)
            grad_down_time_out[half, pl.ds(k * WIDE, WIDE), :] = down[:, lanes]
    last = dot_tn(lowered[...], sent[pl.ds(DOWN, DOWN), :])
    for half in range(2):
        grad_last_out[half] = last[:, half * CH : (half + 1) * CH]
    for load in loads:
        load.wait()
    part_out[...] = dot_nt(grad_pre, down_time[2])
    times_out[...] = down_time[pl.ds(0, 2)]
    for row_par, col_par, row_off, col_off, row, tap in BACK:
        rows = pl.ds((row_par * 2 + col_par) * CH, CH)
        lanes = pl.ds((row_off * 2 + col_off) * WIDE, WIDE)
        kernels_out[rows, lanes] = down_plane[row, tap]


def back_body(ahead, part, times, kernels, grad_strided_out, sent_out, shifted):
    following = ahead[pl.ds(0, DOWN), :]
    for half in range(2):
        sent_out[pl.ds(4 * CELLS + half * DOWN, DOWN), :] = ahead[
            pl.ds(DOWN, DOWN), pl.ds(half * CH, CH)
        ]
    even = part[...] + dot_nt(following, times[0])
    odd = dot_nt(following, times[1])
    for frame, strided in ((0, even.astype(BF16)), (1, odd.astype(BF16))):
        grad_strided_out[pl.ds(frame * DOWN, DOWN), :] = strided
        planes = strided.reshape(4, HALF, WIDE)
        for row_off, rows in ((0, planes), (1, row_after(planes))):
            flat = rows.reshape(DOWN, WIDE)
            here = pl.ds((row_off * 2) * WIDE, WIDE)
            after = pl.ds((row_off * 2 + 1) * WIDE, WIDE)
            shifted[pl.ds(frame * DOWN, DOWN), here] = flat
            shifted[pl.ds(frame * DOWN, DOWN - HALF), after] = flat[HALF:]
            shifted[pl.ds(frame * DOWN + DOWN - HALF, HALF), after] = jnp.zeros((HALF, WIDE), BF16)
    mixed = dot_nt(shifted[...], kernels[...]).astype(BF16)
    for frame in range(2):
        for par in range(2):
            for col_par in range(2):
                lanes = slice((par * 2 + col_par) * CH, (par * 2 + col_par + 1) * CH)
                for col in range(4):
                    rows = slice(frame * DOWN + col * HALF, frame * DOWN + (col + 1) * HALF)
                    plane = (frame * 2 + par) * COLS + 2 * col + col_par
                    sent_out[pl.ds(plane * HALF, HALF), :] = mixed[rows, lanes]


def plane_grads_body(
    core, grad_strided, grad_mixed, cells, hidden, source, pre, time_far,
    grad_down_time, grad_last, lowered, lowered_rows, ahead,
    mine_out, other_out, windows_out, slope_out, part_out, time_out,
    flat, sems,
):
    loads = start(sems, (0, time_far, time_out))
    base = 3 * CH + 18 * CH
    flat[pl.ds(base, 6 * WIDE), :] = grad_down_time[...].reshape(6 * WIDE, CH)
    base += 6 * WIDE
    flat[pl.ds(base, 2 * WIDE), :] = grad_last[...].reshape(2 * WIDE, CH)
    base += 2 * WIDE
    last = dot_tn(lowered[...], ahead[pl.ds(DOWN, DOWN), :])
    for half in range(2):
        flat[pl.ds(base + half * WIDE, WIDE), :] = last[:, half * CH : (half + 1) * CH]
    down = dot_tn(cells[...], grad_strided[...])
    for half in range(2):
        at = 3 * CH + half * 9 * CH
        flat[pl.ds(at, 9 * CH), :] = down[:, half * CH : (half + 1) * CH]
    cotan = grad_mixed[pl.ds(0, 4 * CELLS), :]
    for k in range(3):
        taps = hidden[pl.ds(k, 2)].reshape(4 * CELLS, CH)
        flat[pl.ds(k * CH, CH), :] = dot_tn(taps, cotan)
    here = core[0]
    half = mine_out.shape[0]
    mine_out[...] = flat[pl.ds(pl.multiple_of(here * half, 16), half), :]
    other_out[pl.ds(0, half), :] = flat[
        pl.ds(pl.multiple_of((1 - here) * half, 16), half), :
    ].astype(BF16)
    away = lowered_rows[:, pl.ds(1 - here, 1)].astype(F32).reshape(DOWN, CH)
    other_out[pl.ds(half, DOWN), :] = away.astype(BF16)
    loads[0].wait()
    for frame in range(2):
        fill_windows(windows_out, frame * CELLS, source[frame, 0], source[frame, 1])
    slope_out[...] = silu_slope(pre[...])
    for par in range(2):
        first, second = [
            grad_mixed[pl.ds((frame * 2 + par) * CELLS, CELLS), :] for frame in range(2)
        ]
        part_out[0, par] = dot_nt(first, time_out[2]) + dot_nt(second, time_out[1])
        part_out[1, par] = dot_nt(second, time_out[2])


def last_body(
    core, ahead, windows, slope, part, first_time, lowered, early_other,
    mine_out, other_out,
    flat,
):
    cotans = [[], []]
    for par in range(2):
        first, second = [
            ahead[pl.ds((frame * 2 + par) * CELLS, CELLS), :] for frame in range(2)
        ]
        hidden = (
            part[0, par] + dot_nt(first, first_time[0]),
            part[1, par] + dot_nt(first, first_time[1]) + dot_nt(second, first_time[0]),
        )
        for frame in range(2):
            cotans[frame].append((hidden[frame] * slope[frame, par]).astype(BF16))
    cotan = jnp.concatenate([jnp.concatenate(parts, axis=1) for parts in cotans], axis=0)
    product = dot_tn(windows[...], cotan)
    for row in range(3):
        for tap in range(3):
            at = (tap * 4 + row) * CH
            flat[pl.ds((row * 3 + tap) * CH, CH), :] = (
                product[at : at + CH, :CH] + product[at + CH : at + 2 * CH, CH:]
            )
    further = [ahead[pl.ds(4 * CELLS + half * DOWN, DOWN), :] for half in range(2)]
    for half in range(2):
        flat[pl.ds(9 * CH + half * WIDE, WIDE), :] = dot_tn(lowered[...], further[half])
    here = core[0]
    half = mine_out.shape[0]
    mine_out[...] = flat[pl.ds(pl.multiple_of(here * half, 16), half), :]
    rows = early_other.shape[0]
    other_out[pl.ds(0, rows), :] = early_other[...]
    other_out[pl.ds(rows, half), :] = flat[
        pl.ds(pl.multiple_of((1 - here) * half, 16), half), :
    ].astype(BF16)


def halves_body(early, late, other, half_out):
    rows, more = early.shape[0], late.shape[0]
    half_out[pl.ds(0, rows), :] = (early[...] + other[pl.ds(0, rows), :].astype(F32)).astype(BF16)
    half_out[pl.ds(rows, more), :] = (
        late[...] + other[pl.ds(rows + DOWN, more), :].astype(F32)
    ).astype(BF16)


def sum_body(core, blocks, own, other, sent_out, padded):
    rows = blocks.shape[1]
    total = blocks[0].astype(F32)
    for block in range(1, blocks.shape[0]):
        total = total + blocks[block].astype(F32)
    padded[...] = jnp.zeros_like(padded)
    padded[pl.ds(0, rows), :] = total
    chips = sent_out.shape[0]
    sent_out[:, pl.ds(0, 16), :] = padded[...].reshape(chips, 16, CH).astype(BF16)
    here = core[0]
    mine = own[:, pl.ds(here, 1)].astype(F32).reshape(chips, 8, CH)
    theirs = other[pl.ds(EARLY // 2, DOWN), :].astype(F32).reshape(chips, 8, CH)
    frames = [jnp.where(here == 0, mine, theirs), jnp.where(here == 0, theirs, mine)]
    sent_out[:, pl.ds(16, 16), :] = jnp.concatenate(frames, axis=1).astype(BF16)


def piece_body(received, piece_out):
    chips = received.shape[0]
    total = received[0, pl.ds(0, 16), :].astype(F32)
    for chip in range(1, chips):
        total = total + received[chip, pl.ds(0, 16), :].astype(F32)
    piece = total.astype(BF16)
    for chip in range(chips):
        piece_out[chip] = piece


def spread_body(pieces, part_out):
    flat = pieces[...].reshape(-1, CH).astype(F32)
    part = flat[: part_out.shape[1]].astype(BF16)
    for block in range(part_out.shape[0]):
        part_out[block] = part


def results_body(
    core, mine, other,
    first_plane_out, first_time_out, down_plane_out, down_time_out, last_time_out,
    early, late,
):
    here = core[0]
    rows, more = EARLY // 2, LATE // 2
    for half, at in ((mine, here), (other, 1 - here)):
        early[pl.ds(pl.multiple_of(at * rows, 16), rows), :] = half[pl.ds(0, rows), :]
        late[pl.ds(pl.multiple_of(at * more, 16), more), :] = half[pl.ds(rows, more), :]
    first_plane_out[...] = late[pl.ds(0, 9 * CH), :]
    first_time_out[...] = early[pl.ds(0, 3 * CH), :]
    for half in range(2):
        lanes = pl.ds(half * CH, CH)
        down_plane_out[:, lanes] = early[pl.ds(3 * CH + half * 9 * CH, 9 * CH), :]
        down_time_out[:, lanes] = early[pl.ds(21 * CH + half * 6 * CH, 6 * CH), :]
        last_time_out[pl.ds(0, WIDE), lanes] = late[pl.ds(9 * CH + half * WIDE, WIDE), :]
        last_time_out[pl.ds(WIDE, WIDE), lanes] = early[pl.ds(37 * CH + half * WIDE, WIDE), :]
        last_time_out[pl.ds(2 * WIDE, WIDE), lanes] = early[pl.ds(33 * CH + half * WIDE, WIDE), :]


def output_body(received, last_time, output, spread, padded):
    frames = received[:, pl.ds(16, 16), :]
    spread[...] = frames.astype(F32).reshape(HALF * 8, CH)
    padded[pl.ds(0, 8), :] = jnp.zeros((8, WIDE), F32)
    for half in range(2):
        padded[pl.ds(8, DOWN), pl.ds(half * CH, CH)] = spread[pl.ds(half, DOWN, stride=2), :]
    total = padded[pl.ds(8, DOWN), :]
    for k in range(3):
        taps = padded[pl.ds(4 * k, DOWN), :].astype(BF16)
        total = total + dot(taps, last_time[k])
    output[...] = total.astype(BF16)


def from_behind(block, distance):
    devices = range(lax.axis_size("seq"))
    route = [(i - distance, i) for i in devices if i - distance in devices]
    return lax.ppermute(block, "seq", route)


def swap_cores(block):
    count = lax.axis_size("seq")
    return lax.ppermute(block, "seq", [(i, i ^ 1) for i in range(count)])


def exchange_clip(blocks):
    return lax.all_to_all(blocks, "clip", split_axis=0, concat_axis=0, tiled=True)


def exchange_seq(blocks):
    return lax.all_to_all(blocks, "seq", split_axis=0, concat_axis=0, tiled=True)


def exchange_depth(blocks):
    count = lax.axis_size("seq")
    groups = [list(range(core, count, 2)) for core in range(2)]
    return lax.all_to_all(
        blocks, "seq", split_axis=0, concat_axis=0, axis_index_groups=groups, tiled=True
    )


def local(clip_in, first_plane, first_time, down_plane, down_time, last_time, cotan_out):
    own = clip_in.reshape(4 * CELLS, CH)
    prior = from_behind(own, 1)
    (sent,) = call(
        rows_body,
        [(V, cotan_out[0].reshape(HALF, 8, CH)), (H, last_time)],
        [(V, (HALF, 16, CH), BF16)],
        [
            ((3, WIDE, WIDE), BF16),
            ((HALF * 8, CH), F32),
            ((DOWN + 8, WIDE), F32),
            ((HALF * 8, CH), F32),
        ],
        copies=1,
        flops=60000000,
    )
    sent, prior = lax.optimization_barrier((sent, prior))
    received = exchange_seq(sent)
    flat_frames = (2, 2, CELLS, CH)
    pre_first, hidden, cells, source, strided = call(
        first_body,
        [(V, prior), (H, own), (H, first_plane), (H, first_time), (H, down_plane)],
        [
            (P_, flat_frames, F32),
            (P_, (4, 2, CELLS, CH), BF16),
            (P_, (2 * DOWN, 9 * CH), BF16),
            (P_, (2, 2, COLS, HALF, CH), BF16),
            (P_, (2, DOWN, WIDE), BF16),
        ],
        [
            ((4 * CELLS, CH), BF16),
            ((3, 3, CH, CH), BF16),
            ((3, CH, CH), BF16),
            ((3, 3, CH, WIDE), BF16),
            ((2 * CELLS, CH), F32),
            ((4 * CELLS, 12 * CH), BF16),
            ((12 * CH, WIDE), BF16),
        ],
        copies=4,
        flops=2000000000,
    )
    strided_prior = from_behind(strided, 1)
    times = (P_, (2, WIDE, WIDE), BF16)
    down = (P_, (DOWN, WIDE), BF16)
    grad_lowered, cot, part, near_times = call(
        cotan_body,
        [(P_, strided), (V, received), (H, down_time)],
        [down, down, (P_, (DOWN, WIDE), F32), times],
        [((3, WIDE, WIDE), BF16), ((HALF * 16, CH), F32)],
        copies=1,
        flops=100000000,
    )
    lowered, sent = call(
        middle_body,
        [(V, strided_prior), (P_, part), (P_, near_times), (P_, grad_lowered), (P_, cot)],
        [down, (P_, (2 * DOWN, WIDE), BF16)],
        flops=60000000,
    )
    ahead = from_behind(sent, -1)
    part, near_times, kernels, grad_down_time, grad_last, lowered_rows = call(
        time_grads_body,
        [
            (P_, sent), (P_, lowered), (V, strided_prior), (P_, strided),
            (H, down_time), (H, down_plane),
        ],
        [
            (P_, (DOWN, WIDE), F32),
            times,
            (P_, (4 * CH, 4 * WIDE), BF16),
            (P_, (2, 3 * WIDE, CH), F32),
            (P_, (2, WIDE, CH), F32),
            (P_, (HALF // 2, 2, 8, CH), BF16),
        ],
        [((3, WIDE, WIDE), BF16), ((3, 3, CH, WIDE), BF16), ((HALF * 8, CH), F32)],
        copies=2,
        flops=120000000,
    )
    grad_strided, sent = call(
        back_body,
        [(V, ahead), (P_, part), (P_, near_times), (P_, kernels)],
        [(P_, (2 * DOWN, WIDE), BF16), (P_, (4 * CELLS + 2 * DOWN, CH), BF16)],
        [((2 * DOWN, 4 * WIDE), BF16)],
        flops=300000000,
    )
    further = from_behind(sent, -1)
    core = (lax.axis_index("seq") % 2).astype(jnp.int32).reshape(1)
    early, early_other, windows, slope, part, near_time = call(
        plane_grads_body,
        [
            (S, core), (P_, grad_strided), (P_, sent),
            (P_, cells), (P_, hidden), (P_, source), (P_, pre_first), (H, first_time),
            (P_, grad_down_time), (P_, grad_last), (P_, lowered), (P_, lowered_rows), (V, ahead),
        ],
        [
            (P_, (EARLY // 2, CH), F32),
            (P_, (EARLY // 2 + DOWN, CH), BF16),
            (P_, (2 * CELLS, 12 * CH), BF16),
            (P_, flat_frames, F32),
            (P_, flat_frames, F32),
            (P_, (3, CH, CH), BF16),
        ],
        [((EARLY, CH), F32)],
        copies=1,
        flops=500000000,
    )
    late, other = call(
        last_body,
        [
            (S, core), (V, further), (P_, windows), (P_, slope), (P_, part), (P_, near_time),
            (P_, lowered), (P_, early_other),
        ],
        [(P_, (LATE // 2, CH), F32), (P_, ((EARLY + LATE) // 2 + DOWN, CH), BF16)],
        [((LATE, CH), F32)],
        flops=600000000,
    )

    clips = lax.axis_size("clip")
    chips = lax.axis_size("seq") // 2
    half_rows = (EARLY + LATE) // 2
    part_rows = half_rows // clips
    other = swap_cores(other)
    (half,) = call(
        halves_body,
        [(P_, early), (P_, late), (V, other)],
        [(P_, (half_rows, CH), BF16)],
    )
    blocks = exchange_clip(half.reshape(clips, part_rows, CH))
    (sent,) = call(
        sum_body,
        [(S, core), (V, blocks), (P_, lowered_rows), (V, other)],
        [(V, (chips, 32, CH), BF16)],
        [((16 * chips, CH), F32)],
    )
    received = exchange_depth(sent)
    (pieces,) = call(piece_body, [(V, received)], [(V, (chips, 16, CH), BF16)])
    pieces = exchange_depth(pieces)
    (output,) = call(
        output_body,
        [(V, received), (V, last_time)],
        [(V, (DOWN, WIDE), BF16)],
        [((HALF * 8, CH), F32), ((DOWN + 8, WIDE), F32)],
        flops=60000000,
    )
    (parts,) = call(spread_body, [(V, pieces)], [(V, (clips, part_rows, CH), BF16)])
    half = exchange_clip(parts).reshape(half_rows, CH)
    other = swap_cores(half)
    grads = call(
        results_body,
        [(S, core), (V, half), (V, other)],
        [
            (V, (9 * CH, CH), BF16),
            (V, (3 * CH, CH), BF16),
            (V, (9 * CH, WIDE), BF16),
            (V, (3 * WIDE, WIDE), BF16),
            (V, (3 * WIDE, WIDE), BF16),
        ],
        [((EARLY, CH), BF16), ((LATE, CH), BF16)],
    )
    shapes = ((3, 3, CH, CH), (3, CH, CH), (3, 3, CH, WIDE), (3, WIDE, WIDE), (3, WIDE, WIDE))
    grads = [grad.reshape(shape) for grad, shape in zip(grads, shapes)]
    return (output.reshape(1, HALF, 1, 4, WIDE), *grads)


def solution(mesh):
    placed = (
        P("clip", "seq", None, None, None),
        P(),
        P(),
        P(),
        P(),
        P(),
        P("clip", None, "seq", None, None),
    )
    return jax.shard_map(
        local,
        mesh=mesh,
        in_specs=placed,
        out_specs=(P("clip", None, "seq", None, None), P(), P(), P(), P(), P()),
        check_vma=False,
    )
```

```python
import jax
import jax.numpy as jnp
from jax import lax
from jax.experimental import pallas as pl
from jax.experimental.pallas import tpu as pltpu
from jax.sharding import PartitionSpec as P


F32 = jnp.float32
BF16 = jnp.bfloat16
COLS = 8
HALF = 32
CELLS = COLS * HALF
DOWN = CELLS // 2
CH = 128
WIDE = 256
EARLY = (3 + 18 + 12 + 8) * CH
LATE = (9 + 4) * CH
NEAR = 4


def dot(left, right):
    return lax.dot_general(left, right, (((1,), (0,)), ((), ())), preferred_element_type=F32)


def dot_nt(left, right):
    return lax.dot_general(left, right, (((1,), (1,)), ((), ())), preferred_element_type=F32)


def dot_tn(left, right):
    return lax.dot_general(left, right, (((0,), (0,)), ((), ())), preferred_element_type=F32)


V, P_, H, S = "vmem", "pinned", "hbm", "smem"
SPACES = {V: pltpu.VMEM, P_: pltpu.VMEM, H: pltpu.HBM, S: pltpu.SMEM}


def placed_input(space, array):
    if space in (P_, H):
        return pltpu.with_memory_space_constraint(array, SPACES[space])
    return array


def placed_output(space, shape, kind):
    if space in (P_, H):
        return SPACES[space](shape, kind)
    return jax.ShapeDtypeStruct(shape, kind)


def call(body, ins, outs, scratch=(), copies=0, flops=0):
    scratch = [pltpu.VMEM(shape, kind) for shape, kind in scratch]
    if copies:
        scratch.append(pltpu.SemaphoreType.DMA((copies,)))
    return pl.pallas_call(
        body,
        out_shape=[placed_output(*out) for out in outs],
        in_specs=[pl.BlockSpec(memory_space=SPACES[space]) for space, _ in ins],
        out_specs=[pl.BlockSpec(memory_space=SPACES[space]) for space, _, _ in outs],
        scratch_shapes=scratch,
        compiler_params=pltpu.CompilerParams(vmem_limit_bytes=24 * 1024 * 1024),
        cost_estimate=pl.CostEstimate(flops=flops, bytes_accessed=2000000, transcendentals=0),
    )(*[placed_input(*given) for given in ins])


def start(sems, *pairs):
    copies = [
        pltpu.make_async_copy(source, target, sems.at[at]) for at, source, target in pairs
    ]
    for copy in copies:
        copy.start()
    return copies


def row_before(planes):
    wide = planes.astype(F32)
    rolled = pltpu.roll(wide, 1, 1)
    at = lax.broadcasted_iota(jnp.int32, wide.shape, 1)
    return jnp.where(at == 0, 0.0, rolled).astype(BF16)


def row_after(planes):
    wide = planes.astype(F32)
    rolled = pltpu.roll(wide, HALF - 1, 1)
    at = lax.broadcasted_iota(jnp.int32, wide.shape, 1)
    return jnp.where(at == HALF - 1, 0.0, rolled).astype(BF16)


def fill_windows(windows, at, even, odd):
    by_row = (row_before(odd), even, odd, row_after(even))
    edge = jnp.zeros((HALF, CH), BF16)
    for row, planes in enumerate(by_row):
        flat = planes.reshape(CELLS, CH)
        for tap in range(3):
            lanes = pl.ds((tap * 4 + row) * CH, CH)
            if tap == 0:
                windows[pl.ds(at, HALF), lanes] = edge
                windows[pl.ds(at + HALF, CELLS - HALF), lanes] = flat[: CELLS - HALF]
            elif tap == 1:
                windows[pl.ds(at, CELLS), lanes] = flat
            else:
                windows[pl.ds(at, CELLS - HALF), lanes] = flat[HALF:]
                windows[pl.ds(at + CELLS - HALF, HALF), lanes] = edge


def silu_slope(preact):
    sigma = jax.nn.sigmoid(preact)
    return sigma * (1.0 + preact * (1.0 - sigma))


def parity_planes(source, frame, spread):
    spread[...] = source[pl.ds(frame * 2 * CELLS, 2 * CELLS), :].astype(F32)
    planes = []
    for par in range(2):
        cols = [spread[pl.ds(par * COLS + col, HALF, stride=2 * COLS), :] for col in range(COLS)]
        planes.append(jnp.stack(cols, axis=0).astype(BF16))
    return planes


def first_body(
    prior, acts, both, time_far, down_far,
    hidden_out, cells_out, strided_out,
    first_time, down_plane, spread, windows, sems,
):
    loads = start(sems, (0, time_far, first_time), (1, down_far, down_plane))
    for frame in range(2):
        fill_windows(windows, frame * CELLS, *parity_planes(prior, frame, spread))
    for frame in range(2):
        pre = dot(windows[pl.ds(frame * CELLS, CELLS), :], both[...])
        hid = (pre * jax.nn.sigmoid(pre)).astype(BF16)
        for par in range(2):
            hidden_out[frame, par] = hid[:, par * CH : (par + 1) * CH]
    loads[0].wait()
    times = first_time[...].reshape(3 * CH, CH)
    for frame in range(2):
        mixed = []
        for par in range(2):
            hid = [hidden_out[0, par], hidden_out[1, par], acts[0, par], acts[1, par]]
            taps = jnp.concatenate(hid[frame : frame + 3], axis=1)
            here = acts[2 + frame, par].astype(F32) + dot(taps, times)
            mixed.append(here.astype(BF16).reshape(COLS, HALF, CH))
        by_row = (row_before(mixed[1]), mixed[0], mixed[1])
        for row in range(3):
            for tap in range(3):
                lanes = pl.ds((row * 3 + tap) * CH, CH)
                for col in range(COLS // 2):
                    rows = pl.ds(frame * DOWN + col * HALF, HALF)
                    where = 2 * col + tap - 1
                    if where < 0:
                        cells_out[rows, lanes] = jnp.zeros((HALF, CH), BF16)
                    else:
                        cells_out[rows, lanes] = by_row[row][where]
    loads[1].wait()
    kernel = down_plane[...].reshape(9 * CH, WIDE)
    strided_out[...] = dot(cells_out[...], kernel).astype(BF16).reshape(2, DOWN, WIDE)


def own_body(
    rows, last_far, own_far, plane_far,
    sent_out, acts_out, pre_out, both_out,
    last_time, own, first_plane, spread, padded, turned, cells, windows, sems,
):
    loads = start(
        sems, (0, last_far, last_time), (1, own_far, own), (2, plane_far, first_plane)
    )
    both_out[...] = jnp.zeros_like(both_out)
    cotan = rows[...].astype(F32)
    spread[...] = cotan.reshape(HALF * 8, CH)
    for half in range(2):
        padded[pl.ds(0, DOWN), pl.ds(half * CH, CH)] = spread[pl.ds(half, DOWN, stride=2), :]
    padded[pl.ds(DOWN, 8), :] = jnp.zeros((8, WIDE), F32)
    loads[0].wait()
    total = padded[pl.ds(0, DOWN), :]
    for k in range(3):
        taps = padded[pl.ds(4 * (2 - k), DOWN), :].astype(BF16)
        total = total + dot_nt(taps, last_time[k])
    for half in range(2):
        turned[pl.ds(half, DOWN, stride=2), :] = total[:, half * CH : (half + 1) * CH]
    both = jnp.concatenate([turned[...].reshape(HALF, 8, CH), cotan], axis=1)
    sent_out[...] = both.astype(BF16)

    loads[1].wait()
    for frame in range(2):
        planes = parity_planes(own, frame, cells)
        fill_windows(windows, frame * CELLS, *planes)
        for par in range(2):
            acts_out[2 + frame, par] = planes[par].reshape(CELLS, CH)
    loads[2].wait()
    for tap in range(3):
        for row in range(4):
            at = pl.ds((tap * 4 + row) * CH, CH)
            if row < 3:
                both_out[at, pl.ds(0, CH)] = first_plane[row, tap]
            if row > 0:
                both_out[at, pl.ds(CH, CH)] = first_plane[row - 1, tap]
    for frame in range(2):
        pre = dot(windows[pl.ds(frame * CELLS, CELLS), :], both_out[...])
        hid = (pre * jax.nn.sigmoid(pre)).astype(BF16)
        for par in range(2):
            acts_out[frame, par] = hid[:, par * CH : (par + 1) * CH]
            pre_out[frame, par] = pre[:, par * CH : (par + 1) * CH]


def cotan_body(
    own, received, down_far,
    grad_lowered_out, cot_out, part_out, times_out,
    down_time, spread, sems,
):
    loads = start(sems, (0, down_far, down_time))
    spread[...] = received[...].astype(F32).reshape(HALF * 16, CH)
    for at, out in ((0, grad_lowered_out), (8, cot_out)):
        parts = []
        for col in range(4):
            halves = [
                spread[pl.ds(at + col * 2 + half, HALF, stride=16), :] for half in range(2)
            ]
            parts.append(jnp.concatenate(halves, axis=1))
        out[...] = jnp.concatenate(parts, axis=0).astype(BF16)
    loads[0].wait()
    part_out[...] = dot(own[0], down_time[2])
    times_out[...] = down_time[pl.ds(0, 2)]


def middle_body(prior, part, times, grad_lowered, cot, lowered_out, sent_out):
    pre = dot(prior[0], times[0]) + dot(prior[1], times[1]) + part[...]
    lowered_out[...] = (pre * jax.nn.sigmoid(pre)).astype(BF16)
    sent_out[pl.ds(0, DOWN), :] = (grad_lowered[...].astype(F32) * silu_slope(pre)).astype(BF16)
    sent_out[pl.ds(DOWN, DOWN), :] = cot[...]


BACK = (
    (0, 0, 0, 0, 1, 1),
    (0, 1, 0, 1, 1, 0),
    (0, 1, 0, 0, 1, 2),
    (1, 0, 1, 0, 0, 1),
    (1, 0, 0, 0, 2, 1),
    (1, 1, 1, 1, 0, 0),
    (1, 1, 1, 0, 0, 2),
    (1, 1, 0, 1, 2, 0),
    (1, 1, 0, 0, 2, 2),
)


def time_grads_body(
    sent, lowered, prior, own, down_far, plane_far,
    part_out, times_out, kernels_out, grads_out, lowered_out,
    down_time, down_plane, turned, sems,
):
    loads = start(sems, (0, down_far, down_time), (1, plane_far, down_plane))
    kernels_out[...] = jnp.zeros_like(kernels_out)
    wide = lowered[...].astype(F32)
    for col in range(4):
        for half in range(2):
            turned[pl.ds(col * 2 + half, HALF, stride=8), :] = wide[
                col * HALF : (col + 1) * HALF, half * CH : (half + 1) * CH
            ]
    lowered_out[...] = turned[...].reshape(HALF // 2, 2, 8, CH).astype(BF16)
    taps = (prior[0], prior[1], own[0])
    grad_pre = sent[pl.ds(0, DOWN), :]
    for k in range(3):
        down = dot_tn(taps[k], grad_pre)
        for half in range(2):
            lanes = slice(half * CH, (half + 1) * CH)
            grads_out[pl.ds((half * 3 + k) * WIDE, WIDE), :] = down[:, lanes]
    last = dot_tn(lowered[...], sent[pl.ds(DOWN, DOWN), :])
    for half in range(2):
        grads_out[pl.ds((6 + half) * WIDE, WIDE), :] = last[:, half * CH : (half + 1) * CH]
    for load in loads:
        load.wait()
    part_out[...] = dot_nt(grad_pre, down_time[2])
    times_out[...] = down_time[pl.ds(0, 2)]
    for row_par, col_par, row_off, col_off, row, tap in BACK:
        rows = pl.ds((row_par * 2 + col_par) * CH, CH)
        lanes = pl.ds((row_off * 2 + col_off) * WIDE, WIDE)
        kernels_out[rows, lanes] = down_plane[row, tap]


def back_body(ahead, part, times, kernels, grad_strided_out, sent_out, shifted):
    following = ahead[pl.ds(0, DOWN), :]
    for half in range(2):
        sent_out[pl.ds(4 * CELLS + half * DOWN, DOWN), :] = ahead[
            pl.ds(DOWN, DOWN), pl.ds(half * CH, CH)
        ]
    even = part[...] + dot_nt(following, times[0])
    odd = dot_nt(following, times[1])
    for frame, strided in ((0, even.astype(BF16)), (1, odd.astype(BF16))):
        grad_strided_out[pl.ds(frame * DOWN, DOWN), :] = strided
        planes = strided.reshape(4, HALF, WIDE)
        for row_off, rows in ((0, planes), (1, row_after(planes))):
            flat = rows.reshape(DOWN, WIDE)
            here = pl.ds((row_off * 2) * WIDE, WIDE)
            after = pl.ds((row_off * 2 + 1) * WIDE, WIDE)
            shifted[pl.ds(frame * DOWN, DOWN), here] = flat
            shifted[pl.ds(frame * DOWN, DOWN - HALF), after] = flat[HALF:]
            shifted[pl.ds(frame * DOWN + DOWN - HALF, HALF), after] = jnp.zeros((HALF, WIDE), BF16)
    mixed = dot_nt(shifted[...], kernels[...]).astype(BF16)
    for frame in range(2):
        for par in range(2):
            for col_par in range(2):
                lanes = slice((par * 2 + col_par) * CH, (par * 2 + col_par + 1) * CH)
                for col in range(4):
                    rows = slice(frame * DOWN + col * HALF, frame * DOWN + (col + 1) * HALF)
                    plane = (frame * 2 + par) * COLS + 2 * col + col_par
                    sent_out[pl.ds(plane * HALF, HALF), :] = mixed[rows, lanes]


def plane_grads_body(
    core, grad_strided, grad_mixed, cells, prior_hidden, acts, pre, time_far,
    grads, lowered, lowered_rows, ahead,
    mine_out, other_out, windows_out, slope_out, part_out, time_out,
    flat, sems,
):
    loads = start(sems, (0, time_far, time_out))
    base = 3 * CH + 18 * CH
    flat[pl.ds(base, 8 * WIDE), :] = grads[...]
    base += 8 * WIDE
    last = dot_tn(lowered[...], ahead[pl.ds(DOWN, DOWN), :])
    for half in range(2):
        flat[pl.ds(base + half * WIDE, WIDE), :] = last[:, half * CH : (half + 1) * CH]
    down = dot_tn(cells[...], grad_strided[...])
    for half in range(2):
        at = 3 * CH + half * 9 * CH
        flat[pl.ds(at, 9 * CH), :] = down[:, half * CH : (half + 1) * CH]
    cotan = grad_mixed[pl.ds(0, 4 * CELLS), :]
    early = prior_hidden[...].reshape(4 * CELLS, CH)
    late = acts[pl.ds(0, 2)].reshape(4 * CELLS, CH)
    for k in range(3):
        taps = (early, jnp.concatenate([early[2 * CELLS :], late[: 2 * CELLS]], axis=0), late)[k]
        flat[pl.ds(k * CH, CH), :] = dot_tn(taps, cotan)
    here = core[0]
    half = mine_out.shape[0]
    mine_out[...] = flat[pl.ds(pl.multiple_of(here * half, 16), half), :]
    other_out[pl.ds(0, half), :] = flat[
        pl.ds(pl.multiple_of((1 - here) * half, 16), half), :
    ].astype(BF16)
    away = lowered_rows[:, pl.ds(1 - here, 1)].astype(F32).reshape(DOWN, CH)
    other_out[pl.ds(half, DOWN), :] = away.astype(BF16)
    loads[0].wait()
    for frame in range(2):
        planes = [acts[2 + frame, par].reshape(COLS, HALF, CH) for par in range(2)]
        fill_windows(windows_out, frame * CELLS, *planes)
    slope_out[...] = silu_slope(pre[...])
    for par in range(2):
        first, second = [
            grad_mixed[pl.ds((frame * 2 + par) * CELLS, CELLS), :] for frame in range(2)
        ]
        part_out[0, par] = dot_nt(first, time_out[2]) + dot_nt(second, time_out[1])
        part_out[1, par] = dot_nt(second, time_out[2])


def last_body(
    core, ahead, windows, slope, part, first_time, lowered, early_other,
    mine_out, other_out,
    flat,
):
    cotans = [[], []]
    for par in range(2):
        first, second = [
            ahead[pl.ds((frame * 2 + par) * CELLS, CELLS), :] for frame in range(2)
        ]
        hidden = (
            part[0, par] + dot_nt(first, first_time[0]),
            part[1, par] + dot_nt(first, first_time[1]) + dot_nt(second, first_time[0]),
        )
        for frame in range(2):
            cotans[frame].append((hidden[frame] * slope[frame, par]).astype(BF16))
    cotan = jnp.concatenate([jnp.concatenate(parts, axis=1) for parts in cotans], axis=0)
    product = dot_tn(windows[...], cotan)
    for row in range(3):
        for tap in range(3):
            at = (tap * 4 + row) * CH
            flat[pl.ds((row * 3 + tap) * CH, CH), :] = (
                product[at : at + CH, :CH] + product[at + CH : at + 2 * CH, CH:]
            )
    further = [ahead[pl.ds(4 * CELLS + half * DOWN, DOWN), :] for half in range(2)]
    for half in range(2):
        flat[pl.ds(9 * CH + half * WIDE, WIDE), :] = dot_tn(lowered[...], further[half])
    here = core[0]
    half = mine_out.shape[0]
    mine_out[...] = flat[pl.ds(pl.multiple_of(here * half, 16), half), :]
    rows = early_other.shape[0]
    other_out[pl.ds(0, rows), :] = early_other[...]
    other_out[pl.ds(rows, half), :] = flat[
        pl.ds(pl.multiple_of((1 - here) * half, 16), half), :
    ].astype(BF16)


def halves_body(early, late, other, half_out):
    rows, more = early.shape[0], late.shape[0]
    half_out[pl.ds(0, rows), :] = (early[...] + other[pl.ds(0, rows), :].astype(F32)).astype(BF16)
    half_out[pl.ds(rows, more), :] = (
        late[...] + other[pl.ds(rows + DOWN, more), :].astype(F32)
    ).astype(BF16)


def sum_body(core, blocks, own, other, sent_out, padded):
    rows = blocks.shape[1]
    total = blocks[0].astype(F32)
    for block in range(1, blocks.shape[0]):
        total = total + blocks[block].astype(F32)
    padded[...] = jnp.zeros_like(padded)
    padded[pl.ds(0, rows), :] = total
    here = core[0]
    chips = own.shape[0]
    mine = own[:, pl.ds(here, 1)].astype(F32).reshape(chips, 8, CH)
    theirs = other[pl.ds(EARLY // 2, DOWN), :].astype(F32).reshape(chips, 8, CH)
    frames = [jnp.where(here == 0, mine, theirs), jnp.where(here == 0, theirs, mine)]
    frames = jnp.concatenate(frames, axis=1)
    near = sent_out.shape[0]
    share = padded.shape[0] // near
    for chip in range(near):
        sent_out[chip, pl.ds(0, share), :] = padded[pl.ds(chip * share, share), :].astype(BF16)
        for far in range(chips // near):
            sent_out[chip, pl.ds(share + far * 16, 16), :] = frames[far * near + chip].astype(BF16)


def first_rows(received, share):
    total = received[0, pl.ds(0, share), :].astype(F32)
    for chip in range(1, received.shape[0]):
        total = total + received[chip, pl.ds(0, share), :].astype(F32)
    return total.astype(BF16)


def near_body(received, sent_out):
    near, far = received.shape[0], sent_out.shape[0]
    share = sent_out.shape[1] - near * 16
    piece = first_rows(received, share)
    for there in range(far):
        sent_out[there, pl.ds(0, share), :] = piece
        for chip in range(near):
            sent_out[there, pl.ds(share + chip * 16, 16), :] = received[
                chip, pl.ds(share + there * 16, 16), :
            ]


def piece_body(received, piece_out):
    piece = first_rows(received, piece_out.shape[1])
    for chip in range(piece_out.shape[0]):
        piece_out[chip] = piece


def spread_body(pieces, part_out):
    flat = pieces[...].reshape(-1, CH).astype(F32)
    part = flat[: part_out.shape[1]].astype(BF16)
    for block in range(part_out.shape[0]):
        part_out[block] = part


def results_body(
    core, mine, other,
    first_plane_out, first_time_out, down_plane_out, down_time_out, last_time_out,
    early, late,
):
    here = core[0]
    rows, more = EARLY // 2, LATE // 2
    for half, at in ((mine, here), (other, 1 - here)):
        early[pl.ds(pl.multiple_of(at * rows, 16), rows), :] = half[pl.ds(0, rows), :]
        late[pl.ds(pl.multiple_of(at * more, 16), more), :] = half[pl.ds(rows, more), :]
    first_plane_out[...] = late[pl.ds(0, 9 * CH), :]
    first_time_out[...] = early[pl.ds(0, 3 * CH), :]
    for half in range(2):
        lanes = pl.ds(half * CH, CH)
        down_plane_out[:, lanes] = early[pl.ds(3 * CH + half * 9 * CH, 9 * CH), :]
        down_time_out[:, lanes] = early[pl.ds(21 * CH + half * 6 * CH, 6 * CH), :]
        last_time_out[pl.ds(0, WIDE), lanes] = late[pl.ds(9 * CH + half * WIDE, WIDE), :]
        last_time_out[pl.ds(WIDE, WIDE), lanes] = early[pl.ds(37 * CH + half * WIDE, WIDE), :]
        last_time_out[pl.ds(2 * WIDE, WIDE), lanes] = early[pl.ds(33 * CH + half * WIDE, WIDE), :]


def output_body(received, last_time, output, spread, padded):
    share = received.shape[1] - 16 * HALF // 2 // received.shape[0]
    for far in range(received.shape[0]):
        rows = received.shape[1] - share
        spread[pl.ds(far * rows, rows), :] = received[far, pl.ds(share, rows), :].astype(F32)
    padded[pl.ds(0, 8), :] = jnp.zeros((8, WIDE), F32)
    for half in range(2):
        padded[pl.ds(8, DOWN), pl.ds(half * CH, CH)] = spread[pl.ds(half, DOWN, stride=2), :]
    total = padded[pl.ds(8, DOWN), :]
    for k in range(3):
        taps = padded[pl.ds(4 * k, DOWN), :].astype(BF16)
        total = total + dot(taps, last_time[k])
    output[...] = total.astype(BF16)


def from_behind(block, distance):
    devices = range(lax.axis_size("seq"))
    route = [(i - distance, i) for i in devices if i - distance in devices]
    return lax.ppermute(block, "seq", route)


def swap_cores(block):
    count = lax.axis_size("seq")
    return lax.ppermute(block, "seq", [(i, i ^ 1) for i in range(count)])


def exchange_clip(blocks):
    return lax.all_to_all(blocks, "clip", split_axis=0, concat_axis=0, tiled=True)


def exchange_seq(blocks):
    return lax.all_to_all(blocks, "seq", split_axis=0, concat_axis=0, tiled=True)


def exchange_chips(blocks, near):
    count = lax.axis_size("seq") // 2
    runs = [list(range(first, first + NEAR)) for first in range(0, count, NEAR)]
    if not near:
        runs = [list(place) for place in zip(*runs)]
    groups = [[2 * chip + core for chip in run] for run in runs for core in range(2)]
    return lax.all_to_all(
        blocks, "seq", split_axis=0, concat_axis=0, axis_index_groups=groups, tiled=True
    )


def sum_body(core, blocks, own, other, sent_out, padded):
    rows = blocks.shape[1]
    total = blocks[0].astype(F32)
    for block in range(1, blocks.shape[0]):
        total = total + blocks[block].astype(F32)
    padded[...] = jnp.zeros_like(padded)
    padded[pl.ds(0, rows), :] = total
    here = core[0]
    chips = own.shape[0]
    mine = own[:, pl.ds(here, 1)].astype(F32).reshape(chips, 8, CH)
    theirs = other[pl.ds(EARLY // 2, DOWN), :].astype(F32).reshape(chips, 8, CH)
    frames = [jnp.where(here == 0, mine, theirs), jnp.where(here == 0, theirs, mine)]
    frames = jnp.concatenate(frames, axis=1)
    near = sent_out.shape[0]
    share = padded.shape[0] // near
    for chip in range(near):
        sent_out[chip, pl.ds(0, share), :] = padded[pl.ds(chip * share, share), :].astype(BF16)
        for far in range(chips // near):
            sent_out[chip, pl.ds(share + far * 16, 16), :] = frames[far * near + chip].astype(BF16)


def first_rows(received, share):
    total = received[0, pl.ds(0, share), :].astype(F32)
    for chip in range(1, received.shape[0]):
        total = total + received[chip, pl.ds(0, share), :].astype(F32)
    return total.astype(BF16)


def near_body(received, sent_out):
    near, far = received.shape[0], sent_out.shape[0]
    share = sent_out.shape[1] - near * 16
    piece = first_rows(received, share)
    for there in range(far):
        sent_out[there, pl.ds(0, share), :] = piece
        for chip in range(near):
            sent_out[there, pl.ds(share + chip * 16, 16), :] = received[
                chip, pl.ds(share + there * 16, 16), :
            ]


def piece_body(received, piece_out):
    piece = first_rows(received, piece_out.shape[1])
    for chip in range(piece_out.shape[0]):
        piece_out[chip] = piece


def spread_body(pieces, part_out):
    flat = pieces[...].reshape(-1, CH).astype(F32)
    part = flat[: part_out.shape[1]].astype(BF16)
    for block in range(part_out.shape[0]):
        part_out[block] = part


def results_body(
    core, mine, other,
    first_plane_out, first_time_out, down_plane_out, down_time_out, last_time_out,
    early, late,
):
    here = core[0]
    rows, more = EARLY // 2, LATE // 2
    for half, at in ((mine, here), (other, 1 - here)):
        early[pl.ds(pl.multiple_of(at * rows, 16), rows), :] = half[pl.ds(0, rows), :]
        late[pl.ds(pl.multiple_of(at * more, 16), more), :] = half[pl.ds(rows, more), :]
    first_plane_out[...] = late[pl.ds(0, 9 * CH), :]
    first_time_out[...] = early[pl.ds(0, 3 * CH), :]
    for half in range(2):
        lanes = pl.ds(half * CH, CH)
        down_plane_out[:, lanes] = early[pl.ds(3 * CH + half * 9 * CH, 9 * CH), :]
        down_time_out[:, lanes] = early[pl.ds(21 * CH + half * 6 * CH, 6 * CH), :]
        last_time_out[pl.ds(0, WIDE), lanes] = late[pl.ds(9 * CH + half * WIDE, WIDE), :]
        last_time_out[pl.ds(WIDE, WIDE), lanes] = early[pl.ds(37 * CH + half * WIDE, WIDE), :]
        last_time_out[pl.ds(2 * WIDE, WIDE), lanes] = early[pl.ds(33 * CH + half * WIDE, WIDE), :]


def output_body(received, last_time, output, spread, padded):
    share = received.shape[1] - 16 * HALF // 2 // received.shape[0]
    for far in range(received.shape[0]):
        rows = received.shape[1] - share
        spread[pl.ds(far * rows, rows), :] = received[far, pl.ds(share, rows), :].astype(F32)
    padded[pl.ds(0, 8), :] = jnp.zeros((8, WIDE), F32)
    for half in range(2):
        padded[pl.ds(8, DOWN), pl.ds(half * CH, CH)] = spread[pl.ds(half, DOWN, stride=2), :]
    total = padded[pl.ds(8, DOWN), :]
    for k in range(3):
        taps = padded[pl.ds(4 * k, DOWN), :].astype(BF16)
        total = total + dot(taps, last_time[k])
    output[...] = total.astype(BF16)


def from_behind(block, distance):
    devices = range(lax.axis_size("seq"))
    route = [(i - distance, i) for i in devices if i - distance in devices]
    return lax.ppermute(block, "seq", route)


def swap_cores(block):
    count = lax.axis_size("seq")
    return lax.ppermute(block, "seq", [(i, i ^ 1) for i in range(count)])


def exchange_clip(blocks):
    return lax.all_to_all(blocks, "clip", split_axis=0, concat_axis=0, tiled=True)


def exchange_seq(blocks):
    return lax.all_to_all(blocks, "seq", split_axis=0, concat_axis=0, tiled=True)


def exchange_depth(blocks):
    count = lax.axis_size("seq")
    groups = [list(range(core, count, 2)) for core in range(2)]
    return lax.all_to_all(
        blocks, "seq", split_axis=0, concat_axis=0, axis_index_groups=groups, tiled=True
    )


def local(clip_in, first_plane, first_time, down_plane, down_time, last_time, cotan_out):
    own = clip_in.reshape(4 * CELLS, CH)
    prior = from_behind(own, 1)
    flat_frames = (2, 2, CELLS, CH)
    sent, acts, pre_first, both = call(
        own_body,
        [(V, cotan_out[0].reshape(HALF, 8, CH)), (H, last_time), (H, own), (H, first_plane)],
        [
            (V, (HALF, 16, CH), BF16),
            (P_, (4, 2, CELLS, CH), BF16),
            (P_, flat_frames, F32),
            (P_, (12 * CH, WIDE), BF16),
        ],
        [
            ((3, WIDE, WIDE), BF16),
            ((4 * CELLS, CH), BF16),
            ((3, 3, CH, CH), BF16),
            ((HALF * 8, CH), F32),
            ((DOWN + 8, WIDE), F32),
            ((HALF * 8, CH), F32),
            ((2 * CELLS, CH), F32),
            ((2 * CELLS, 12 * CH), BF16),
        ],
        copies=3,
        flops=600000000,
    )
    sent, prior = lax.optimization_barrier((sent, prior))
    received = exchange_seq(sent)
    prior_hidden, cells, strided = call(
        first_body,
        [(V, prior), (P_, acts), (P_, both), (H, first_time), (H, down_plane)],
        [
            (P_, flat_frames, BF16),
            (P_, (2 * DOWN, 9 * CH), BF16),
            (P_, (2, DOWN, WIDE), BF16),
        ],
        [
            ((3, CH, CH), BF16),
            ((3, 3, CH, WIDE), BF16),
            ((2 * CELLS, CH), F32),
            ((2 * CELLS, 12 * CH), BF16),
        ],
        copies=2,
        flops=1000000000,
    )
    strided_prior = from_behind(strided, 1)
    times = (P_, (2, WIDE, WIDE), BF16)
    down = (P_, (DOWN, WIDE), BF16)
    grad_lowered, cot, part, near_times = call(
        cotan_body,
        [(P_, strided), (V, received), (H, down_time)],
        [down, down, (P_, (DOWN, WIDE), F32), times],
        [((3, WIDE, WIDE), BF16), ((HALF * 16, CH), F32)],
        copies=1,
        flops=100000000,
    )
    lowered, sent = call(
        middle_body,
        [(V, strided_prior), (P_, part), (P_, near_times), (P_, grad_lowered), (P_, cot)],
        [down, (P_, (2 * DOWN, WIDE), BF16)],
        flops=60000000,
    )
    ahead = from_behind(sent, -1)
    part, near_times, kernels, time_grads, lowered_rows = call(
        time_grads_body,
        [
            (P_, sent), (P_, lowered), (V, strided_prior), (P_, strided),
            (H, down_time), (H, down_plane),
        ],
        [
            (P_, (DOWN, WIDE), F32),
            times,
            (P_, (4 * CH, 4 * WIDE), BF16),
            (P_, (8 * WIDE, CH), F32),
            (P_, (HALF // 2, 2, 8, CH), BF16),
        ],
        [((3, WIDE, WIDE), BF16), ((3, 3, CH, WIDE), BF16), ((HALF * 8, CH), F32)],
        copies=2,
        flops=120000000,
    )
    grad_strided, sent = call(
        back_body,
        [(V, ahead), (P_, part), (P_, near_times), (P_, kernels)],
        [(P_, (2 * DOWN, WIDE), BF16), (P_, (4 * CELLS + 2 * DOWN, CH), BF16)],
        [((2 * DOWN, 4 * WIDE), BF16)],
        flops=300000000,
    )
    further = from_behind(sent, -1)
    core = (lax.axis_index("seq") % 2).astype(jnp.int32).reshape(1)
    early, early_other, windows, slope, part, near_time = call(
        plane_grads_body,
        [
            (S, core), (P_, grad_strided), (P_, sent),
            (P_, cells), (P_, prior_hidden), (P_, acts), (P_, pre_first), (H, first_time),
            (P_, time_grads), (P_, lowered), (P_, lowered_rows), (V, ahead),
        ],
        [
            (P_, (EARLY // 2, CH), F32),
            (P_, (EARLY // 2 + DOWN, CH), BF16),
            (P_, (2 * CELLS, 12 * CH), BF16),
            (P_, flat_frames, F32),
            (P_, flat_frames, F32),
            (P_, (3, CH, CH), BF16),
        ],
        [((EARLY, CH), F32)],
        copies=1,
        flops=500000000,
    )
    late, other = call(
        last_body,
        [
            (S, core), (V, further), (P_, windows), (P_, slope), (P_, part), (P_, near_time),
            (P_, lowered), (P_, early_other),
        ],
        [(P_, (LATE // 2, CH), F32), (P_, ((EARLY + LATE) // 2 + DOWN, CH), BF16)],
        [((LATE, CH), F32)],
        flops=600000000,
    )

    clips = lax.axis_size("clip")
    chips = lax.axis_size("seq") // 2
    half_rows = (EARLY + LATE) // 2
    part_rows = half_rows // clips
    other = swap_cores(other)
    (half,) = call(
        halves_body,
        [(P_, early), (P_, late), (V, other)],
        [(P_, (half_rows, CH), BF16)],
    )
    blocks = exchange_clip(half.reshape(clips, part_rows, CH))
    far = chips // NEAR
    share = 16 * (-(-part_rows // (16 * NEAR)))
    (sent,) = call(
        sum_body,
        [(S, core), (V, blocks), (P_, lowered_rows), (V, other)],
        [(V, (NEAR, share + far * 16, CH), BF16)],
        [((NEAR * share, CH), F32)],
    )
    received = exchange_chips(sent, True)
    (sent,) = call(near_body, [(V, received)], [(V, (far, share + NEAR * 16, CH), BF16)])
    received = exchange_chips(sent, False)
    (pieces,) = call(piece_body, [(V, received)], [(V, (NEAR, share, CH), BF16)])
    pieces = exchange_chips(pieces, True)
    (output,) = call(
        output_body,
        [(V, received), (V, last_time)],
        [(V, (DOWN, WIDE), BF16)],
        [((HALF * 8, CH), F32), ((DOWN + 8, WIDE), F32)],
        flops=60000000,
    )
    (parts,) = call(spread_body, [(V, pieces)], [(V, (clips, part_rows, CH), BF16)])
    half = exchange_clip(parts).reshape(half_rows, CH)
    other = swap_cores(half)
    grads = call(
        results_body,
        [(S, core), (V, half), (V, other)],
        [
            (V, (9 * CH, CH), BF16),
            (V, (3 * CH, CH), BF16),
            (V, (9 * CH, WIDE), BF16),
            (V, (3 * WIDE, WIDE), BF16),
            (V, (3 * WIDE, WIDE), BF16),
        ],
        [((EARLY, CH), BF16), ((LATE, CH), BF16)],
    )
    shapes = ((3, 3, CH, CH), (3, CH, CH), (3, 3, CH, WIDE), (3, WIDE, WIDE), (3, WIDE, WIDE))
    grads = [grad.reshape(shape) for grad, shape in zip(grads, shapes)]
    return (output.reshape(1, HALF, 1, 4, WIDE), *grads)


def solution(mesh):
    placed = (
        P("clip", "seq", None, None, None),
        P(),
        P(),
        P(),
        P(),
        P(),
        P("clip", None, "seq", None, None),
    )
    return jax.shard_map(
        local,
        mesh=mesh,
        in_specs=placed,
        out_specs=(P("clip", None, "seq", None, None), P(), P(), P(), P(), P()),
        check_vma=False,
    )
```

```python
import jax
import jax.numpy as jnp
from jax import lax
from jax.experimental import pallas as pl
from jax.experimental.pallas import tpu as pltpu
from jax.sharding import PartitionSpec as P


F32 = jnp.float32
BF16 = jnp.bfloat16
COLS = 8
HALF = 32
CELLS = COLS * HALF
DOWN = CELLS // 2
CH = 128
WIDE = 256
STRIDED_AT = 9 * 2 * DOWN
KEPT = STRIDED_AT + 2 * DOWN
LOWERED_AT = 8 * WIDE
PART_AT = LOWERED_AT + 2 * DOWN
EARLY = (3 + 18 + 12 + 8) * CH
LATE = (9 + 4) * CH
NEAR = 4


def dot(left, right):
    return lax.dot_general(left, right, (((1,), (0,)), ((), ())), preferred_element_type=F32)


def dot_nt(left, right):
    return lax.dot_general(left, right, (((1,), (1,)), ((), ())), preferred_element_type=F32)


def dot_tn(left, right):
    return lax.dot_general(left, right, (((0,), (0,)), ((), ())), preferred_element_type=F32)


V, P_, H, S = "vmem", "pinned", "hbm", "smem"
SPACES = {V: pltpu.VMEM, P_: pltpu.VMEM, H: pltpu.HBM, S: pltpu.SMEM}


def placed_input(space, array):
    if space in (P_, H):
        return pltpu.with_memory_space_constraint(array, SPACES[space])
    return array


def placed_output(space, shape, kind):
    if space in (P_, H):
        return SPACES[space](shape, kind)
    return jax.ShapeDtypeStruct(shape, kind)


def call(body, ins, outs, scratch=(), copies=0):
    scratch = [pltpu.VMEM(shape, kind) for shape, kind in scratch]
    if copies:
        scratch.append(pltpu.SemaphoreType.DMA((copies,)))
    return pl.pallas_call(
        body,
        out_shape=[placed_output(*out) for out in outs],
        in_specs=[pl.BlockSpec(memory_space=SPACES[space]) for space, _ in ins],
        out_specs=[pl.BlockSpec(memory_space=SPACES[space]) for space, _, _ in outs],
        scratch_shapes=scratch,
        compiler_params=pltpu.CompilerParams(vmem_limit_bytes=24 * 1024 * 1024),
        cost_estimate=pl.CostEstimate(flops=1000, bytes_accessed=8000000, transcendentals=0),
    )(*[placed_input(*given) for given in ins])


def start(sems, *pairs):
    copies = [
        pltpu.make_async_copy(source, target, sems.at[at]) for at, source, target in pairs
    ]
    for copy in copies:
        copy.start()
    return copies


def row_before(planes):
    wide = planes.astype(F32)
    rolled = pltpu.roll(wide, 1, 1)
    at = lax.broadcasted_iota(jnp.int32, wide.shape, 1)
    return jnp.where(at == 0, 0.0, rolled).astype(BF16)


def row_after(planes):
    wide = planes.astype(F32)
    rolled = pltpu.roll(wide, HALF - 1, 1)
    at = lax.broadcasted_iota(jnp.int32, wide.shape, 1)
    return jnp.where(at == HALF - 1, 0.0, rolled).astype(BF16)


def fill_windows(windows, at, even, odd):
    by_row = (row_before(odd), even, odd, row_after(even))
    edge = jnp.zeros((HALF, CH), BF16)
    for row, planes in enumerate(by_row):
        flat = planes.reshape(CELLS, CH)
        for tap in range(3):
            lanes = pl.ds((tap * 4 + row) * CH, CH)
            if tap == 0:
                windows[pl.ds(at, HALF), lanes] = edge
                windows[pl.ds(at + HALF, CELLS - HALF), lanes] = flat[: CELLS - HALF]
            elif tap == 1:
                windows[pl.ds(at, CELLS), lanes] = flat
            else:
                windows[pl.ds(at, CELLS - HALF), lanes] = flat[HALF:]
                windows[pl.ds(at + CELLS - HALF, HALF), lanes] = edge


def silu_slope(preact):
    sigma = jax.nn.sigmoid(preact)
    return sigma * (1.0 + preact * (1.0 - sigma))


def parity_planes(source, frame, spread):
    spread[...] = source[pl.ds(frame * 2 * CELLS, 2 * CELLS), :].astype(F32)
    planes = []
    for par in range(2):
        cols = [spread[pl.ds(par * COLS + col, HALF, stride=2 * COLS), :] for col in range(COLS)]
        planes.append(jnp.stack(cols, axis=0).astype(BF16))
    return planes


def cells_of(kept):
    return jnp.concatenate([kept[pl.ds(tap * 2 * DOWN, 2 * DOWN), :] for tap in range(9)], axis=1)


def prior_body(prior, own_acts, both, acts_out, spread, windows):
    for frame in range(2):
        fill_windows(windows, frame * CELLS, *parity_planes(prior, frame, spread))
    acts_out[pl.ds(2, 4)] = own_acts[...]
    for frame in range(2):
        pre = dot(windows[pl.ds(frame * CELLS, CELLS), :], both[...])
        hid = (pre * jax.nn.sigmoid(pre)).astype(BF16)
        for par in range(2):
            acts_out[frame, par] = hid[:, par * CH : (par + 1) * CH]


def first_body(
    acts, time_far, plane_far, down_far,
    kept_out, strided_out, part_out, times_out,
    first_time, down_plane, down_time, sems,
):
    loads = start(
        sems, (0, time_far, first_time), (1, plane_far, down_plane), (2, down_far, down_time)
    )
    loads[0].wait()
    times = first_time[...].reshape(3 * CH, CH)
    for frame in range(2):
        mixed = []
        for par in range(2):
            taps = jnp.concatenate([acts[frame + k, par] for k in range(3)], axis=1)
            here = acts[4 + frame, par].astype(F32) + dot(taps, times)
            mixed.append(here.astype(BF16).reshape(COLS, HALF, CH))
        by_row = (row_before(mixed[1]), mixed[0], mixed[1])
        for row in range(3):
            for tap in range(3):
                at = (row * 3 + tap) * 2 * DOWN + frame * DOWN
                for col in range(COLS // 2):
                    rows = pl.ds(at + col * HALF, HALF)
                    where = 2 * col + tap - 1
                    if where < 0:
                        kept_out[rows, :] = jnp.zeros((HALF, CH), BF16)
                    else:
                        kept_out[rows, :] = by_row[row][where]
    loads[1].wait()
    kernel = down_plane[...].reshape(9 * CH, WIDE)
    strided = dot(cells_of(kept_out), kernel).astype(BF16).reshape(2, DOWN, WIDE)
    strided_out[...] = strided
    for half in range(2):
        kept_out[pl.ds(STRIDED_AT + half * DOWN, DOWN), :] = strided[
            0, :, half * CH : (half + 1) * CH
        ]
    loads[2].wait()
    part_out[...] = dot(strided[0], down_time[2])
    times_out[...] = down_time[pl.ds(0, 2)]


def own_body(
    rows, last_far, own_far, plane_far,
    sent_out, acts_out, pre_out, both_out,
    last_time, own, first_plane, spread, padded, turned, cells, windows, sems,
):
    loads = start(
        sems, (0, last_far, last_time), (1, own_far, own), (2, plane_far, first_plane)
    )
    both_out[...] = jnp.zeros_like(both_out)
    cotan = rows[...].astype(F32)
    spread[...] = cotan.reshape(HALF * 8, CH)
    for half in range(2):
        padded[pl.ds(0, DOWN), pl.ds(half * CH, CH)] = spread[pl.ds(half, DOWN, stride=2), :]
    padded[pl.ds(DOWN, 8), :] = jnp.zeros((8, WIDE), F32)
    loads[0].wait()
    total = padded[pl.ds(0, DOWN), :]
    for k in range(3):
        taps = padded[pl.ds(4 * (2 - k), DOWN), :].astype(BF16)
        total = total + dot_nt(taps, last_time[k])
    for half in range(2):
        turned[pl.ds(half, DOWN, stride=2), :] = total[:, half * CH : (half + 1) * CH]
    both = jnp.concatenate([turned[...].reshape(HALF, 8, CH), cotan], axis=1)
    sent_out[...] = both.astype(BF16)

    loads[1].wait()
    for frame in range(2):
        planes = parity_planes(own, frame, cells)
        fill_windows(windows, frame * CELLS, *planes)
        for par in range(2):
            acts_out[2 + frame, par] = planes[par].reshape(CELLS, CH)
    loads[2].wait()
    for tap in range(3):
        for row in range(4):
            at = pl.ds((tap * 4 + row) * CH, CH)
            if row < 3:
                both_out[at, pl.ds(0, CH)] = first_plane[row, tap]
            if row > 0:
                both_out[at, pl.ds(CH, CH)] = first_plane[row - 1, tap]
    for frame in range(2):
        pre = dot(windows[pl.ds(frame * CELLS, CELLS), :], both_out[...])
        hid = (pre * jax.nn.sigmoid(pre)).astype(BF16)
        for par in range(2):
            acts_out[frame, par] = hid[:, par * CH : (par + 1) * CH]
            pre_out[frame, par] = pre[:, par * CH : (par + 1) * CH]


def cotan_body(
    received,
    grad_lowered_out, cot_out,
    spread,
):
    spread[...] = received[...].astype(F32).reshape(HALF * 16, CH)
    for at, out in ((0, grad_lowered_out), (8, cot_out)):
        parts = []
        for col in range(4):
            halves = [
                spread[pl.ds(at + col * 2 + half, HALF, stride=16), :] for half in range(2)
            ]
            parts.append(jnp.concatenate(halves, axis=1))
        out[...] = jnp.concatenate(parts, axis=0).astype(BF16)


def middle_body(prior, part, times, grad_lowered, cot, lowered_out, sent_out):
    pre = dot(prior[0], times[0]) + dot(prior[1], times[1]) + part[...]
    lowered_out[...] = (pre * jax.nn.sigmoid(pre)).astype(BF16)
    sent_out[pl.ds(0, DOWN), :] = (grad_lowered[...].astype(F32) * silu_slope(pre)).astype(BF16)
    sent_out[pl.ds(DOWN, DOWN), :] = cot[...]


BACK = (
    (0, 0, 0, 0, 1, 1),
    (0, 1, 0, 1, 1, 0),
    (0, 1, 0, 0, 1, 2),
    (1, 0, 1, 0, 0, 1),
    (1, 0, 0, 0, 2, 1),
    (1, 1, 1, 1, 0, 0),
    (1, 1, 1, 0, 0, 2),
    (1, 1, 0, 1, 2, 0),
    (1, 1, 0, 0, 2, 2),
)


def time_grads_body(
    sent, lowered, prior, kept, down_far, plane_far,
    times_out, kernels_out, grads_out,
    down_time, down_plane, sems,
):
    loads = start(sems, (0, down_far, down_time), (1, plane_far, down_plane))
    kernels_out[...] = jnp.zeros_like(kernels_out)
    wide = lowered[...].astype(F32)
    for col in range(4):
        for half in range(2):
            grads_out[pl.ds(LOWERED_AT + col * 2 + half, HALF, stride=8), :] = wide[
                col * HALF : (col + 1) * HALF, half * CH : (half + 1) * CH
            ]
    own = [kept[pl.ds(STRIDED_AT + half * DOWN, DOWN), :] for half in range(2)]
    taps = (prior[0], prior[1], jnp.concatenate(own, axis=1))
    grad_pre = sent[pl.ds(0, DOWN), :]
    for k in range(3):
        down = dot_tn(taps[k], grad_pre)
        for half in range(2):
            lanes = slice(half * CH, (half + 1) * CH)
            grads_out[pl.ds((half * 3 + k) * WIDE, WIDE), :] = down[:, lanes]
    last = dot_tn(lowered[...], sent[pl.ds(DOWN, DOWN), :])
    for half in range(2):
        grads_out[pl.ds((6 + half) * WIDE, WIDE), :] = last[:, half * CH : (half + 1) * CH]
    for load in loads:
        load.wait()
    part = dot_nt(grad_pre, down_time[2])
    for half in range(2):
        grads_out[pl.ds(PART_AT + half * DOWN, DOWN), :] = part[:, half * CH : (half + 1) * CH]
    times_out[...] = down_time[pl.ds(0, 2)]
    for row_par, col_par, row_off, col_off, row, tap in BACK:
        rows = pl.ds((row_par * 2 + col_par) * CH, CH)
        lanes = pl.ds((row_off * 2 + col_off) * WIDE, WIDE)
        kernels_out[rows, lanes] = down_plane[row, tap]


def grad_strided_of(grads, ahead, times):
    following = ahead[pl.ds(0, DOWN), :]
    part = [grads[pl.ds(PART_AT + half * DOWN, DOWN), :] for half in range(2)]
    even = jnp.concatenate(part, axis=1) + dot_nt(following, times[0])
    return even.astype(BF16), dot_nt(following, times[1]).astype(BF16)


def back_body(ahead, grads, times, kernels, sent_out, shifted):
    for half in range(2):
        sent_out[pl.ds(4 * CELLS + half * DOWN, DOWN), :] = ahead[
            pl.ds(DOWN, DOWN), pl.ds(half * CH, CH)
        ]
    for frame, strided in enumerate(grad_strided_of(grads, ahead, times)):
        planes = strided.reshape(4, HALF, WIDE)
        for row_off, rows in ((0, planes), (1, row_after(planes))):
            flat = rows.reshape(DOWN, WIDE)
            here = pl.ds((row_off * 2) * WIDE, WIDE)
            after = pl.ds((row_off * 2 + 1) * WIDE, WIDE)
            shifted[pl.ds(frame * DOWN, DOWN), here] = flat
            shifted[pl.ds(frame * DOWN, DOWN - HALF), after] = flat[HALF:]
            shifted[pl.ds(frame * DOWN + DOWN - HALF, HALF), after] = jnp.zeros((HALF, WIDE), BF16)
    mixed = dot_nt(shifted[...], kernels[...]).astype(BF16)
    for frame in range(2):
        for par in range(2):
            for col_par in range(2):
                lanes = slice((par * 2 + col_par) * CH, (par * 2 + col_par + 1) * CH)
                for col in range(4):
                    rows = slice(frame * DOWN + col * HALF, frame * DOWN + (col + 1) * HALF)
                    plane = (frame * 2 + par) * COLS + 2 * col + col_par
                    sent_out[pl.ds(plane * HALF, HALF), :] = mixed[rows, lanes]


def plane_grads_body(
    core, grad_mixed, kept, acts, pre, time_far, down_far,
    grads, lowered, ahead,
    mine_out, other_out, windows_out, slope_out, part_out, time_out,
    flat, rows_here, times, sems,
):
    loads = start(sems, (0, time_far, time_out), (1, down_far, times))
    base = 3 * CH + 18 * CH
    flat[pl.ds(base, 8 * WIDE), :] = grads[pl.ds(0, 8 * WIDE), :]
    base += 8 * WIDE
    last = dot_tn(lowered[...], ahead[pl.ds(DOWN, DOWN), :])
    for half in range(2):
        flat[pl.ds(base + half * WIDE, WIDE), :] = last[:, half * CH : (half + 1) * CH]
    loads[1].wait()
    grad_strided = jnp.concatenate(grad_strided_of(grads, ahead, times), axis=0)
    down = dot_tn(cells_of(kept), grad_strided)
    for half in range(2):
        at = 3 * CH + half * 9 * CH
        flat[pl.ds(at, 9 * CH), :] = down[:, half * CH : (half + 1) * CH]
    cotan = grad_mixed[pl.ds(0, 4 * CELLS), :]
    for k in range(3):
        taps = acts[pl.ds(k, 2)].reshape(4 * CELLS, CH)
        flat[pl.ds(k * CH, CH), :] = dot_tn(taps, cotan)
    here = core[0]
    half = EARLY // 2
    mine_out[pl.ds(0, half), :] = flat[pl.ds(pl.multiple_of(here * half, 16), half), :]
    other_out[pl.ds(0, half), :] = flat[
        pl.ds(pl.multiple_of((1 - here) * half, 16), half), :
    ].astype(BF16)
    rows_here[...] = grads[pl.ds(LOWERED_AT, 2 * DOWN), :].reshape(HALF // 2, 2, 8, CH)
    mine_out[pl.ds(half, DOWN), :] = rows_here[:, pl.ds(here, 1)].reshape(DOWN, CH)
    away = rows_here[:, pl.ds(1 - here, 1)].reshape(DOWN, CH)
    other_out[pl.ds(half, DOWN), :] = away.astype(BF16)
    loads[0].wait()
    for frame in range(2):
        planes = [acts[4 + frame, par].reshape(COLS, HALF, CH) for par in range(2)]
        fill_windows(windows_out, frame * CELLS, *planes)
    slope_out[...] = silu_slope(pre[...])
    for par in range(2):
        first, second = [
            grad_mixed[pl.ds((frame * 2 + par) * CELLS, CELLS), :] for frame in range(2)
        ]
        part_out[0, par] = dot_nt(first, time_out[2]) + dot_nt(second, time_out[1])
        part_out[1, par] = dot_nt(second, time_out[2])


def last_body(
    core, ahead, windows, slope, part, first_time, lowered, early_other,
    mine_out, other_out,
    flat,
):
    cotans = [[], []]
    for par in range(2):
        first, second = [
            ahead[pl.ds((frame * 2 + par) * CELLS, CELLS), :] for frame in range(2)
        ]
        hidden = (
            part[0, par] + dot_nt(first, first_time[0]),
            part[1, par] + dot_nt(first, first_time[1]) + dot_nt(second, first_time[0]),
        )
        for frame in range(2):
            cotans[frame].append((hidden[frame] * slope[frame, par]).astype(BF16))
    cotan = jnp.concatenate([jnp.concatenate(parts, axis=1) for parts in cotans], axis=0)
    product = dot_tn(windows[...], cotan)
    for row in range(3):
        for tap in range(3):
            at = (tap * 4 + row) * CH
            flat[pl.ds((row * 3 + tap) * CH, CH), :] = (
                product[at : at + CH, :CH] + product[at + CH : at + 2 * CH, CH:]
            )
    further = [ahead[pl.ds(4 * CELLS + half * DOWN, DOWN), :] for half in range(2)]
    for half in range(2):
        flat[pl.ds(9 * CH + half * WIDE, WIDE), :] = dot_tn(lowered[...], further[half])
    here = core[0]
    half = mine_out.shape[0]
    mine_out[...] = flat[pl.ds(pl.multiple_of(here * half, 16), half), :]
    rows = early_other.shape[0]
    other_out[pl.ds(0, rows), :] = early_other[...]
    other_out[pl.ds(rows, half), :] = flat[
        pl.ds(pl.multiple_of((1 - here) * half, 16), half), :
    ].astype(BF16)


def halves_body(core, early, late, other, half_out, frames_out):
    rows, more = EARLY // 2, LATE // 2
    half_out[pl.ds(0, rows), :] = (
        early[pl.ds(0, rows), :] + other[pl.ds(0, rows), :].astype(F32)
    ).astype(BF16)
    here = core[0]
    chips = HALF // 2
    mine = early[pl.ds(rows, DOWN), :].reshape(chips, 8, CH)
    theirs = other[pl.ds(rows, DOWN), :].astype(F32).reshape(chips, 8, CH)
    frames = [jnp.where(here == 0, mine, theirs), jnp.where(here == 0, theirs, mine)]
    frames_out[...] = jnp.concatenate(frames, axis=1).astype(BF16)
    half_out[pl.ds(rows, more), :] = (
        late[...] + other[pl.ds(rows + DOWN, more), :].astype(F32)
    ).astype(BF16)


def sum_body(blocks, frames, sent_out, padded):
    rows = blocks.shape[1]
    total = blocks[0].astype(F32)
    for block in range(1, blocks.shape[0]):
        total = total + blocks[block].astype(F32)
    padded[...] = jnp.zeros_like(padded)
    padded[pl.ds(0, rows), :] = total
    chips = frames.shape[0]
    near = sent_out.shape[0]
    share = padded.shape[0] // near
    for chip in range(near):
        sent_out[chip, pl.ds(0, share), :] = padded[pl.ds(chip * share, share), :].astype(BF16)
        for far in range(chips // near):
            sent_out[chip, pl.ds(share + far * 16, 16), :] = frames[far * near + chip]


def first_rows(received, share):
    total = received[0, pl.ds(0, share), :].astype(F32)
    for chip in range(1, received.shape[0]):
        total = total + received[chip, pl.ds(0, share), :].astype(F32)
    return total.astype(BF16)


def near_body(received, sent_out):
    near, far = received.shape[0], sent_out.shape[0]
    share = sent_out.shape[1] - near * 16
    piece = first_rows(received, share)
    for there in range(far):
        sent_out[there, pl.ds(0, share), :] = piece
        for chip in range(near):
            sent_out[there, pl.ds(share + chip * 16, 16), :] = received[
                chip, pl.ds(share + there * 16, 16), :
            ]


def piece_body(received, piece_out):
    piece = first_rows(received, piece_out.shape[1])
    for chip in range(piece_out.shape[0]):
        piece_out[chip] = piece


def spread_body(pieces, part_out):
    flat = pieces[...].reshape(-1, CH).astype(F32)
    part = flat[: part_out.shape[1]].astype(BF16)
    for block in range(part_out.shape[0]):
        part_out[block] = part


def results_body(
    core, mine, other,
    first_plane_out, first_time_out, down_plane_out, down_time_out, last_time_out,
    early, late,
):
    here = core[0]
    rows, more = EARLY // 2, LATE // 2
    for half, at in ((mine, here), (other, 1 - here)):
        early[pl.ds(pl.multiple_of(at * rows, 16), rows), :] = half[pl.ds(0, rows), :]
        late[pl.ds(pl.multiple_of(at * more, 16), more), :] = half[pl.ds(rows, more), :]
    first_plane_out[...] = late[pl.ds(0, 9 * CH), :]
    first_time_out[...] = early[pl.ds(0, 3 * CH), :]
    for half in range(2):
        lanes = pl.ds(half * CH, CH)
        down_plane_out[:, lanes] = early[pl.ds(3 * CH + half * 9 * CH, 9 * CH), :]
        down_time_out[:, lanes] = early[pl.ds(21 * CH + half * 6 * CH, 6 * CH), :]
        last_time_out[pl.ds(0, WIDE), lanes] = late[pl.ds(9 * CH + half * WIDE, WIDE), :]
        last_time_out[pl.ds(WIDE, WIDE), lanes] = early[pl.ds(37 * CH + half * WIDE, WIDE), :]
        last_time_out[pl.ds(2 * WIDE, WIDE), lanes] = early[pl.ds(33 * CH + half * WIDE, WIDE), :]


def output_body(received, last_time, output, spread, padded):
    share = received.shape[1] - 16 * HALF // 2 // received.shape[0]
    for far in range(received.shape[0]):
        rows = received.shape[1] - share
        spread[pl.ds(far * rows, rows), :] = received[far, pl.ds(share, rows), :].astype(F32)
    padded[pl.ds(0, 8), :] = jnp.zeros((8, WIDE), F32)
    for half in range(2):
        padded[pl.ds(8, DOWN), pl.ds(half * CH, CH)] = spread[pl.ds(half, DOWN, stride=2), :]
    total = padded[pl.ds(8, DOWN), :]
    for k in range(3):
        taps = padded[pl.ds(4 * k, DOWN), :].astype(BF16)
        total = total + dot(taps, last_time[k])
    output[...] = total.astype(BF16)


def from_behind(block, distance):
    devices = range(lax.axis_size("seq"))
    route = [(i - distance, i) for i in devices if i - distance in devices]
    return lax.ppermute(block, "seq", route)


def swap_cores(block):
    count = lax.axis_size("seq")
    return lax.ppermute(block, "seq", [(i, i ^ 1) for i in range(count)])


def exchange_clip(blocks):
    return lax.all_to_all(blocks, "clip", split_axis=0, concat_axis=0, tiled=True)


def exchange_seq(blocks):
    return lax.all_to_all(blocks, "seq", split_axis=0, concat_axis=0, tiled=True)


def exchange_chips(blocks, near):
    count = lax.axis_size("seq") // 2
    runs = [list(range(first, first + NEAR)) for first in range(0, count, NEAR)]
    if not near:
        runs = [list(place) for place in zip(*runs)]
    groups = [[2 * chip + core for chip in run] for run in runs for core in range(2)]
    return lax.all_to_all(
        blocks, "seq", split_axis=0, concat_axis=0, axis_index_groups=groups, tiled=True
    )


def local(clip_in, first_plane, first_time, down_plane, down_time, last_time, cotan_out):
    own = clip_in.reshape(4 * CELLS, CH)
    prior = from_behind(own, 1)
    flat_frames = (2, 2, CELLS, CH)
    sent, acts, pre_first, both = call(
        own_body,
        [(V, cotan_out[0].reshape(HALF, 8, CH)), (H, last_time), (H, own), (H, first_plane)],
        [
            (V, (HALF, 16, CH), BF16),
            (P_, (4, 2, CELLS, CH), BF16),
            (P_, flat_frames, F32),
            (P_, (12 * CH, WIDE), BF16),
        ],
        [
            ((3, WIDE, WIDE), BF16),
            ((4 * CELLS, CH), BF16),
            ((3, 3, CH, CH), BF16),
            ((HALF * 8, CH), F32),
            ((DOWN + 8, WIDE), F32),
            ((HALF * 8, CH), F32),
            ((2 * CELLS, CH), F32),
            ((2 * CELLS, 12 * CH), BF16),
        ],
        copies=3,
    )
    (acts,) = call(
        prior_body,
        [(V, prior), (P_, acts), (P_, both)],
        [(P_, (6, 2, CELLS, CH), BF16)],
        [((2 * CELLS, CH), F32), ((2 * CELLS, 12 * CH), BF16)],
    )
    sent, acts = lax.optimization_barrier((sent, acts))
    received = exchange_seq(sent)
    times = (P_, (2, WIDE, WIDE), BF16)
    kept, strided, part, near_times = call(
        first_body,
        [
            (P_, acts), (H, first_time), (H, down_plane), (H, down_time),
        ],
        [
            (P_, (KEPT, CH), BF16),
            (P_, (2, DOWN, WIDE), BF16),
            (P_, (DOWN, WIDE), F32),
            times,
        ],
        [
            ((3, CH, CH), BF16),
            ((3, 3, CH, WIDE), BF16),
            ((3, WIDE, WIDE), BF16),
        ],
        copies=3,
    )
    strided_prior = from_behind(strided, 1)
    down = (P_, (DOWN, WIDE), BF16)
    grad_lowered, cot = call(
        cotan_body, [(V, received)], [down, down], [((HALF * 16, CH), F32)]
    )
    lowered, sent = call(
        middle_body,
        [(V, strided_prior), (P_, part), (P_, near_times), (P_, grad_lowered), (P_, cot)],
        [down, (P_, (2 * DOWN, WIDE), BF16)],
    )
    ahead = from_behind(sent, -1)
    near_times, kernels, time_grads = call(
        time_grads_body,
        [
            (P_, sent), (P_, lowered), (V, strided_prior), (P_, kept),
            (H, down_time), (H, down_plane),
        ],
        [
            times,
            (P_, (4 * CH, 4 * WIDE), BF16),
            (P_, (PART_AT + 2 * DOWN, CH), F32),
        ],
        [((3, WIDE, WIDE), BF16), ((3, 3, CH, WIDE), BF16)],
        copies=2,
    )
    (sent,) = call(
        back_body,
        [(V, ahead), (P_, time_grads), (P_, near_times), (P_, kernels)],
        [(P_, (4 * CELLS + 2 * DOWN, CH), BF16)],
        [((2 * DOWN, 4 * WIDE), BF16)],
    )
    further = from_behind(sent, -1)
    core = (lax.axis_index("seq") % 2).astype(jnp.int32).reshape(1)
    early, early_other, windows, slope, part, near_time = call(
        plane_grads_body,
        [
            (S, core), (P_, sent), (P_, kept), (P_, acts), (P_, pre_first),
            (H, first_time), (H, down_time), (P_, time_grads), (P_, lowered), (V, ahead),
        ],
        [
            (P_, (EARLY // 2 + DOWN, CH), F32),
            (P_, (EARLY // 2 + DOWN, CH), BF16),
            (P_, (2 * CELLS, 12 * CH), BF16),
            (P_, flat_frames, F32),
            (P_, flat_frames, F32),
            (P_, (3, CH, CH), BF16),
        ],
        [((EARLY, CH), F32), ((HALF // 2, 2, 8, CH), F32), ((3, WIDE, WIDE), BF16)],
        copies=2,
    )
    late, other = call(
        last_body,
        [
            (S, core), (V, further), (P_, windows), (P_, slope), (P_, part), (P_, near_time),
            (P_, lowered), (P_, early_other),
        ],
        [(P_, (LATE // 2, CH), F32), (P_, ((EARLY + LATE) // 2 + DOWN, CH), BF16)],
        [((LATE, CH), F32)],
    )

    clips = lax.axis_size("clip")
    chips = lax.axis_size("seq") // 2
    half_rows = (EARLY + LATE) // 2
    part_rows = half_rows // clips
    other = swap_cores(other)
    half, frames = call(
        halves_body,
        [(S, core), (P_, early), (P_, late), (V, other)],
        [(P_, (half_rows, CH), BF16), (V, (chips, 16, CH), BF16)],
    )
    blocks = exchange_clip(half.reshape(clips, part_rows, CH))
    far = chips // NEAR
    share = 16 * (-(-part_rows // (16 * NEAR)))
    (sent,) = call(
        sum_body,
        [(V, blocks), (V, frames)],
        [(V, (NEAR, share + far * 16, CH), BF16)],
        [((NEAR * share, CH), F32)],
    )
    received = exchange_chips(sent, True)
    (sent,) = call(near_body, [(V, received)], [(V, (far, share + NEAR * 16, CH), BF16)])
    received = exchange_chips(sent, False)
    (pieces,) = call(piece_body, [(V, received)], [(V, (NEAR, share, CH), BF16)])
    pieces = exchange_chips(pieces, True)
    (output,) = call(
        output_body,
        [(V, received), (V, last_time)],
        [(V, (DOWN, WIDE), BF16)],
        [((HALF * 8, CH), F32), ((DOWN + 8, WIDE), F32)],
    )
    (parts,) = call(spread_body, [(V, pieces)], [(V, (clips, part_rows, CH), BF16)])
    half = exchange_clip(parts).reshape(half_rows, CH)
    other = swap_cores(half)
    grads = call(
        results_body,
        [(S, core), (V, half), (V, other)],
        [
            (V, (9 * CH, CH), BF16),
            (V, (3 * CH, CH), BF16),
            (V, (9 * CH, WIDE), BF16),
            (V, (3 * WIDE, WIDE), BF16),
            (V, (3 * WIDE, WIDE), BF16),
        ],
        [((EARLY, CH), BF16), ((LATE, CH), BF16)],
    )
    shapes = ((3, 3, CH, CH), (3, CH, CH), (3, 3, CH, WIDE), (3, WIDE, WIDE), (3, WIDE, WIDE))
    grads = [grad.reshape(shape) for grad, shape in zip(grads, shapes)]
    return (output.reshape(1, HALF, 1, 4, WIDE), *grads)


def solution(mesh):
    placed = (
        P("clip", "seq", None, None, None),
        P(),
        P(),
        P(),
        P(),
        P(),
        P("clip", None, "seq", None, None),
    )
    return jax.shard_map(
        local,
        mesh=mesh,
        in_specs=placed,
        out_specs=(P("clip", None, "seq", None, None), P(), P(), P(), P(), P()),
        check_vma=False,
    )
```

```python
import jax
import jax.numpy as jnp
from jax import lax
from jax.experimental import pallas as pl
from jax.experimental.pallas import tpu as pltpu
from jax.sharding import PartitionSpec as P


F32 = jnp.float32
BF16 = jnp.bfloat16
COLS = 8
HALF = 32
CELLS = COLS * HALF
DOWN = CELLS // 2
CH = 128
WIDE = 256
STRIDED_AT = 9 * 2 * DOWN
KEPT = STRIDED_AT + 2 * DOWN
LOWERED_AT = 8 * WIDE
PART_AT = LOWERED_AT + 2 * DOWN
EARLY = (3 + 18 + 12 + 8) * CH
LATE = (9 + 4) * CH
NEAR = 4


def dot(left, right):
    return lax.dot_general(left, right, (((1,), (0,)), ((), ())), preferred_element_type=F32)


def dot_nt(left, right):
    return lax.dot_general(left, right, (((1,), (1,)), ((), ())), preferred_element_type=F32)


def dot_tn(left, right):
    return lax.dot_general(left, right, (((0,), (0,)), ((), ())), preferred_element_type=F32)


V, P_, H, S = "vmem", "pinned", "hbm", "smem"
SPACES = {V: pltpu.VMEM, P_: pltpu.VMEM, H: pltpu.HBM, S: pltpu.SMEM}


def placed_input(space, array):
    if space in (P_, H):
        return pltpu.with_memory_space_constraint(array, SPACES[space])
    return array


def placed_output(space, shape, kind):
    if space in (P_, H):
        return SPACES[space](shape, kind)
    return jax.ShapeDtypeStruct(shape, kind)


def call(body, ins, outs, scratch=(), copies=0, cost=8000000):
    scratch = [pltpu.VMEM(shape, kind) for shape, kind in scratch]
    if copies:
        scratch.append(pltpu.SemaphoreType.DMA((copies,)))
    return pl.pallas_call(
        body,
        out_shape=[placed_output(*out) for out in outs],
        in_specs=[pl.BlockSpec(memory_space=SPACES[space]) for space, _ in ins],
        out_specs=[pl.BlockSpec(memory_space=SPACES[space]) for space, _, _ in outs],
        scratch_shapes=scratch,
        compiler_params=pltpu.CompilerParams(vmem_limit_bytes=24 * 1024 * 1024),
        cost_estimate=pl.CostEstimate(flops=1000, bytes_accessed=cost, transcendentals=0),
    )(*[placed_input(*given) for given in ins])


def start(sems, *pairs):
    copies = [
        pltpu.make_async_copy(source, target, sems.at[at]) for at, source, target in pairs
    ]
    for copy in copies:
        copy.start()
    return copies


def row_before(planes):
    wide = planes.astype(F32)
    rolled = pltpu.roll(wide, 1, 1)
    at = lax.broadcasted_iota(jnp.int32, wide.shape, 1)
    return jnp.where(at == 0, 0.0, rolled).astype(BF16)


def row_after(planes):
    wide = planes.astype(F32)
    rolled = pltpu.roll(wide, HALF - 1, 1)
    at = lax.broadcasted_iota(jnp.int32, wide.shape, 1)
    return jnp.where(at == HALF - 1, 0.0, rolled).astype(BF16)


def fill_windows(windows, at, even, odd):
    by_row = (row_before(odd), even, odd, row_after(even))
    edge = jnp.zeros((HALF, CH), BF16)
    for row, planes in enumerate(by_row):
        flat = planes.reshape(CELLS, CH)
        for tap in range(3):
            lanes = pl.ds((tap * 4 + row) * CH, CH)
            if tap == 0:
                windows[pl.ds(at, HALF), lanes] = edge
                windows[pl.ds(at + HALF, CELLS - HALF), lanes] = flat[: CELLS - HALF]
            elif tap == 1:
                windows[pl.ds(at, CELLS), lanes] = flat
            else:
                windows[pl.ds(at, CELLS - HALF), lanes] = flat[HALF:]
                windows[pl.ds(at + CELLS - HALF, HALF), lanes] = edge


def silu_slope(preact):
    sigma = jax.nn.sigmoid(preact)
    return sigma * (1.0 + preact * (1.0 - sigma))


def parity_planes(source, frame, spread):
    spread[...] = source[pl.ds(frame * 2 * CELLS, 2 * CELLS), :].astype(F32)
    planes = []
    for par in range(2):
        cols = [spread[pl.ds(par * COLS + col, HALF, stride=2 * COLS), :] for col in range(COLS)]
        planes.append(jnp.stack(cols, axis=0).astype(BF16))
    return planes


def cells_of(kept):
    return jnp.concatenate([kept[pl.ds(tap * 2 * DOWN, 2 * DOWN), :] for tap in range(9)], axis=1)


def prior_body(prior, own_acts, both, acts_out, spread, windows):
    for frame in range(2):
        fill_windows(windows, frame * CELLS, *parity_planes(prior, frame, spread))
    acts_out[pl.ds(2, 4)] = own_acts[...]
    for frame in range(2):
        pre = dot(windows[pl.ds(frame * CELLS, CELLS), :], both[...])
        hid = (pre * jax.nn.sigmoid(pre)).astype(BF16)
        for par in range(2):
            acts_out[frame, par] = hid[:, par * CH : (par + 1) * CH]


def first_body(
    acts, time_far, plane_far, down_far,
    kept_out, strided_out, part_out, times_out,
    first_time, down_plane, down_time, sems,
):
    loads = start(
        sems, (0, time_far, first_time), (1, plane_far, down_plane), (2, down_far, down_time)
    )
    loads[0].wait()
    times = first_time[...].reshape(3 * CH, CH)
    for frame in range(2):
        mixed = []
        for par in range(2):
            taps = jnp.concatenate([acts[frame + k, par] for k in range(3)], axis=1)
            here = acts[4 + frame, par].astype(F32) + dot(taps, times)
            mixed.append(here.astype(BF16).reshape(COLS, HALF, CH))
        by_row = (row_before(mixed[1]), mixed[0], mixed[1])
        for row in range(3):
            for tap in range(3):
                at = (row * 3 + tap) * 2 * DOWN + frame * DOWN
                for col in range(COLS // 2):
                    rows = pl.ds(at + col * HALF, HALF)
                    where = 2 * col + tap - 1
                    if where < 0:
                        kept_out[rows, :] = jnp.zeros((HALF, CH), BF16)
                    else:
                        kept_out[rows, :] = by_row[row][where]
    loads[1].wait()
    kernel = down_plane[...].reshape(9 * CH, WIDE)
    strided = dot(cells_of(kept_out), kernel).astype(BF16).reshape(2, DOWN, WIDE)
    strided_out[...] = strided
    for half in range(2):
        kept_out[pl.ds(STRIDED_AT + half * DOWN, DOWN), :] = strided[
            0, :, half * CH : (half + 1) * CH
        ]
    loads[2].wait()
    part_out[...] = dot(strided[0], down_time[2])
    times_out[...] = down_time[pl.ds(0, 2)]


def rows_body(rows, last_far, sent_out, last_time, spread, padded, turned, sems):
    loads = start(sems, (0, last_far, last_time))
    cotan = rows[...].astype(F32)
    spread[...] = cotan.reshape(HALF * 8, CH)
    for half in range(2):
        padded[pl.ds(0, DOWN), pl.ds(half * CH, CH)] = spread[pl.ds(half, DOWN, stride=2), :]
    padded[pl.ds(DOWN, 8), :] = jnp.zeros((8, WIDE), F32)
    loads[0].wait()
    total = padded[pl.ds(0, DOWN), :]
    for k in range(3):
        taps = padded[pl.ds(4 * (2 - k), DOWN), :].astype(BF16)
        total = total + dot_nt(taps, last_time[k])
    for half in range(2):
        turned[pl.ds(half, DOWN, stride=2), :] = total[:, half * CH : (half + 1) * CH]
    both = jnp.concatenate([turned[...].reshape(HALF, 8, CH), cotan], axis=1)
    sent_out[...] = both.astype(BF16)


def own_body(
    own_far, plane_far,
    acts_out, pre_out, both_out,
    own, first_plane, cells, windows, sems,
):
    loads = start(sems, (0, own_far, own), (1, plane_far, first_plane))
    both_out[...] = jnp.zeros_like(both_out)
    loads[0].wait()
    for frame in range(2):
        planes = parity_planes(own, frame, cells)
        fill_windows(windows, frame * CELLS, *planes)
        for par in range(2):
            acts_out[2 + frame, par] = planes[par].reshape(CELLS, CH)
    loads[1].wait()
    for tap in range(3):
        for row in range(4):
            at = pl.ds((tap * 4 + row) * CH, CH)
            if row < 3:
                both_out[at, pl.ds(0, CH)] = first_plane[row, tap]
            if row > 0:
                both_out[at, pl.ds(CH, CH)] = first_plane[row - 1, tap]
    for frame in range(2):
        pre = dot(windows[pl.ds(frame * CELLS, CELLS), :], both_out[...])
        hid = (pre * jax.nn.sigmoid(pre)).astype(BF16)
        for par in range(2):
            acts_out[frame, par] = hid[:, par * CH : (par + 1) * CH]
            pre_out[frame, par] = pre[:, par * CH : (par + 1) * CH]


def cotan_body(
    received,
    grad_lowered_out, cot_out,
    spread,
):
    spread[...] = received[...].astype(F32).reshape(HALF * 16, CH)
    for at, out in ((0, grad_lowered_out), (8, cot_out)):
        parts = []
        for col in range(4):
            halves = [
                spread[pl.ds(at + col * 2 + half, HALF, stride=16), :] for half in range(2)
            ]
            parts.append(jnp.concatenate(halves, axis=1))
        out[...] = jnp.concatenate(parts, axis=0).astype(BF16)


def middle_body(prior, part, times, grad_lowered, cot, lowered_out, sent_out):
    pre = dot(prior[0], times[0]) + dot(prior[1], times[1]) + part[...]
    lowered_out[...] = (pre * jax.nn.sigmoid(pre)).astype(BF16)
    sent_out[pl.ds(0, DOWN), :] = (grad_lowered[...].astype(F32) * silu_slope(pre)).astype(BF16)
    sent_out[pl.ds(DOWN, DOWN), :] = cot[...]


BACK = (
    (0, 0, 0, 0, 1, 1),
    (0, 1, 0, 1, 1, 0),
    (0, 1, 0, 0, 1, 2),
    (1, 0, 1, 0, 0, 1),
    (1, 0, 0, 0, 2, 1),
    (1, 1, 1, 1, 0, 0),
    (1, 1, 1, 0, 0, 2),
    (1, 1, 0, 1, 2, 0),
    (1, 1, 0, 0, 2, 2),
)


def time_grads_body(
    sent, lowered, prior, kept, down_far, plane_far,
    times_out, kernels_out, grads_out,
    down_time, down_plane, sems,
):
    loads = start(sems, (0, down_far, down_time), (1, plane_far, down_plane))
    kernels_out[...] = jnp.zeros_like(kernels_out)
    wide = lowered[...].astype(F32)
    for col in range(4):
        for half in range(2):
            grads_out[pl.ds(LOWERED_AT + col * 2 + half, HALF, stride=8), :] = wide[
                col * HALF : (col + 1) * HALF, half * CH : (half + 1) * CH
            ]
    own = [kept[pl.ds(STRIDED_AT + half * DOWN, DOWN), :] for half in range(2)]
    taps = (prior[0], prior[1], jnp.concatenate(own, axis=1))
    grad_pre = sent[pl.ds(0, DOWN), :]
    for k in range(3):
        down = dot_tn(taps[k], grad_pre)
        for half in range(2):
            lanes = slice(half * CH, (half + 1) * CH)
            grads_out[pl.ds((half * 3 + k) * WIDE, WIDE), :] = down[:, lanes]
    last = dot_tn(lowered[...], sent[pl.ds(DOWN, DOWN), :])
    for half in range(2):
        grads_out[pl.ds((6 + half) * WIDE, WIDE), :] = last[:, half * CH : (half + 1) * CH]
    for load in loads:
        load.wait()
    part = dot_nt(grad_pre, down_time[2])
    for half in range(2):
        grads_out[pl.ds(PART_AT + half * DOWN, DOWN), :] = part[:, half * CH : (half + 1) * CH]
    times_out[...] = down_time[pl.ds(0, 2)]
    for row_par, col_par, row_off, col_off, row, tap in BACK:
        rows = pl.ds((row_par * 2 + col_par) * CH, CH)
        lanes = pl.ds((row_off * 2 + col_off) * WIDE, WIDE)
        kernels_out[rows, lanes] = down_plane[row, tap]


def grad_strided_of(grads, ahead, times):
    following = ahead[pl.ds(0, DOWN), :]
    part = [grads[pl.ds(PART_AT + half * DOWN, DOWN), :] for half in range(2)]
    even = jnp.concatenate(part, axis=1) + dot_nt(following, times[0])
    return even.astype(BF16), dot_nt(following, times[1]).astype(BF16)


def back_body(ahead, grads, times, kernels, sent_out, shifted):
    for half in range(2):
        sent_out[pl.ds(4 * CELLS + half * DOWN, DOWN), :] = ahead[
            pl.ds(DOWN, DOWN), pl.ds(half * CH, CH)
        ]
    for frame, strided in enumerate(grad_strided_of(grads, ahead, times)):
        planes = strided.reshape(4, HALF, WIDE)
        for row_off, rows in ((0, planes), (1, row_after(planes))):
            flat = rows.reshape(DOWN, WIDE)
            here = pl.ds((row_off * 2) * WIDE, WIDE)
            after = pl.ds((row_off * 2 + 1) * WIDE, WIDE)
            shifted[pl.ds(frame * DOWN, DOWN), here] = flat
            shifted[pl.ds(frame * DOWN, DOWN - HALF), after] = flat[HALF:]
            shifted[pl.ds(frame * DOWN + DOWN - HALF, HALF), after] = jnp.zeros((HALF, WIDE), BF16)
    mixed = dot_nt(shifted[...], kernels[...]).astype(BF16)
    for frame in range(2):
        for par in range(2):
            for col_par in range(2):
                lanes = slice((par * 2 + col_par) * CH, (par * 2 + col_par + 1) * CH)
                for col in range(4):
                    rows = slice(frame * DOWN + col * HALF, frame * DOWN + (col + 1) * HALF)
                    plane = (frame * 2 + par) * COLS + 2 * col + col_par
                    sent_out[pl.ds(plane * HALF, HALF), :] = mixed[rows, lanes]


def plane_grads_body(
    core, grad_mixed, kept, acts, pre, time_far, down_far,
    grads, lowered, ahead,
    mine_out, other_out, windows_out, slope_out, part_out, time_out,
    flat, rows_here, times, sems,
):
    loads = start(sems, (0, time_far, time_out), (1, down_far, times))
    base = 3 * CH + 18 * CH
    flat[pl.ds(base, 8 * WIDE), :] = grads[pl.ds(0, 8 * WIDE), :]
    base += 8 * WIDE
    last = dot_tn(lowered[...], ahead[pl.ds(DOWN, DOWN), :])
    for half in range(2):
        flat[pl.ds(base + half * WIDE, WIDE), :] = last[:, half * CH : (half + 1) * CH]
    loads[1].wait()
    grad_strided = jnp.concatenate(grad_strided_of(grads, ahead, times), axis=0)
    down = dot_tn(cells_of(kept), grad_strided)
    for half in range(2):
        at = 3 * CH + half * 9 * CH
        flat[pl.ds(at, 9 * CH), :] = down[:, half * CH : (half + 1) * CH]
    cotan = grad_mixed[pl.ds(0, 4 * CELLS), :]
    for k in range(3):
        taps = acts[pl.ds(k, 2)].reshape(4 * CELLS, CH)
        flat[pl.ds(k * CH, CH), :] = dot_tn(taps, cotan)
    here = core[0]
    half = EARLY // 2
    mine_out[pl.ds(0, half), :] = flat[pl.ds(pl.multiple_of(here * half, 16), half), :]
    other_out[pl.ds(0, half), :] = flat[
        pl.ds(pl.multiple_of((1 - here) * half, 16), half), :
    ].astype(BF16)
    rows_here[...] = grads[pl.ds(LOWERED_AT, 2 * DOWN), :].reshape(HALF // 2, 2, 8, CH)
    mine_out[pl.ds(half, DOWN), :] = rows_here[:, pl.ds(here, 1)].reshape(DOWN, CH)
    away = rows_here[:, pl.ds(1 - here, 1)].reshape(DOWN, CH)
    other_out[pl.ds(half, DOWN), :] = away.astype(BF16)
    loads[0].wait()
    for frame in range(2):
        planes = [acts[4 + frame, par].reshape(COLS, HALF, CH) for par in range(2)]
        fill_windows(windows_out, frame * CELLS, *planes)
    slope_out[...] = silu_slope(pre[...])
    for par in range(2):
        first, second = [
            grad_mixed[pl.ds((frame * 2 + par) * CELLS, CELLS), :] for frame in range(2)
        ]
        part_out[0, par] = dot_nt(first, time_out[2]) + dot_nt(second, time_out[1])
        part_out[1, par] = dot_nt(second, time_out[2])


def last_body(
    core, ahead, windows, slope, part, first_time, lowered, early_other,
    mine_out, other_out,
    flat,
):
    cotans = [[], []]
    for par in range(2):
        first, second = [
            ahead[pl.ds((frame * 2 + par) * CELLS, CELLS), :] for frame in range(2)
        ]
        hidden = (
            part[0, par] + dot_nt(first, first_time[0]),
            part[1, par] + dot_nt(first, first_time[1]) + dot_nt(second, first_time[0]),
        )
        for frame in range(2):
            cotans[frame].append((hidden[frame] * slope[frame, par]).astype(BF16))
    cotan = jnp.concatenate([jnp.concatenate(parts, axis=1) for parts in cotans], axis=0)
    product = dot_tn(windows[...], cotan)
    for row in range(3):
        for tap in range(3):
            at = (tap * 4 + row) * CH
            flat[pl.ds((row * 3 + tap) * CH, CH), :] = (
                product[at : at + CH, :CH] + product[at + CH : at + 2 * CH, CH:]
            )
    further = [ahead[pl.ds(4 * CELLS + half * DOWN, DOWN), :] for half in range(2)]
    for half in range(2):
        flat[pl.ds(9 * CH + half * WIDE, WIDE), :] = dot_tn(lowered[...], further[half])
    here = core[0]
    half = mine_out.shape[0]
    mine_out[...] = flat[pl.ds(pl.multiple_of(here * half, 16), half), :]
    rows = early_other.shape[0]
    other_out[pl.ds(0, rows), :] = early_other[...]
    other_out[pl.ds(rows, half), :] = flat[
        pl.ds(pl.multiple_of((1 - here) * half, 16), half), :
    ].astype(BF16)


def halves_body(core, early, late, other, half_out, frames_out):
    rows, more = EARLY // 2, LATE // 2
    half_out[pl.ds(0, rows), :] = (
        early[pl.ds(0, rows), :] + other[pl.ds(0, rows), :].astype(F32)
    ).astype(BF16)
    here = core[0]
    chips = HALF // 2
    mine = early[pl.ds(rows, DOWN), :].reshape(chips, 8, CH)
    theirs = other[pl.ds(rows, DOWN), :].astype(F32).reshape(chips, 8, CH)
    frames = [jnp.where(here == 0, mine, theirs), jnp.where(here == 0, theirs, mine)]
    frames_out[...] = jnp.concatenate(frames, axis=1).astype(BF16)
    half_out[pl.ds(rows, more), :] = (
        late[...] + other[pl.ds(rows + DOWN, more), :].astype(F32)
    ).astype(BF16)


def sum_body(blocks, frames, sent_out, padded):
    rows = blocks.shape[1]
    total = blocks[0].astype(F32)
    for block in range(1, blocks.shape[0]):
        total = total + blocks[block].astype(F32)
    padded[...] = jnp.zeros_like(padded)
    padded[pl.ds(0, rows), :] = total
    chips = frames.shape[0]
    near = sent_out.shape[0]
    share = padded.shape[0] // near
    for chip in range(near):
        sent_out[chip, pl.ds(0, share), :] = padded[pl.ds(chip * share, share), :].astype(BF16)
        for far in range(chips // near):
            sent_out[chip, pl.ds(share + far * 16, 16), :] = frames[far * near + chip]


def first_rows(received, share):
    total = received[0, pl.ds(0, share), :].astype(F32)
    for chip in range(1, received.shape[0]):
        total = total + received[chip, pl.ds(0, share), :].astype(F32)
    return total.astype(BF16)


def near_body(received, sent_out):
    near, far = received.shape[0], sent_out.shape[0]
    share = sent_out.shape[1] - near * 16
    piece = first_rows(received, share)
    for there in range(far):
        sent_out[there, pl.ds(0, share), :] = piece
        for chip in range(near):
            sent_out[there, pl.ds(share + chip * 16, 16), :] = received[
                chip, pl.ds(share + there * 16, 16), :
            ]


def piece_body(received, piece_out):
    piece = first_rows(received, piece_out.shape[1])
    for chip in range(piece_out.shape[0]):
        piece_out[chip] = piece


def spread_body(pieces, part_out):
    flat = pieces[...].reshape(-1, CH).astype(F32)
    part = flat[: part_out.shape[1]].astype(BF16)
    for block in range(part_out.shape[0]):
        part_out[block] = part


def results_body(
    core, mine, other,
    first_plane_out, first_time_out, down_plane_out, down_time_out, last_time_out,
    early, late,
):
    here = core[0]
    rows, more = EARLY // 2, LATE // 2
    for half, at in ((mine, here), (other, 1 - here)):
        early[pl.ds(pl.multiple_of(at * rows, 16), rows), :] = half[pl.ds(0, rows), :]
        late[pl.ds(pl.multiple_of(at * more, 16), more), :] = half[pl.ds(rows, more), :]
    first_plane_out[...] = late[pl.ds(0, 9 * CH), :]
    first_time_out[...] = early[pl.ds(0, 3 * CH), :]
    for half in range(2):
        lanes = pl.ds(half * CH, CH)
        down_plane_out[:, lanes] = early[pl.ds(3 * CH + half * 9 * CH, 9 * CH), :]
        down_time_out[:, lanes] = early[pl.ds(21 * CH + half * 6 * CH, 6 * CH), :]
        last_time_out[pl.ds(0, WIDE), lanes] = late[pl.ds(9 * CH + half * WIDE, WIDE), :]
        last_time_out[pl.ds(WIDE, WIDE), lanes] = early[pl.ds(37 * CH + half * WIDE, WIDE), :]
        last_time_out[pl.ds(2 * WIDE, WIDE), lanes] = early[pl.ds(33 * CH + half * WIDE, WIDE), :]


def output_body(received, last_time, output, spread, padded):
    share = received.shape[1] - 16 * HALF // 2 // received.shape[0]
    for far in range(received.shape[0]):
        rows = received.shape[1] - share
        spread[pl.ds(far * rows, rows), :] = received[far, pl.ds(share, rows), :].astype(F32)
    padded[pl.ds(0, 8), :] = jnp.zeros((8, WIDE), F32)
    for half in range(2):
        padded[pl.ds(8, DOWN), pl.ds(half * CH, CH)] = spread[pl.ds(half, DOWN, stride=2), :]
    total = padded[pl.ds(8, DOWN), :]
    for k in range(3):
        taps = padded[pl.ds(4 * k, DOWN), :].astype(BF16)
        total = total + dot(taps, last_time[k])
    output[...] = total.astype(BF16)


def from_behind(block, distance):
    devices = range(lax.axis_size("seq"))
    route = [(i - distance, i) for i in devices if i - distance in devices]
    return lax.ppermute(block, "seq", route)


def swap_cores(block):
    count = lax.axis_size("seq")
    return lax.ppermute(block, "seq", [(i, i ^ 1) for i in range(count)])


def exchange_clip(blocks):
    return lax.all_to_all(blocks, "clip", split_axis=0, concat_axis=0, tiled=True)


def exchange_seq(blocks):
    return lax.all_to_all(blocks, "seq", split_axis=0, concat_axis=0, tiled=True)


def exchange_chips(blocks, near):
    count = lax.axis_size("seq") // 2
    runs = [list(range(first, first + NEAR)) for first in range(0, count, NEAR)]
    if not near:
        runs = [list(place) for place in zip(*runs)]
    groups = [[2 * chip + core for chip in run] for run in runs for core in range(2)]
    return lax.all_to_all(
        blocks, "seq", split_axis=0, concat_axis=0, axis_index_groups=groups, tiled=True
    )


def local(clip_in, first_plane, first_time, down_plane, down_time, last_time, cotan_out):
    own = clip_in.reshape(4 * CELLS, CH)
    prior = from_behind(own, 1)
    flat_frames = (2, 2, CELLS, CH)
    (sent,) = call(
        rows_body,
        [(V, cotan_out[0].reshape(HALF, 8, CH)), (H, last_time)],
        [(V, (HALF, 16, CH), BF16)],
        [
            ((3, WIDE, WIDE), BF16),
            ((HALF * 8, CH), F32),
            ((DOWN + 8, WIDE), F32),
            ((HALF * 8, CH), F32),
        ],
        copies=1,
    )
    received = exchange_seq(sent)
    acts, pre_first, both = call(
        own_body,
        [(H, own), (H, first_plane)],
        [
            (P_, (4, 2, CELLS, CH), BF16),
            (P_, flat_frames, F32),
            (P_, (12 * CH, WIDE), BF16),
        ],
        [
            ((4 * CELLS, CH), BF16),
            ((3, 3, CH, CH), BF16),
            ((2 * CELLS, CH), F32),
            ((2 * CELLS, 12 * CH), BF16),
        ],
        copies=2,
    )
    (acts,) = call(
        prior_body,
        [(V, prior), (P_, acts), (P_, both)],
        [(P_, (6, 2, CELLS, CH), BF16)],
        [((2 * CELLS, CH), F32), ((2 * CELLS, 12 * CH), BF16)],
    )
    times = (P_, (2, WIDE, WIDE), BF16)
    kept, strided, part, near_times = call(
        first_body,
        [
            (P_, acts), (H, first_time), (H, down_plane), (H, down_time),
        ],
        [
            (P_, (KEPT, CH), BF16),
            (P_, (2, DOWN, WIDE), BF16),
            (P_, (DOWN, WIDE), F32),
            times,
        ],
        [
            ((3, CH, CH), BF16),
            ((3, 3, CH, WIDE), BF16),
            ((3, WIDE, WIDE), BF16),
        ],
        copies=3,
    )
    strided_prior = from_behind(strided, 1)
    down = (P_, (DOWN, WIDE), BF16)
    grad_lowered, cot = call(
        cotan_body, [(V, received)], [down, down], [((HALF * 16, CH), F32)]
    )
    lowered, sent = call(
        middle_body,
        [(V, strided_prior), (P_, part), (P_, near_times), (P_, grad_lowered), (P_, cot)],
        [down, (P_, (2 * DOWN, WIDE), BF16)],
    )
    ahead = from_behind(sent, -1)
    near_times, kernels, time_grads = call(
        time_grads_body,
        [
            (P_, sent), (P_, lowered), (V, strided_prior), (P_, kept),
            (H, down_time), (H, down_plane),
        ],
        [
            times,
            (P_, (4 * CH, 4 * WIDE), BF16),
            (P_, (PART_AT + 2 * DOWN, CH), F32),
        ],
        [((3, WIDE, WIDE), BF16), ((3, 3, CH, WIDE), BF16)],
        copies=2,
    )
    (sent,) = call(
        back_body,
        [(V, ahead), (P_, time_grads), (P_, near_times), (P_, kernels)],
        [(P_, (4 * CELLS + 2 * DOWN, CH), BF16)],
        [((2 * DOWN, 4 * WIDE), BF16)],
    )
    further = from_behind(sent, -1)
    core = (lax.axis_index("seq") % 2).astype(jnp.int32).reshape(1)
    early, early_other, windows, slope, part, near_time = call(
        plane_grads_body,
        [
            (S, core), (P_, sent), (P_, kept), (P_, acts), (P_, pre_first),
            (H, first_time), (H, down_time), (P_, time_grads), (P_, lowered), (V, ahead),
        ],
        [
            (P_, (EARLY // 2 + DOWN, CH), F32),
            (P_, (EARLY // 2 + DOWN, CH), BF16),
            (P_, (2 * CELLS, 12 * CH), BF16),
            (P_, flat_frames, F32),
            (P_, flat_frames, F32),
            (P_, (3, CH, CH), BF16),
        ],
        [((EARLY, CH), F32), ((HALF // 2, 2, 8, CH), F32), ((3, WIDE, WIDE), BF16)],
        copies=2,
    )
    late, other = call(
        last_body,
        [
            (S, core), (V, further), (P_, windows), (P_, slope), (P_, part), (P_, near_time),
            (P_, lowered), (P_, early_other),
        ],
        [(P_, (LATE // 2, CH), F32), (P_, ((EARLY + LATE) // 2 + DOWN, CH), BF16)],
        [((LATE, CH), F32)],
    )

    clips = lax.axis_size("clip")
    chips = lax.axis_size("seq") // 2
    half_rows = (EARLY + LATE) // 2
    part_rows = half_rows // clips
    other = swap_cores(other)
    half, frames = call(
        halves_body,
        [(S, core), (P_, early), (P_, late), (V, other)],
        [(P_, (half_rows, CH), BF16), (V, (chips, 16, CH), BF16)],
    )
    blocks = exchange_clip(half.reshape(clips, part_rows, CH))
    far = chips // NEAR
    share = 16 * (-(-part_rows // (16 * NEAR)))
    (sent,) = call(
        sum_body,
        [(V, blocks), (V, frames)],
        [(V, (NEAR, share + far * 16, CH), BF16)],
        [((NEAR * share, CH), F32)],
    )
    received = exchange_chips(sent, True)
    (sent,) = call(near_body, [(V, received)], [(V, (far, share + NEAR * 16, CH), BF16)])
    received = exchange_chips(sent, False)
    (pieces,) = call(piece_body, [(V, received)], [(V, (NEAR, share, CH), BF16)])
    pieces = exchange_chips(pieces, True)
    (output,) = call(
        output_body,
        [(V, received), (V, last_time)],
        [(V, (DOWN, WIDE), BF16)],
        [((HALF * 8, CH), F32), ((DOWN + 8, WIDE), F32)],
    )
    (parts,) = call(spread_body, [(V, pieces)], [(V, (clips, part_rows, CH), BF16)])
    half = exchange_clip(parts).reshape(half_rows, CH)
    other = swap_cores(half)
    grads = call(
        results_body,
        [(S, core), (V, half), (V, other)],
        [
            (V, (9 * CH, CH), BF16),
            (V, (3 * CH, CH), BF16),
            (V, (9 * CH, WIDE), BF16),
            (V, (3 * WIDE, WIDE), BF16),
            (V, (3 * WIDE, WIDE), BF16),
        ],
        [((EARLY, CH), BF16), ((LATE, CH), BF16)],
    )
    shapes = ((3, 3, CH, CH), (3, CH, CH), (3, 3, CH, WIDE), (3, WIDE, WIDE), (3, WIDE, WIDE))
    grads = [grad.reshape(shape) for grad, shape in zip(grads, shapes)]
    return (output.reshape(1, HALF, 1, 4, WIDE), *grads)


def solution(mesh):
    placed = (
        P("clip", "seq", None, None, None),
        P(),
        P(),
        P(),
        P(),
        P(),
        P("clip", None, "seq", None, None),
    )
    return jax.shard_map(
        local,
        mesh=mesh,
        in_specs=placed,
        out_specs=(P("clip", None, "seq", None, None), P(), P(), P(), P(), P()),
        check_vma=False,
    )
```

```python
import jax
import jax.numpy as jnp
from jax import lax
from jax.experimental import pallas as pl
from jax.experimental.pallas import tpu as pltpu
from jax.sharding import PartitionSpec as P


F32 = jnp.float32
BF16 = jnp.bfloat16
COLS = 8
HALF = 32
CELLS = COLS * HALF
DOWN = CELLS // 2
CH = 128
WIDE = 256
STRIDED_AT = 9 * 2 * DOWN
KEPT = STRIDED_AT + 2 * DOWN
LOWERED_AT = 8 * WIDE
PART_AT = LOWERED_AT + 2 * DOWN
EARLY = (3 + 18 + 12 + 8) * CH
LATE = (9 + 4) * CH


def dot(left, right):
    return lax.dot_general(left, right, (((1,), (0,)), ((), ())), preferred_element_type=F32)


def dot_nt(left, right):
    return lax.dot_general(left, right, (((1,), (1,)), ((), ())), preferred_element_type=F32)


def dot_tn(left, right):
    return lax.dot_general(left, right, (((0,), (0,)), ((), ())), preferred_element_type=F32)


V, P_, H, S = "vmem", "pinned", "hbm", "smem"
SPACES = {V: pltpu.VMEM, P_: pltpu.VMEM, H: pltpu.HBM, S: pltpu.SMEM}


def placed_input(space, array):
    if space in (P_, H):
        return pltpu.with_memory_space_constraint(array, SPACES[space])
    return array


def placed_output(space, shape, kind):
    if space in (P_, H):
        return SPACES[space](shape, kind)
    return jax.ShapeDtypeStruct(shape, kind)


def call(body, ins, outs, scratch=(), copies=0, flops=1000, size=8000000):
    scratch = [pltpu.VMEM(shape, kind) for shape, kind in scratch]
    if copies:
        scratch.append(pltpu.SemaphoreType.DMA((copies,)))
    return pl.pallas_call(
        body,
        out_shape=[placed_output(*out) for out in outs],
        in_specs=[pl.BlockSpec(memory_space=SPACES[space]) for space, _ in ins],
        out_specs=[pl.BlockSpec(memory_space=SPACES[space]) for space, _, _ in outs],
        scratch_shapes=scratch,
        compiler_params=pltpu.CompilerParams(vmem_limit_bytes=24 * 1024 * 1024),
        cost_estimate=pl.CostEstimate(flops=flops, bytes_accessed=size, transcendentals=0),
    )(*[placed_input(*given) for given in ins])


def start(sems, *pairs):
    copies = [
        pltpu.make_async_copy(source, target, sems.at[at]) for at, source, target in pairs
    ]
    for copy in copies:
        copy.start()
    return copies


def row_before(planes):
    wide = planes.astype(F32)
    rolled = pltpu.roll(wide, 1, 1)
    at = lax.broadcasted_iota(jnp.int32, wide.shape, 1)
    return jnp.where(at == 0, 0.0, rolled).astype(BF16)


def row_after(planes):
    wide = planes.astype(F32)
    rolled = pltpu.roll(wide, HALF - 1, 1)
    at = lax.broadcasted_iota(jnp.int32, wide.shape, 1)
    return jnp.where(at == HALF - 1, 0.0, rolled).astype(BF16)


def fill_windows(windows, at, even, odd):
    by_row = (row_before(odd), even, odd, row_after(even))
    edge = jnp.zeros((HALF, CH), BF16)
    for row, planes in enumerate(by_row):
        flat = planes.reshape(CELLS, CH)
        for tap in range(3):
            lanes = pl.ds((tap * 4 + row) * CH, CH)
            if tap == 0:
                windows[pl.ds(at, HALF), lanes] = edge
                windows[pl.ds(at + HALF, CELLS - HALF), lanes] = flat[: CELLS - HALF]
            elif tap == 1:
                windows[pl.ds(at, CELLS), lanes] = flat
            else:
                windows[pl.ds(at, CELLS - HALF), lanes] = flat[HALF:]
                windows[pl.ds(at + CELLS - HALF, HALF), lanes] = edge


def silu_slope(preact):
    sigma = jax.nn.sigmoid(preact)
    return sigma * (1.0 + preact * (1.0 - sigma))


def parity_planes(source, frame, spread):
    spread[...] = source[pl.ds(frame * 2 * CELLS, 2 * CELLS), :].astype(F32)
    planes = []
    for par in range(2):
        cols = [spread[pl.ds(par * COLS + col, HALF, stride=2 * COLS), :] for col in range(COLS)]
        planes.append(jnp.stack(cols, axis=0).astype(BF16))
    return planes


def cells_of(kept):
    return jnp.concatenate([kept[pl.ds(tap * 2 * DOWN, 2 * DOWN), :] for tap in range(9)], axis=1)


def prior_body(prior, own_acts, both, acts_out, spread, windows):
    for frame in range(2):
        fill_windows(windows, frame * CELLS, *parity_planes(prior, frame, spread))
    acts_out[pl.ds(2, 4)] = own_acts[...]
    for frame in range(2):
        pre = dot(windows[pl.ds(frame * CELLS, CELLS), :], both[...])
        hid = (pre * jax.nn.sigmoid(pre)).astype(BF16)
        for par in range(2):
            acts_out[frame, par] = hid[:, par * CH : (par + 1) * CH]


def first_body(
    acts, time_far, plane_far, down_far,
    kept_out, strided_out, part_out, times_out,
    first_time, down_plane, down_time, sems,
):
    loads = start(
        sems, (0, time_far, first_time), (1, plane_far, down_plane), (2, down_far, down_time)
    )
    loads[0].wait()
    times = first_time[...].reshape(3 * CH, CH)
    for frame in range(2):
        mixed = []
        for par in range(2):
            taps = jnp.concatenate([acts[frame + k, par] for k in range(3)], axis=1)
            here = acts[4 + frame, par].astype(F32) + dot(taps, times)
            mixed.append(here.astype(BF16).reshape(COLS, HALF, CH))
        by_row = (row_before(mixed[1]), mixed[0], mixed[1])
        for row in range(3):
            for tap in range(3):
                at = (row * 3 + tap) * 2 * DOWN + frame * DOWN
                for col in range(COLS // 2):
                    rows = pl.ds(at + col * HALF, HALF)
                    where = 2 * col + tap - 1
                    if where < 0:
                        kept_out[rows, :] = jnp.zeros((HALF, CH), BF16)
                    else:
                        kept_out[rows, :] = by_row[row][where]
    loads[1].wait()
    kernel = down_plane[...].reshape(9 * CH, WIDE)
    strided = dot(cells_of(kept_out), kernel).astype(BF16).reshape(2, DOWN, WIDE)
    strided_out[...] = strided
    for half in range(2):
        kept_out[pl.ds(STRIDED_AT + half * DOWN, DOWN), :] = strided[
            0, :, half * CH : (half + 1) * CH
        ]
    loads[2].wait()
    part_out[...] = dot(strided[0], down_time[2])
    times_out[...] = down_time[pl.ds(0, 2)]


def rows_body(
    core, rows, last_far, mine_out, away_out, last_time, spread, padded, turned, frames, sems
):
    loads = start(sems, (0, last_far, last_time))
    cotan = rows[...].astype(F32)
    spread[...] = cotan.reshape(HALF * 8, CH)
    for half in range(2):
        padded[pl.ds(0, DOWN), pl.ds(half * CH, CH)] = spread[pl.ds(half, DOWN, stride=2), :]
    padded[pl.ds(DOWN, 8), :] = jnp.zeros((8, WIDE), F32)
    loads[0].wait()
    total = padded[pl.ds(0, DOWN), :]
    for k in range(3):
        taps = padded[pl.ds(4 * (2 - k), DOWN), :].astype(BF16)
        total = total + dot_nt(taps, last_time[k])
    for half in range(2):
        turned[pl.ds(half, DOWN, stride=2), :] = total[:, half * CH : (half + 1) * CH]
    both = jnp.concatenate([turned[...].reshape(HALF, 8, CH), cotan], axis=1)
    frames[...] = both.reshape(HALF // 2, 2, 16, CH)
    here = core[0]
    mine_out[...] = frames[:, pl.ds(here, 1)].reshape(HALF // 2, 16, CH).astype(BF16)
    away_out[...] = frames[:, pl.ds(1 - here, 1)].reshape(HALF // 2, 16, CH).astype(BF16)


def join_body(core, mine, theirs, sent_out):
    here = core[0]
    own, other = mine[...].astype(F32), theirs[...].astype(F32)
    sent_out[:, pl.ds(0, 16), :] = jnp.where(here == 0, own, other).astype(BF16)
    sent_out[:, pl.ds(16, 16), :] = jnp.where(here == 0, other, own).astype(BF16)


def own_body(
    own_far, plane_far,
    acts_out, pre_out, both_out,
    own, first_plane, cells, windows, sems,
):
    loads = start(sems, (0, own_far, own), (1, plane_far, first_plane))
    both_out[...] = jnp.zeros_like(both_out)
    loads[0].wait()
    for frame in range(2):
        planes = parity_planes(own, frame, cells)
        fill_windows(windows, frame * CELLS, *planes)
        for par in range(2):
            acts_out[2 + frame, par] = planes[par].reshape(CELLS, CH)
    loads[1].wait()
    for tap in range(3):
        for row in range(4):
            at = pl.ds((tap * 4 + row) * CH, CH)
            if row < 3:
                both_out[at, pl.ds(0, CH)] = first_plane[row, tap]
            if row > 0:
                both_out[at, pl.ds(CH, CH)] = first_plane[row - 1, tap]
    for frame in range(2):
        pre = dot(windows[pl.ds(frame * CELLS, CELLS), :], both_out[...])
        hid = (pre * jax.nn.sigmoid(pre)).astype(BF16)
        for par in range(2):
            acts_out[frame, par] = hid[:, par * CH : (par + 1) * CH]
            pre_out[frame, par] = pre[:, par * CH : (par + 1) * CH]


def cotan_body(
    received,
    grad_lowered_out, cot_out,
    spread,
):
    spread[...] = received[...].astype(F32).reshape(HALF * 16, CH)
    for at, out in ((0, grad_lowered_out), (8, cot_out)):
        parts = []
        for col in range(4):
            halves = [
                spread[pl.ds(at + col * 2 + half, HALF, stride=16), :] for half in range(2)
            ]
            parts.append(jnp.concatenate(halves, axis=1))
        out[...] = jnp.concatenate(parts, axis=0).astype(BF16)


def middle_body(prior, part, times, grad_lowered, cot, lowered_out, sent_out):
    pre = dot(prior[0], times[0]) + dot(prior[1], times[1]) + part[...]
    lowered_out[...] = (pre * jax.nn.sigmoid(pre)).astype(BF16)
    sent_out[pl.ds(0, DOWN), :] = (grad_lowered[...].astype(F32) * silu_slope(pre)).astype(BF16)
    sent_out[pl.ds(DOWN, DOWN), :] = cot[...]


BACK = (
    (0, 0, 0, 0, 1, 1),
    (0, 1, 0, 1, 1, 0),
    (0, 1, 0, 0, 1, 2),
    (1, 0, 1, 0, 0, 1),
    (1, 0, 0, 0, 2, 1),
    (1, 1, 1, 1, 0, 0),
    (1, 1, 1, 0, 0, 2),
    (1, 1, 0, 1, 2, 0),
    (1, 1, 0, 0, 2, 2),
)


def time_grads_body(
    sent, lowered, prior, kept, down_far, plane_far,
    times_out, kernels_out, grads_out,
    down_time, down_plane, sems,
):
    loads = start(sems, (0, down_far, down_time), (1, plane_far, down_plane))
    kernels_out[...] = jnp.zeros_like(kernels_out)
    wide = lowered[...].astype(F32)
    for col in range(4):
        for half in range(2):
            grads_out[pl.ds(LOWERED_AT + col * 2 + half, HALF, stride=8), :] = wide[
                col * HALF : (col + 1) * HALF, half * CH : (half + 1) * CH
            ]
    own = [kept[pl.ds(STRIDED_AT + half * DOWN, DOWN), :] for half in range(2)]
    taps = (prior[0], prior[1], jnp.concatenate(own, axis=1))
    grad_pre = sent[pl.ds(0, DOWN), :]
    for k in range(3):
        down = dot_tn(taps[k], grad_pre)
        for half in range(2):
            lanes = slice(half * CH, (half + 1) * CH)
            grads_out[pl.ds((half * 3 + k) * WIDE, WIDE), :] = down[:, lanes]
    last = dot_tn(lowered[...], sent[pl.ds(DOWN, DOWN), :])
    for half in range(2):
        grads_out[pl.ds((6 + half) * WIDE, WIDE), :] = last[:, half * CH : (half + 1) * CH]
    for load in loads:
        load.wait()
    part = dot_nt(grad_pre, down_time[2])
    for half in range(2):
        grads_out[pl.ds(PART_AT + half * DOWN, DOWN), :] = part[:, half * CH : (half + 1) * CH]
    times_out[...] = down_time[pl.ds(0, 2)]
    for row_par, col_par, row_off, col_off, row, tap in BACK:
        rows = pl.ds((row_par * 2 + col_par) * CH, CH)
        lanes = pl.ds((row_off * 2 + col_off) * WIDE, WIDE)
        kernels_out[rows, lanes] = down_plane[row, tap]


def grad_strided_of(grads, ahead, times):
    following = ahead[pl.ds(0, DOWN), :]
    part = [grads[pl.ds(PART_AT + half * DOWN, DOWN), :] for half in range(2)]
    even = jnp.concatenate(part, axis=1) + dot_nt(following, times[0])
    return even.astype(BF16), dot_nt(following, times[1]).astype(BF16)


def back_body(ahead, grads, times, kernels, sent_out, shifted):
    for half in range(2):
        sent_out[pl.ds(4 * CELLS + half * DOWN, DOWN), :] = ahead[
            pl.ds(DOWN, DOWN), pl.ds(half * CH, CH)
        ]
    for frame, strided in enumerate(grad_strided_of(grads, ahead, times)):
        planes = strided.reshape(4, HALF, WIDE)
        for row_off, rows in ((0, planes), (1, row_after(planes))):
            flat = rows.reshape(DOWN, WIDE)
            here = pl.ds((row_off * 2) * WIDE, WIDE)
            after = pl.ds((row_off * 2 + 1) * WIDE, WIDE)
            shifted[pl.ds(frame * DOWN, DOWN), here] = flat
            shifted[pl.ds(frame * DOWN, DOWN - HALF), after] = flat[HALF:]
            shifted[pl.ds(frame * DOWN + DOWN - HALF, HALF), after] = jnp.zeros((HALF, WIDE), BF16)
    mixed = dot_nt(shifted[...], kernels[...]).astype(BF16)
    for frame in range(2):
        for par in range(2):
            for col_par in range(2):
                lanes = slice((par * 2 + col_par) * CH, (par * 2 + col_par + 1) * CH)
                for col in range(4):
                    rows = slice(frame * DOWN + col * HALF, frame * DOWN + (col + 1) * HALF)
                    plane = (frame * 2 + par) * COLS + 2 * col + col_par
                    sent_out[pl.ds(plane * HALF, HALF), :] = mixed[rows, lanes]


def plane_grads_body(
    core, grad_mixed, kept, acts, pre, time_far, down_far,
    grads, lowered, ahead,
    mine_out, other_out, windows_out, slope_out, part_out, time_out,
    flat, rows_here, times, sems,
):
    loads = start(sems, (0, time_far, time_out), (1, down_far, times))
    base = 3 * CH + 18 * CH
    flat[pl.ds(base, 8 * WIDE), :] = grads[pl.ds(0, 8 * WIDE), :]
    base += 8 * WIDE
    last = dot_tn(lowered[...], ahead[pl.ds(DOWN, DOWN), :])
    for half in range(2):
        flat[pl.ds(base + half * WIDE, WIDE), :] = last[:, half * CH : (half + 1) * CH]
    cotan = grad_mixed[pl.ds(0, 4 * CELLS), :]
    for k in range(3):
        taps = acts[pl.ds(k, 2)].reshape(4 * CELLS, CH)
        flat[pl.ds(k * CH, CH), :] = dot_tn(taps, cotan)
    for frame in range(2):
        planes = [acts[4 + frame, par].reshape(COLS, HALF, CH) for par in range(2)]
        fill_windows(windows_out, frame * CELLS, *planes)
    slope_out[...] = silu_slope(pre[...])
    loads[0].wait()
    for par in range(2):
        first, second = [
            grad_mixed[pl.ds((frame * 2 + par) * CELLS, CELLS), :] for frame in range(2)
        ]
        part_out[0, par] = dot_nt(first, time_out[2]) + dot_nt(second, time_out[1])
        part_out[1, par] = dot_nt(second, time_out[2])
    loads[1].wait()
    grad_strided = jnp.concatenate(grad_strided_of(grads, ahead, times), axis=0)
    down = dot_tn(cells_of(kept), grad_strided)
    for half in range(2):
        at = 3 * CH + half * 9 * CH
        flat[pl.ds(at, 9 * CH), :] = down[:, half * CH : (half + 1) * CH]
    here = core[0]
    half = EARLY // 2
    mine_out[pl.ds(0, half), :] = flat[pl.ds(pl.multiple_of(here * half, 16), half), :]
    other_out[pl.ds(0, half), :] = flat[
        pl.ds(pl.multiple_of((1 - here) * half, 16), half), :
    ].astype(BF16)
    rows_here[...] = grads[pl.ds(LOWERED_AT, 2 * DOWN), :].reshape(HALF // 2, 2, 8, CH)
    mine_out[pl.ds(half, DOWN), :] = rows_here[:, pl.ds(here, 1)].reshape(DOWN, CH)
    away = rows_here[:, pl.ds(1 - here, 1)].reshape(DOWN, CH)
    other_out[pl.ds(half, DOWN), :] = away.astype(BF16)


def last_body(
    core, ahead, windows, slope, part, first_time, lowered, early_other,
    mine_out, other_out,
    flat,
):
    cotans = [[], []]
    for par in range(2):
        first, second = [
            ahead[pl.ds((frame * 2 + par) * CELLS, CELLS), :] for frame in range(2)
        ]
        hidden = (
            part[0, par] + dot_nt(first, first_time[0]),
            part[1, par] + dot_nt(first, first_time[1]) + dot_nt(second, first_time[0]),
        )
        for frame in range(2):
            cotans[frame].append((hidden[frame] * slope[frame, par]).astype(BF16))
    cotan = jnp.concatenate([jnp.concatenate(parts, axis=1) for parts in cotans], axis=0)
    product = dot_tn(windows[...], cotan)
    for row in range(3):
        for tap in range(3):
            at = (tap * 4 + row) * CH
            flat[pl.ds((row * 3 + tap) * CH, CH), :] = (
                product[at : at + CH, :CH] + product[at + CH : at + 2 * CH, CH:]
            )
    further = [ahead[pl.ds(4 * CELLS + half * DOWN, DOWN), :] for half in range(2)]
    for half in range(2):
        flat[pl.ds(9 * CH + half * WIDE, WIDE), :] = dot_tn(lowered[...], further[half])
    here = core[0]
    half = mine_out.shape[0]
    mine_out[...] = flat[pl.ds(pl.multiple_of(here * half, 16), half), :]
    rows = early_other.shape[0]
    other_out[pl.ds(0, rows), :] = early_other[...]
    other_out[pl.ds(rows, half), :] = flat[
        pl.ds(pl.multiple_of((1 - here) * half, 16), half), :
    ].astype(BF16)


def halves_body(core, early, late, other, half_out, frames_out):
    rows, more = EARLY // 2, LATE // 2
    half_out[pl.ds(0, rows), :] = (
        early[pl.ds(0, rows), :] + other[pl.ds(0, rows), :].astype(F32)
    ).astype(BF16)
    here = core[0]
    chips = HALF // 2
    mine = early[pl.ds(rows, DOWN), :].reshape(chips, 8, CH)
    theirs = other[pl.ds(rows, DOWN), :].astype(F32).reshape(chips, 8, CH)
    frames = [jnp.where(here == 0, mine, theirs), jnp.where(here == 0, theirs, mine)]
    frames_out[...] = jnp.concatenate(frames, axis=1).astype(BF16)
    half_out[pl.ds(rows, more), :] = (
        late[...] + other[pl.ds(rows + DOWN, more), :].astype(F32)
    ).astype(BF16)


def sum_body(blocks, frames, sent_out, padded):
    rows = blocks.shape[1]
    total = blocks[0].astype(F32)
    for block in range(1, blocks.shape[0]):
        total = total + blocks[block].astype(F32)
    padded[...] = jnp.zeros_like(padded)
    padded[pl.ds(0, rows), :] = total
    chips = frames.shape[0]
    share = padded.shape[0] // chips
    for chip in range(chips):
        sent_out[chip, pl.ds(0, share), :] = padded[pl.ds(chip * share, share), :].astype(BF16)
        sent_out[chip, pl.ds(share, 16), :] = frames[chip]


def piece_body(received, piece_out):
    share = piece_out.shape[1]
    total = received[0, pl.ds(0, share), :].astype(F32)
    for chip in range(1, received.shape[0]):
        total = total + received[chip, pl.ds(0, share), :].astype(F32)
    piece = total.astype(BF16)
    for chip in range(piece_out.shape[0]):
        piece_out[chip] = piece


def spread_body(pieces, part_out):
    flat = pieces[...].reshape(-1, CH).astype(F32)
    part = flat[: part_out.shape[1]].astype(BF16)
    for block in range(part_out.shape[0]):
        part_out[block] = part


def results_body(
    core, mine, other,
    first_plane_out, first_time_out, down_plane_out, down_time_out, last_time_out,
    early, late,
):
    here = core[0]
    rows, more = EARLY // 2, LATE // 2
    for half, at in ((mine, here), (other, 1 - here)):
        early[pl.ds(pl.multiple_of(at * rows, 16), rows), :] = half[pl.ds(0, rows), :]
        late[pl.ds(pl.multiple_of(at * more, 16), more), :] = half[pl.ds(rows, more), :]
    first_plane_out[...] = late[pl.ds(0, 9 * CH), :]
    first_time_out[...] = early[pl.ds(0, 3 * CH), :]
    for half in range(2):
        lanes = pl.ds(half * CH, CH)
        down_plane_out[:, lanes] = early[pl.ds(3 * CH + half * 9 * CH, 9 * CH), :]
        down_time_out[:, lanes] = early[pl.ds(21 * CH + half * 6 * CH, 6 * CH), :]
        last_time_out[pl.ds(0, WIDE), lanes] = late[pl.ds(9 * CH + half * WIDE, WIDE), :]
        last_time_out[pl.ds(WIDE, WIDE), lanes] = early[pl.ds(37 * CH + half * WIDE, WIDE), :]
        last_time_out[pl.ds(2 * WIDE, WIDE), lanes] = early[pl.ds(33 * CH + half * WIDE, WIDE), :]


def output_body(received, last_time, output, spread, padded):
    frames = received[:, pl.ds(received.shape[1] - 16, 16), :]
    spread[...] = frames.astype(F32).reshape(HALF * 8, CH)
    padded[pl.ds(0, 8), :] = jnp.zeros((8, WIDE), F32)
    for half in range(2):
        padded[pl.ds(8, DOWN), pl.ds(half * CH, CH)] = spread[pl.ds(half, DOWN, stride=2), :]
    total = padded[pl.ds(8, DOWN), :]
    for k in range(3):
        taps = padded[pl.ds(4 * k, DOWN), :].astype(BF16)
        total = total + dot(taps, last_time[k])
    output[...] = total.astype(BF16)


def from_behind(block, distance):
    devices = range(lax.axis_size("seq"))
    route = [(i - distance, i) for i in devices if i - distance in devices]
    return lax.ppermute(block, "seq", route)


def swap_cores(block):
    count = lax.axis_size("seq")
    return lax.ppermute(block, "seq", [(i, i ^ 1) for i in range(count)])


def exchange_clip(blocks):
    return lax.all_to_all(blocks, "clip", split_axis=0, concat_axis=0, tiled=True)


def exchange_chips(blocks):
    count = lax.axis_size("seq")
    groups = [list(range(core, count, 2)) for core in range(2)]
    return lax.all_to_all(
        blocks, "seq", split_axis=0, concat_axis=0, axis_index_groups=groups, tiled=True
    )


def local(clip_in, first_plane, first_time, down_plane, down_time, last_time, cotan_out):
    own = clip_in.reshape(4 * CELLS, CH)
    prior = from_behind(own, 1)
    flat_frames = (2, 2, CELLS, CH)
    core = (lax.axis_index("seq") % 2).astype(jnp.int32).reshape(1)
    mine, away = call(
        rows_body,
        [(S, core), (V, cotan_out[0].reshape(HALF, 8, CH)), (H, last_time)],
        [(P_, (HALF // 2, 16, CH), BF16), (V, (HALF // 2, 16, CH), BF16)],
        [
            ((3, WIDE, WIDE), BF16),
            ((HALF * 8, CH), F32),
            ((DOWN + 8, WIDE), F32),
            ((HALF * 8, CH), F32),
            ((HALF // 2, 2, 16, CH), F32),
        ],
        copies=1,
    )
    theirs = swap_cores(away)
    acts, pre_first, both = call(
        own_body,
        [(H, own), (H, first_plane)],
        [
            (P_, (4, 2, CELLS, CH), BF16),
            (P_, flat_frames, F32),
            (P_, (12 * CH, WIDE), BF16),
        ],
        [
            ((4 * CELLS, CH), BF16),
            ((3, 3, CH, CH), BF16),
            ((2 * CELLS, CH), F32),
            ((2 * CELLS, 12 * CH), BF16),
        ],
        copies=2,
    )
    (acts,) = call(
        prior_body,
        [(P_, prior), (P_, acts), (P_, both)],
        [(P_, (6, 2, CELLS, CH), BF16)],
        [((2 * CELLS, CH), F32), ((2 * CELLS, 12 * CH), BF16)],
    )
    times = (P_, (2, WIDE, WIDE), BF16)
    theirs, acts = lax.optimization_barrier((theirs, acts))
    (sent,) = call(
        join_body,
        [(S, core), (P_, mine), (P_, theirs)],
        [(V, (HALF // 2, HALF, CH), BF16)],
    )
    received = exchange_chips(sent).reshape(HALF, 16, CH)
    kept, strided, part, near_times = call(
        first_body,
        [
            (P_, acts), (H, first_time), (H, down_plane), (H, down_time),
        ],
        [
            (P_, (KEPT, CH), BF16),
            (P_, (2, DOWN, WIDE), BF16),
            (P_, (DOWN, WIDE), F32),
            times,
        ],
        [
            ((3, CH, CH), BF16),
            ((3, 3, CH, WIDE), BF16),
            ((3, WIDE, WIDE), BF16),
        ],
        copies=3,
    )
    strided_prior = from_behind(strided, 1)
    down = (P_, (DOWN, WIDE), BF16)
    grad_lowered, cot = call(
        cotan_body, [(P_, received)], [down, down], [((HALF * 16, CH), F32)]
    )
    lowered, sent = call(
        middle_body,
        [(P_, strided_prior), (P_, part), (P_, near_times), (P_, grad_lowered), (P_, cot)],
        [down, (P_, (2 * DOWN, WIDE), BF16)],
    )
    ahead = from_behind(sent, -1)
    near_times, kernels, time_grads = call(
        time_grads_body,
        [
            (P_, sent), (P_, lowered), (P_, strided_prior), (P_, kept),
            (H, down_time), (H, down_plane),
        ],
        [
            times,
            (P_, (4 * CH, 4 * WIDE), BF16),
            (P_, (PART_AT + 2 * DOWN, CH), F32),
        ],
        [((3, WIDE, WIDE), BF16), ((3, 3, CH, WIDE), BF16)],
        copies=2,
    )
    (sent,) = call(
        back_body,
        [(P_, ahead), (P_, time_grads), (P_, near_times), (P_, kernels)],
        [(P_, (4 * CELLS + 2 * DOWN, CH), BF16)],
        [((2 * DOWN, 4 * WIDE), BF16)],
    )
    further = from_behind(sent, -1)
    early, early_other, windows, slope, part, near_time = call(
        plane_grads_body,
        [
            (S, core), (P_, sent), (P_, kept), (P_, acts), (P_, pre_first),
            (H, first_time), (H, down_time), (P_, time_grads), (P_, lowered), (P_, ahead),
        ],
        [
            (P_, (EARLY // 2 + DOWN, CH), F32),
            (P_, (EARLY // 2 + DOWN, CH), BF16),
            (P_, (2 * CELLS, 12 * CH), BF16),
            (P_, flat_frames, F32),
            (P_, flat_frames, F32),
            (P_, (3, CH, CH), BF16),
        ],
        [((EARLY, CH), F32), ((HALF // 2, 2, 8, CH), F32), ((3, WIDE, WIDE), BF16)],
        copies=2,
    )
    late, other = call(
        last_body,
        [
            (S, core), (P_, further), (P_, windows), (P_, slope), (P_, part), (P_, near_time),
            (P_, lowered), (P_, early_other),
        ],
        [(P_, (LATE // 2, CH), F32), (P_, ((EARLY + LATE) // 2 + DOWN, CH), BF16)],
        [((LATE, CH), F32)],
        flops=600000000,
        size=2000000,
    )

    clips = lax.axis_size("clip")
    chips = lax.axis_size("seq") // 2
    half_rows = (EARLY + LATE) // 2
    part_rows = half_rows // clips
    other = swap_cores(other)
    half, frames = call(
        halves_body,
        [(S, core), (P_, early), (P_, late), (V, other)],
        [(P_, (half_rows, CH), BF16), (V, (chips, 16, CH), BF16)],
    )
    blocks = exchange_clip(half.reshape(clips, part_rows, CH))
    share = 16 * (-(-part_rows // (16 * chips)))
    (sent,) = call(
        sum_body,
        [(V, blocks), (V, frames)],
        [(V, (chips, share + 16, CH), BF16)],
        [((chips * share, CH), F32)],
    )
    received = exchange_chips(sent)
    (pieces,) = call(piece_body, [(V, received)], [(V, (chips, share, CH), BF16)])
    pieces = exchange_chips(pieces)
    (output,) = call(
        output_body,
        [(V, received), (V, last_time)],
        [(V, (DOWN, WIDE), BF16)],
        [((HALF * 8, CH), F32), ((DOWN + 8, WIDE), F32)],
    )
    (parts,) = call(spread_body, [(V, pieces)], [(V, (clips, part_rows, CH), BF16)])
    half = exchange_clip(parts).reshape(half_rows, CH)
    other = swap_cores(half)
    grads = call(
        results_body,
        [(S, core), (V, half), (V, other)],
        [
            (V, (9 * CH, CH), BF16),
            (V, (3 * CH, CH), BF16),
            (V, (9 * CH, WIDE), BF16),
            (V, (3 * WIDE, WIDE), BF16),
            (V, (3 * WIDE, WIDE), BF16),
        ],
        [((EARLY, CH), BF16), ((LATE, CH), BF16)],
    )
    shapes = ((3, 3, CH, CH), (3, CH, CH), (3, 3, CH, WIDE), (3, WIDE, WIDE), (3, WIDE, WIDE))
    grads = [grad.reshape(shape) for grad, shape in zip(grads, shapes)]
    return (output.reshape(1, HALF, 1, 4, WIDE), *grads)


def solution(mesh):
    placed = (
        P("clip", "seq", None, None, None),
        P(),
        P(),
        P(),
        P(),
        P(),
        P("clip", None, "seq", None, None),
    )
    return jax.shard_map(
        local,
        mesh=mesh,
        in_specs=placed,
        out_specs=(P("clip", None, "seq", None, None), P(), P(), P(), P(), P()),
        check_vma=False,
    )
```

```python
import jax
import jax.numpy as jnp
from jax import lax
from jax.experimental import pallas as pl
from jax.experimental.pallas import tpu as pltpu
from jax.sharding import PartitionSpec as P


F32 = jnp.float32
BF16 = jnp.bfloat16
COLS = 8
HALF = 32
CELLS = COLS * HALF
DOWN = CELLS // 2
CH = 128
WIDE = 256
STRIDED_AT = 9 * 2 * DOWN
KEPT = STRIDED_AT + 2 * DOWN
LOWERED_AT = 8 * WIDE
PART_AT = LOWERED_AT + 2 * DOWN
GRADS = (9 + 3 + 18 + 12 + 12) * CH


def dot(left, right):
    return lax.dot_general(left, right, (((1,), (0,)), ((), ())), preferred_element_type=F32)


def dot_nt(left, right):
    return lax.dot_general(left, right, (((1,), (1,)), ((), ())), preferred_element_type=F32)


def dot_tn(left, right):
    return lax.dot_general(left, right, (((0,), (0,)), ((), ())), preferred_element_type=F32)


V, P_, H, S = "vmem", "pinned", "hbm", "smem"
SPACES = {V: pltpu.VMEM, P_: pltpu.VMEM, H: pltpu.HBM, S: pltpu.SMEM}


def placed_input(space, array):
    if space in (P_, H):
        return pltpu.with_memory_space_constraint(array, SPACES[space])
    return array


def placed_output(space, shape, kind):
    if space in (P_, H):
        return SPACES[space](shape, kind)
    return jax.ShapeDtypeStruct(shape, kind)


def call(body, ins, outs, scratch=(), copies=0, flops=1000, size=8000000):
    scratch = [pltpu.VMEM(shape, kind) for shape, kind in scratch]
    if copies:
        scratch.append(pltpu.SemaphoreType.DMA((copies,)))
    return pl.pallas_call(
        body,
        out_shape=[placed_output(*out) for out in outs],
        in_specs=[pl.BlockSpec(memory_space=SPACES[space]) for space, _ in ins],
        out_specs=[pl.BlockSpec(memory_space=SPACES[space]) for space, _, _ in outs],
        scratch_shapes=scratch,
        compiler_params=pltpu.CompilerParams(vmem_limit_bytes=24 * 1024 * 1024),
        cost_estimate=pl.CostEstimate(flops=flops, bytes_accessed=size, transcendentals=0),
    )(*[placed_input(*given) for given in ins])


def start(sems, *pairs):
    copies = [
        pltpu.make_async_copy(source, target, sems.at[at]) for at, source, target in pairs
    ]
    for copy in copies:
        copy.start()
    return copies


def row_before(planes):
    wide = planes.astype(F32)
    rolled = pltpu.roll(wide, 1, 1)
    at = lax.broadcasted_iota(jnp.int32, wide.shape, 1)
    return jnp.where(at == 0, 0.0, rolled).astype(BF16)


def row_after(planes):
    wide = planes.astype(F32)
    rolled = pltpu.roll(wide, HALF - 1, 1)
    at = lax.broadcasted_iota(jnp.int32, wide.shape, 1)
    return jnp.where(at == HALF - 1, 0.0, rolled).astype(BF16)


def fill_windows(windows, at, even, odd):
    by_row = (row_before(odd), even, odd, row_after(even))
    edge = jnp.zeros((HALF, CH), BF16)
    for row, planes in enumerate(by_row):
        flat = planes.reshape(CELLS, CH)
        for tap in range(3):
            lanes = pl.ds((tap * 4 + row) * CH, CH)
            if tap == 0:
                windows[pl.ds(at, HALF), lanes] = edge
                windows[pl.ds(at + HALF, CELLS - HALF), lanes] = flat[: CELLS - HALF]
            elif tap == 1:
                windows[pl.ds(at, CELLS), lanes] = flat
            else:
                windows[pl.ds(at, CELLS - HALF), lanes] = flat[HALF:]
                windows[pl.ds(at + CELLS - HALF, HALF), lanes] = edge


def silu_slope(preact):
    sigma = jax.nn.sigmoid(preact)
    return sigma * (1.0 + preact * (1.0 - sigma))


def parity_planes(source, frame, spread):
    spread[...] = source[pl.ds(frame * 2 * CELLS, 2 * CELLS), :].astype(F32)
    planes = []
    for par in range(2):
        cols = [spread[pl.ds(par * COLS + col, HALF, stride=2 * COLS), :] for col in range(COLS)]
        planes.append(jnp.stack(cols, axis=0).astype(BF16))
    return planes


def cells_of(kept):
    return jnp.concatenate([kept[pl.ds(tap * 2 * DOWN, 2 * DOWN), :] for tap in range(9)], axis=1)


def prior_body(prior, own_acts, both, acts_out, spread, windows):
    for frame in range(2):
        fill_windows(windows, frame * CELLS, *parity_planes(prior, frame, spread))
    acts_out[pl.ds(2, 4)] = own_acts[...]
    for frame in range(2):
        pre = dot(windows[pl.ds(frame * CELLS, CELLS), :], both[...])
        hid = (pre * jax.nn.sigmoid(pre)).astype(BF16)
        for par in range(2):
            acts_out[frame, par] = hid[:, par * CH : (par + 1) * CH]


def first_body(
    acts, time_far, plane_far, down_far,
    kept_out, strided_out, part_out, times_out,
    first_time, down_plane, down_time, sems,
):
    loads = start(
        sems, (0, time_far, first_time), (1, plane_far, down_plane), (2, down_far, down_time)
    )
    loads[0].wait()
    times = first_time[...].reshape(3 * CH, CH)
    for frame in range(2):
        mixed = []
        for par in range(2):
            taps = jnp.concatenate([acts[frame + k, par] for k in range(3)], axis=1)
            here = acts[4 + frame, par].astype(F32) + dot(taps, times)
            mixed.append(here.astype(BF16).reshape(COLS, HALF, CH))
        by_row = (row_before(mixed[1]), mixed[0], mixed[1])
        for row in range(3):
            for tap in range(3):
                at = (row * 3 + tap) * 2 * DOWN + frame * DOWN
                for col in range(COLS // 2):
                    rows = pl.ds(at + col * HALF, HALF)
                    where = 2 * col + tap - 1
                    if where < 0:
                        kept_out[rows, :] = jnp.zeros((HALF, CH), BF16)
                    else:
                        kept_out[rows, :] = by_row[row][where]
    loads[1].wait()
    kernel = down_plane[...].reshape(9 * CH, WIDE)
    strided = dot(cells_of(kept_out), kernel).astype(BF16).reshape(2, DOWN, WIDE)
    strided_out[...] = strided
    for half in range(2):
        kept_out[pl.ds(STRIDED_AT + half * DOWN, DOWN), :] = strided[
            0, :, half * CH : (half + 1) * CH
        ]
    loads[2].wait()
    part_out[...] = dot(strided[0], down_time[2])
    times_out[...] = down_time[pl.ds(0, 2)]


def rows_body(
    core, rows, last_far, mine_out, away_out, last_time, spread, padded, turned, frames, sems
):
    loads = start(sems, (0, last_far, last_time))
    cotan = rows[...].astype(F32)
    spread[...] = cotan.reshape(HALF * 8, CH)
    for half in range(2):
        padded[pl.ds(0, DOWN), pl.ds(half * CH, CH)] = spread[pl.ds(half, DOWN, stride=2), :]
    padded[pl.ds(DOWN, 8), :] = jnp.zeros((8, WIDE), F32)
    loads[0].wait()
    total = padded[pl.ds(0, DOWN), :]
    for k in range(3):
        taps = padded[pl.ds(4 * (2 - k), DOWN), :].astype(BF16)
        total = total + dot_nt(taps, last_time[k])
    for half in range(2):
        turned[pl.ds(half, DOWN, stride=2), :] = total[:, half * CH : (half + 1) * CH]
    both = jnp.concatenate([turned[...].reshape(HALF, 8, CH), cotan], axis=1)
    frames[...] = both.reshape(HALF // 2, 2, 16, CH)
    here = core[0]
    mine_out[...] = frames[:, pl.ds(here, 1)].reshape(HALF // 2, 16, CH).astype(BF16)
    away_out[...] = frames[:, pl.ds(1 - here, 1)].reshape(HALF // 2, 16, CH).astype(BF16)


def join_body(core, mine, theirs, sent_out):
    here = core[0]
    own, other = mine[...].astype(F32), theirs[...].astype(F32)
    sent_out[:, pl.ds(0, 16), :] = jnp.where(here == 0, own, other).astype(BF16)
    sent_out[:, pl.ds(16, 16), :] = jnp.where(here == 0, other, own).astype(BF16)


def own_body(
    own_far, plane_far,
    acts_out, pre_out, both_out,
    own, first_plane, cells, windows, sems,
):
    loads = start(sems, (0, own_far, own), (1, plane_far, first_plane))
    both_out[...] = jnp.zeros_like(both_out)
    loads[0].wait()
    for frame in range(2):
        planes = parity_planes(own, frame, cells)
        fill_windows(windows, frame * CELLS, *planes)
        for par in range(2):
            acts_out[2 + frame, par] = planes[par].reshape(CELLS, CH)
    loads[1].wait()
    for tap in range(3):
        for row in range(4):
            at = pl.ds((tap * 4 + row) * CH, CH)
            if row < 3:
                both_out[at, pl.ds(0, CH)] = first_plane[row, tap]
            if row > 0:
                both_out[at, pl.ds(CH, CH)] = first_plane[row - 1, tap]
    for frame in range(2):
        pre = dot(windows[pl.ds(frame * CELLS, CELLS), :], both_out[...])
        hid = (pre * jax.nn.sigmoid(pre)).astype(BF16)
        for par in range(2):
            acts_out[frame, par] = hid[:, par * CH : (par + 1) * CH]
            pre_out[frame, par] = pre[:, par * CH : (par + 1) * CH]


def cotan_body(
    received,
    grad_lowered_out, cot_out,
    spread,
):
    spread[...] = received[...].astype(F32).reshape(HALF * 16, CH)
    for at, out in ((0, grad_lowered_out), (8, cot_out)):
        parts = []
        for col in range(4):
            halves = [
                spread[pl.ds(at + col * 2 + half, HALF, stride=16), :] for half in range(2)
            ]
            parts.append(jnp.concatenate(halves, axis=1))
        out[...] = jnp.concatenate(parts, axis=0).astype(BF16)


def middle_body(prior, part, times, grad_lowered, cot, lowered_out, sent_out):
    pre = dot(prior[0], times[0]) + dot(prior[1], times[1]) + part[...]
    lowered_out[...] = (pre * jax.nn.sigmoid(pre)).astype(BF16)
    sent_out[pl.ds(0, DOWN), :] = (grad_lowered[...].astype(F32) * silu_slope(pre)).astype(BF16)
    sent_out[pl.ds(DOWN, DOWN), :] = cot[...]


BACK = (
    (0, 0, 0, 0, 1, 1),
    (0, 1, 0, 1, 1, 0),
    (0, 1, 0, 0, 1, 2),
    (1, 0, 1, 0, 0, 1),
    (1, 0, 0, 0, 2, 1),
    (1, 1, 1, 1, 0, 0),
    (1, 1, 1, 0, 0, 2),
    (1, 1, 0, 1, 2, 0),
    (1, 1, 0, 0, 2, 2),
)


def time_grads_body(
    sent, lowered, prior, kept, acts, pre, down_far, plane_far,
    times_out, kernels_out, grads_out, windows_out, slope_out,
    down_plane, sems,
):
    loads = start(sems, (0, down_far, times_out), (1, plane_far, down_plane))
    kernels_out[...] = jnp.zeros_like(kernels_out)
    for frame in range(2):
        planes = [acts[4 + frame, par].reshape(COLS, HALF, CH) for par in range(2)]
        fill_windows(windows_out, frame * CELLS, *planes)
    slope_out[...] = silu_slope(pre[...])
    wide = lowered[...].astype(F32)
    for col in range(4):
        for half in range(2):
            grads_out[pl.ds(LOWERED_AT + col * 2 + half, HALF, stride=8), :] = wide[
                col * HALF : (col + 1) * HALF, half * CH : (half + 1) * CH
            ]
    own = [kept[pl.ds(STRIDED_AT + half * DOWN, DOWN), :] for half in range(2)]
    taps = (prior[0], prior[1], jnp.concatenate(own, axis=1))
    grad_pre = sent[pl.ds(0, DOWN), :]
    for k in range(3):
        down = dot_tn(taps[k], grad_pre)
        for half in range(2):
            lanes = slice(half * CH, (half + 1) * CH)
            grads_out[pl.ds((half * 3 + k) * WIDE, WIDE), :] = down[:, lanes]
    last = dot_tn(lowered[...], sent[pl.ds(DOWN, DOWN), :])
    for half in range(2):
        grads_out[pl.ds((6 + half) * WIDE, WIDE), :] = last[:, half * CH : (half + 1) * CH]
    for load in loads:
        load.wait()
    part = dot_nt(grad_pre, times_out[2])
    for half in range(2):
        grads_out[pl.ds(PART_AT + half * DOWN, DOWN), :] = part[:, half * CH : (half + 1) * CH]
    for row_par, col_par, row_off, col_off, row, tap in BACK:
        rows = pl.ds((row_par * 2 + col_par) * CH, CH)
        lanes = pl.ds((row_off * 2 + col_off) * WIDE, WIDE)
        kernels_out[rows, lanes] = down_plane[row, tap]


def back_body(
    core, ahead, further, grads, times, kernels, kept, acts, windows, slope, lowered, time_far,
    mine_out, other_out,
    shifted, mixed, flat, rows_here, first_time, sems,
):
    loads = start(sems, (0, time_far, first_time))
    near, far = ahead[pl.ds(0, DOWN), :], further[pl.ds(0, DOWN), :]
    part = [grads[pl.ds(PART_AT + half * DOWN, DOWN), :] for half in range(2)]
    strided = [
        jnp.concatenate(part, axis=1) + dot_nt(near, times[0]),
        dot_nt(near, times[1]),
        dot_nt(near, times[2]) + dot_nt(far, times[0]),
        dot_nt(far, times[1]),
    ]
    strided = [frame.astype(BF16) for frame in strided]
    for frame in range(4):
        planes = strided[frame].reshape(4, HALF, WIDE)
        for row_off, rows in ((0, planes), (1, row_after(planes))):
            cells = rows.reshape(DOWN, WIDE)
            here = pl.ds((row_off * 2) * WIDE, WIDE)
            after = pl.ds((row_off * 2 + 1) * WIDE, WIDE)
            shifted[pl.ds(frame * DOWN, DOWN), here] = cells
            shifted[pl.ds(frame * DOWN, DOWN - HALF), after] = cells[HALF:]
            shifted[pl.ds(frame * DOWN + DOWN - HALF, HALF), after] = jnp.zeros((HALF, WIDE), BF16)
    product = dot_nt(shifted[...], kernels[...]).astype(BF16)
    for frame in range(4):
        for par in range(2):
            for col_par in range(2):
                lanes = slice((par * 2 + col_par) * CH, (par * 2 + col_par + 1) * CH)
                for col in range(4):
                    rows = slice(frame * DOWN + col * HALF, frame * DOWN + (col + 1) * HALF)
                    plane = (frame * 2 + par) * COLS + 2 * col + col_par
                    mixed[pl.ds(plane * HALF, HALF), :] = product[rows, lanes]

    loads[0].wait()
    taps = jnp.concatenate([first_time[k] for k in range(3)], axis=1)
    cotans = []
    for frame in range(2):
        parts = []
        for par in range(2):
            frames = [
                mixed[pl.ds(((frame + 2 - k) * 2 + par) * CELLS, CELLS), :] for k in range(3)
            ]
            grad_hidden = dot_nt(jnp.concatenate(frames, axis=1), taps)
            parts.append((grad_hidden * slope[frame, par]).astype(BF16))
        cotans.append(jnp.concatenate(parts, axis=1))
    product = dot_tn(windows[...], jnp.concatenate(cotans, axis=0))
    for row in range(3):
        for tap in range(3):
            at = (tap * 4 + row) * CH
            flat[pl.ds((row * 3 + tap) * CH, CH), :] = (
                product[at : at + CH, :CH] + product[at + CH : at + 2 * CH, CH:]
            )
    cotan = mixed[pl.ds(0, 4 * CELLS), :]
    for k in range(3):
        flat[pl.ds((9 + k) * CH, CH), :] = dot_tn(acts[pl.ds(k, 2)].reshape(4 * CELLS, CH), cotan)
    down = dot_tn(cells_of(kept), jnp.concatenate(strided[:2], axis=0))
    last = [dot_tn(lowered[...], sent[pl.ds(DOWN, DOWN), :]) for sent in (further, ahead)]
    flat[pl.ds(30 * CH, 12 * CH), :] = grads[pl.ds(0, 12 * CH), :]
    for half in range(2):
        lanes = slice(half * CH, (half + 1) * CH)
        flat[pl.ds((12 + half * 9) * CH, 9 * CH), :] = down[:, lanes]
        base = (42 + half * 6) * CH
        for k in range(2):
            flat[pl.ds(base + k * WIDE, WIDE), :] = last[k][:, lanes]
        flat[pl.ds(base + 2 * WIDE, WIDE), :] = grads[pl.ds((6 + half) * WIDE, WIDE), :]

    here = core[0]
    half = GRADS // 2
    mine_out[pl.ds(0, half), :] = flat[pl.ds(pl.multiple_of(here * half, 16), half), :]
    other_out[pl.ds(0, half), :] = flat[
        pl.ds(pl.multiple_of((1 - here) * half, 16), half), :
    ].astype(BF16)
    rows_here[...] = grads[pl.ds(LOWERED_AT, 2 * DOWN), :].reshape(HALF // 2, 2, 8, CH)
    mine_out[pl.ds(half, DOWN), :] = rows_here[:, pl.ds(here, 1)].reshape(DOWN, CH)
    away = rows_here[:, pl.ds(1 - here, 1)].reshape(DOWN, CH)
    other_out[pl.ds(half, DOWN), :] = away.astype(BF16)


def halves_body(core, own, other, half_out, frames_out):
    rows = half_out.shape[0]
    half_out[...] = (own[pl.ds(0, rows), :] + other[pl.ds(0, rows), :].astype(F32)).astype(BF16)
    here = core[0]
    chips = HALF // 2
    mine = own[pl.ds(rows, DOWN), :].reshape(chips, 8, CH)
    theirs = other[pl.ds(rows, DOWN), :].astype(F32).reshape(chips, 8, CH)
    frames = [jnp.where(here == 0, mine, theirs), jnp.where(here == 0, theirs, mine)]
    frames_out[...] = jnp.concatenate(frames, axis=1).astype(BF16)


def sum_body(blocks, frames, sent_out, padded):
    rows = blocks.shape[1]
    total = blocks[0].astype(F32)
    for block in range(1, blocks.shape[0]):
        total = total + blocks[block].astype(F32)
    padded[...] = jnp.zeros_like(padded)
    padded[pl.ds(0, rows), :] = total
    chips = frames.shape[0]
    share = padded.shape[0] // chips
    for chip in range(chips):
        sent_out[chip, pl.ds(0, share), :] = padded[pl.ds(chip * share, share), :].astype(BF16)
        sent_out[chip, pl.ds(share, 16), :] = frames[chip]


def piece_body(received, piece_out):
    share = piece_out.shape[1]
    total = received[0, pl.ds(0, share), :].astype(F32)
    for chip in range(1, received.shape[0]):
        total = total + received[chip, pl.ds(0, share), :].astype(F32)
    piece = total.astype(BF16)
    for chip in range(piece_out.shape[0]):
        piece_out[chip] = piece


def spread_body(pieces, part_out):
    flat = pieces[...].reshape(-1, CH).astype(F32)
    part = flat[: part_out.shape[1]].astype(BF16)
    for block in range(part_out.shape[0]):
        part_out[block] = part


def results_body(core, mine, other, *rest):
    outs, whole = rest[:-1], rest[-1]
    here = core[0]
    half = mine.shape[0]
    whole[pl.ds(pl.multiple_of(here * half, 16), half), :] = mine[...]
    whole[pl.ds(pl.multiple_of((1 - here) * half, 16), half), :] = other[...]
    first = 0
    for out in outs:
        rows, lanes = out.shape
        for part in range(lanes // CH):
            out[:, pl.ds(part * CH, CH)] = whole[pl.ds(first, rows), :]
            first += rows


def output_body(received, last_time, output, spread, padded):
    frames = received[:, pl.ds(received.shape[1] - 16, 16), :]
    spread[...] = frames.astype(F32).reshape(HALF * 8, CH)
    padded[pl.ds(0, 8), :] = jnp.zeros((8, WIDE), F32)
    for half in range(2):
        padded[pl.ds(8, DOWN), pl.ds(half * CH, CH)] = spread[pl.ds(half, DOWN, stride=2), :]
    total = padded[pl.ds(8, DOWN), :]
    for k in range(3):
        taps = padded[pl.ds(4 * k, DOWN), :].astype(BF16)
        total = total + dot(taps, last_time[k])
    output[...] = total.astype(BF16)


def from_behind(block, distance):
    devices = range(lax.axis_size("seq"))
    route = [(i - distance, i) for i in devices if i - distance in devices]
    return lax.ppermute(block, "seq", route)


def swap_cores(block):
    count = lax.axis_size("seq")
    return lax.ppermute(block, "seq", [(i, i ^ 1) for i in range(count)])


def exchange_clip(blocks):
    return lax.all_to_all(blocks, "clip", split_axis=0, concat_axis=0, tiled=True)


def exchange_chips(blocks):
    count = lax.axis_size("seq")
    groups = [list(range(core, count, 2)) for core in range(2)]
    return lax.all_to_all(
        blocks, "seq", split_axis=0, concat_axis=0, axis_index_groups=groups, tiled=True
    )


def local(clip_in, first_plane, first_time, down_plane, down_time, last_time, cotan_out):
    own = clip_in.reshape(4 * CELLS, CH)
    prior = from_behind(own, 1)
    flat_frames = (2, 2, CELLS, CH)
    core = (lax.axis_index("seq") % 2).astype(jnp.int32).reshape(1)
    mine, away = call(
        rows_body,
        [(S, core), (V, cotan_out[0].reshape(HALF, 8, CH)), (H, last_time)],
        [(P_, (HALF // 2, 16, CH), BF16), (V, (HALF // 2, 16, CH), BF16)],
        [
            ((3, WIDE, WIDE), BF16),
            ((HALF * 8, CH), F32),
            ((DOWN + 8, WIDE), F32),
            ((HALF * 8, CH), F32),
            ((HALF // 2, 2, 16, CH), F32),
        ],
        copies=1,
    )
    theirs = swap_cores(away)
    acts, pre_first, both = call(
        own_body,
        [(H, own), (H, first_plane)],
        [
            (P_, (4, 2, CELLS, CH), BF16),
            (P_, flat_frames, F32),
            (P_, (12 * CH, WIDE), BF16),
        ],
        [
            ((4 * CELLS, CH), BF16),
            ((3, 3, CH, CH), BF16),
            ((2 * CELLS, CH), F32),
            ((2 * CELLS, 12 * CH), BF16),
        ],
        copies=2,
    )
    (acts,) = call(
        prior_body,
        [(P_, prior), (P_, acts), (P_, both)],
        [(P_, (6, 2, CELLS, CH), BF16)],
        [((2 * CELLS, CH), F32), ((2 * CELLS, 12 * CH), BF16)],
    )
    times = (P_, (2, WIDE, WIDE), BF16)
    theirs, acts = lax.optimization_barrier((theirs, acts))
    (sent,) = call(
        join_body,
        [(S, core), (P_, mine), (P_, theirs)],
        [(V, (HALF // 2, HALF, CH), BF16)],
    )
    received = exchange_chips(sent).reshape(HALF, 16, CH)
    kept, strided, part, near_times = call(
        first_body,
        [
            (P_, acts), (H, first_time), (H, down_plane), (H, down_time),
        ],
        [
            (P_, (KEPT, CH), BF16),
            (P_, (2, DOWN, WIDE), BF16),
            (P_, (DOWN, WIDE), F32),
            times,
        ],
        [
            ((3, CH, CH), BF16),
            ((3, 3, CH, WIDE), BF16),
            ((3, WIDE, WIDE), BF16),
        ],
        copies=3,
    )
    strided_prior = from_behind(strided, 1)
    down = (P_, (DOWN, WIDE), BF16)
    grad_lowered, cot = call(
        cotan_body, [(P_, received)], [down, down], [((HALF * 16, CH), F32)]
    )
    lowered, sent = call(
        middle_body,
        [(P_, strided_prior), (P_, part), (P_, near_times), (P_, grad_lowered), (P_, cot)],
        [down, (P_, (2 * DOWN, WIDE), BF16)],
    )
    ahead = from_behind(sent, -1)
    further = from_behind(sent, -2)
    all_times, kernels, time_grads, windows, slope = call(
        time_grads_body,
        [
            (P_, sent), (P_, lowered), (P_, strided_prior), (P_, kept), (P_, acts),
            (P_, pre_first), (H, down_time), (H, down_plane),
        ],
        [
            (P_, (3, WIDE, WIDE), BF16),
            (P_, (4 * CH, 4 * WIDE), BF16),
            (P_, (PART_AT + 2 * DOWN, CH), F32),
            (P_, (2 * CELLS, 12 * CH), BF16),
            (P_, flat_frames, F32),
        ],
        [((3, 3, CH, WIDE), BF16)],
        copies=2,
    )
    half_rows = GRADS // 2
    mine, other = call(
        back_body,
        [
            (S, core), (P_, ahead), (P_, further), (P_, time_grads), (P_, all_times),
            (P_, kernels), (P_, kept), (P_, acts), (P_, windows), (P_, slope), (P_, lowered),
            (H, first_time),
        ],
        [(P_, (half_rows + DOWN, CH), F32), (P_, (half_rows + DOWN, CH), BF16)],
        [
            ((4 * DOWN, 4 * WIDE), BF16),
            ((8 * CELLS, CH), BF16),
            ((GRADS, CH), F32),
            ((HALF // 2, 2, 8, CH), F32),
            ((3, CH, CH), BF16),
        ],
        copies=1,
        flops=600000000,
        size=2000000,
    )

    clips = lax.axis_size("clip")
    chips = lax.axis_size("seq") // 2
    part_rows = half_rows // clips
    other = swap_cores(other)
    half, frames = call(
        halves_body,
        [(S, core), (P_, mine), (V, other)],
        [(P_, (half_rows, CH), BF16), (V, (chips, 16, CH), BF16)],
    )
    blocks = exchange_clip(half.reshape(clips, part_rows, CH))
    share = 16 * (-(-part_rows // (16 * chips)))
    (sent,) = call(
        sum_body,
        [(V, blocks), (V, frames)],
        [(V, (chips, share + 16, CH), BF16)],
        [((chips * share, CH), F32)],
    )
    received = exchange_chips(sent)
    (pieces,) = call(piece_body, [(V, received)], [(V, (chips, share, CH), BF16)])
    pieces = exchange_chips(pieces)
    (output,) = call(
        output_body,
        [(V, received), (V, last_time)],
        [(V, (DOWN, WIDE), BF16)],
        [((HALF * 8, CH), F32), ((DOWN + 8, WIDE), F32)],
    )
    (parts,) = call(spread_body, [(V, pieces)], [(V, (clips, part_rows, CH), BF16)])
    half = exchange_clip(parts).reshape(half_rows, CH)
    other = swap_cores(half)
    grads = call(
        results_body,
        [(S, core), (V, half), (V, other)],
        [
            (V, (9 * CH, CH), BF16),
            (V, (3 * CH, CH), BF16),
            (V, (9 * CH, WIDE), BF16),
            (V, (3 * WIDE, WIDE), BF16),
            (V, (3 * WIDE, WIDE), BF16),
        ],
        [((GRADS, CH), BF16)],
    )
    shapes = ((3, 3, CH, CH), (3, CH, CH), (3, 3, CH, WIDE), (3, WIDE, WIDE), (3, WIDE, WIDE))
    grads = [grad.reshape(shape) for grad, shape in zip(grads, shapes)]
    return (output.reshape(1, HALF, 1, 4, WIDE), *grads)


def solution(mesh):
    placed = (
        P("clip", "seq", None, None, None),
        P(),
        P(),
        P(),
        P(),
        P(),
        P("clip", None, "seq", None, None),
    )
    return jax.shard_map(
        local,
        mesh=mesh,
        in_specs=placed,
        out_specs=(P("clip", None, "seq", None, None), P(), P(), P(), P(), P()),
        check_vma=False,
    )
```

```python
import jax
import jax.numpy as jnp
from jax import lax
from jax.experimental import pallas as pl
from jax.experimental.pallas import tpu as pltpu
from jax.sharding import PartitionSpec as P


F32 = jnp.float32
BF16 = jnp.bfloat16
COLS = 8
HALF = 32
CELLS = COLS * HALF
DOWN = CELLS // 2
CH = 128
WIDE = 256
STRIDED_AT = 9 * 2 * DOWN
KEPT = STRIDED_AT + 2 * DOWN
LOWERED_AT = 8 * WIDE
PART_AT = LOWERED_AT + 2 * DOWN
GRADS = (9 + 3 + 18 + 12 + 12) * CH


def dot(left, right):
    return lax.dot_general(left, right, (((1,), (0,)), ((), ())), preferred_element_type=F32)


def dot_nt(left, right):
    return lax.dot_general(left, right, (((1,), (1,)), ((), ())), preferred_element_type=F32)


def dot_tn(left, right):
    return lax.dot_general(left, right, (((0,), (0,)), ((), ())), preferred_element_type=F32)


V, P_, H, S = "vmem", "pinned", "hbm", "smem"
SPACES = {V: pltpu.VMEM, P_: pltpu.VMEM, H: pltpu.HBM, S: pltpu.SMEM}


def placed_input(space, array):
    if space in (P_, H):
        return pltpu.with_memory_space_constraint(array, SPACES[space])
    return array


def placed_output(space, shape, kind):
    if space in (P_, H):
        return SPACES[space](shape, kind)
    return jax.ShapeDtypeStruct(shape, kind)


def call(body, ins, outs, scratch=(), copies=0, flops=1000, size=8000000):
    scratch = [pltpu.VMEM(shape, kind) for shape, kind in scratch]
    if copies:
        scratch.append(pltpu.SemaphoreType.DMA((copies,)))
    return pl.pallas_call(
        body,
        out_shape=[placed_output(*out) for out in outs],
        in_specs=[pl.BlockSpec(memory_space=SPACES[space]) for space, _ in ins],
        out_specs=[pl.BlockSpec(memory_space=SPACES[space]) for space, _, _ in outs],
        scratch_shapes=scratch,
        compiler_params=pltpu.CompilerParams(vmem_limit_bytes=24 * 1024 * 1024),
        cost_estimate=pl.CostEstimate(flops=flops, bytes_accessed=size, transcendentals=0),
    )(*[placed_input(*given) for given in ins])


def start(sems, *pairs):
    copies = [
        pltpu.make_async_copy(source, target, sems.at[at]) for at, source, target in pairs
    ]
    for copy in copies:
        copy.start()
    return copies


def row_before(planes):
    wide = planes.astype(F32)
    rolled = pltpu.roll(wide, 1, 1)
    at = lax.broadcasted_iota(jnp.int32, wide.shape, 1)
    return jnp.where(at == 0, 0.0, rolled).astype(BF16)


def row_after(planes):
    wide = planes.astype(F32)
    rolled = pltpu.roll(wide, HALF - 1, 1)
    at = lax.broadcasted_iota(jnp.int32, wide.shape, 1)
    return jnp.where(at == HALF - 1, 0.0, rolled).astype(BF16)


def fill_windows(windows, at, even, odd):
    by_row = (row_before(odd), even, odd, row_after(even))
    edge = jnp.zeros((HALF, CH), BF16)
    for row, planes in enumerate(by_row):
        flat = planes.reshape(CELLS, CH)
        for tap in range(3):
            lanes = pl.ds((tap * 4 + row) * CH, CH)
            if tap == 0:
                windows[pl.ds(at, HALF), lanes] = edge
                windows[pl.ds(at + HALF, CELLS - HALF), lanes] = flat[: CELLS - HALF]
            elif tap == 1:
                windows[pl.ds(at, CELLS), lanes] = flat
            else:
                windows[pl.ds(at, CELLS - HALF), lanes] = flat[HALF:]
                windows[pl.ds(at + CELLS - HALF, HALF), lanes] = edge


def silu_slope(preact):
    sigma = jax.nn.sigmoid(preact)
    return sigma * (1.0 + preact * (1.0 - sigma))


def parity_planes(source, frame, spread):
    spread[...] = source[pl.ds(frame * 2 * CELLS, 2 * CELLS), :].astype(F32)
    planes = []
    for par in range(2):
        cols = [spread[pl.ds(par * COLS + col, HALF, stride=2 * COLS), :] for col in range(COLS)]
        planes.append(jnp.stack(cols, axis=0).astype(BF16))
    return planes


def cells_of(kept):
    return jnp.concatenate([kept[pl.ds(tap * 2 * DOWN, 2 * DOWN), :] for tap in range(9)], axis=1)


def prior_body(prior, own_acts, both, acts_out, spread, windows):
    for frame in range(2):
        fill_windows(windows, frame * CELLS, *parity_planes(prior, frame, spread))
    acts_out[pl.ds(2, 4)] = own_acts[...]
    for frame in range(2):
        pre = dot(windows[pl.ds(frame * CELLS, CELLS), :], both[...])
        hid = (pre * jax.nn.sigmoid(pre)).astype(BF16)
        for par in range(2):
            acts_out[frame, par] = hid[:, par * CH : (par + 1) * CH]


def first_body(
    acts, time_far, plane_far, down_far,
    kept_out, strided_out, part_out, times_out,
    first_time, down_plane, down_time, sems,
):
    loads = start(
        sems, (0, time_far, first_time), (1, plane_far, down_plane), (2, down_far, down_time)
    )
    loads[0].wait()
    times = first_time[...].reshape(3 * CH, CH)
    for frame in range(2):
        mixed = []
        for par in range(2):
            taps = jnp.concatenate([acts[frame + k, par] for k in range(3)], axis=1)
            here = acts[4 + frame, par].astype(F32) + dot(taps, times)
            mixed.append(here.astype(BF16).reshape(COLS, HALF, CH))
        by_row = (row_before(mixed[1]), mixed[0], mixed[1])
        for row in range(3):
            for tap in range(3):
                at = (row * 3 + tap) * 2 * DOWN + frame * DOWN
                for col in range(COLS // 2):
                    rows = pl.ds(at + col * HALF, HALF)
                    where = 2 * col + tap - 1
                    if where < 0:
                        kept_out[rows, :] = jnp.zeros((HALF, CH), BF16)
                    else:
                        kept_out[rows, :] = by_row[row][where]
    loads[1].wait()
    kernel = down_plane[...].reshape(9 * CH, WIDE)
    strided = dot(cells_of(kept_out), kernel).astype(BF16).reshape(2, DOWN, WIDE)
    strided_out[...] = strided
    for half in range(2):
        kept_out[pl.ds(STRIDED_AT + half * DOWN, DOWN), :] = strided[
            0, :, half * CH : (half + 1) * CH
        ]
    loads[2].wait()
    part_out[...] = dot(strided[0], down_time[2])
    times_out[...] = down_time[pl.ds(0, 2)]


def rows_body(rows, last_far, sent_out, last_time, spread, padded, turned, sems):
    loads = start(sems, (0, last_far, last_time))
    cotan = rows[...].astype(F32)
    spread[...] = cotan.reshape(HALF * 8, CH)
    for half in range(2):
        padded[pl.ds(0, DOWN), pl.ds(half * CH, CH)] = spread[pl.ds(half, DOWN, stride=2), :]
    padded[pl.ds(DOWN, 8), :] = jnp.zeros((8, WIDE), F32)
    loads[0].wait()
    total = padded[pl.ds(0, DOWN), :]
    for k in range(3):
        taps = padded[pl.ds(4 * (2 - k), DOWN), :].astype(BF16)
        total = total + dot_nt(taps, last_time[k])
    for half in range(2):
        turned[pl.ds(half, DOWN, stride=2), :] = total[:, half * CH : (half + 1) * CH]
    both = jnp.concatenate([turned[...].reshape(HALF, 8, CH), cotan], axis=1)
    sent_out[...] = both.astype(BF16)


def own_body(
    own_far, plane_far,
    acts_out, pre_out, both_out,
    own, first_plane, cells, windows, sems,
):
    loads = start(sems, (0, own_far, own), (1, plane_far, first_plane))
    both_out[...] = jnp.zeros_like(both_out)
    loads[0].wait()
    for frame in range(2):
        planes = parity_planes(own, frame, cells)
        fill_windows(windows, frame * CELLS, *planes)
        for par in range(2):
            acts_out[2 + frame, par] = planes[par].reshape(CELLS, CH)
    loads[1].wait()
    for tap in range(3):
        for row in range(4):
            at = pl.ds((tap * 4 + row) * CH, CH)
            if row < 3:
                both_out[at, pl.ds(0, CH)] = first_plane[row, tap]
            if row > 0:
                both_out[at, pl.ds(CH, CH)] = first_plane[row - 1, tap]
    for frame in range(2):
        pre = dot(windows[pl.ds(frame * CELLS, CELLS), :], both_out[...])
        hid = (pre * jax.nn.sigmoid(pre)).astype(BF16)
        for par in range(2):
            acts_out[frame, par] = hid[:, par * CH : (par + 1) * CH]
            pre_out[frame, par] = pre[:, par * CH : (par + 1) * CH]


def cotan_body(
    received,
    grad_lowered_out, cot_out,
    spread,
):
    spread[...] = received[...].astype(F32).reshape(HALF * 16, CH)
    for at, out in ((0, grad_lowered_out), (8, cot_out)):
        parts = []
        for col in range(4):
            halves = [
                spread[pl.ds(at + col * 2 + half, HALF, stride=16), :] for half in range(2)
            ]
            parts.append(jnp.concatenate(halves, axis=1))
        out[...] = jnp.concatenate(parts, axis=0).astype(BF16)


def middle_body(prior, part, times, grad_lowered, cot, lowered_out, sent_out):
    pre = dot(prior[0], times[0]) + dot(prior[1], times[1]) + part[...]
    lowered_out[...] = (pre * jax.nn.sigmoid(pre)).astype(BF16)
    sent_out[pl.ds(0, DOWN), :] = (grad_lowered[...].astype(F32) * silu_slope(pre)).astype(BF16)
    sent_out[pl.ds(DOWN, DOWN), :] = cot[...]


BACK = (
    (0, 0, 0, 0, 1, 1),
    (0, 1, 0, 1, 1, 0),
    (0, 1, 0, 0, 1, 2),
    (1, 0, 1, 0, 0, 1),
    (1, 0, 0, 0, 2, 1),
    (1, 1, 1, 1, 0, 0),
    (1, 1, 1, 0, 0, 2),
    (1, 1, 0, 1, 2, 0),
    (1, 1, 0, 0, 2, 2),
)


def time_grads_body(
    sent, lowered, prior, kept, acts, pre, down_far, plane_far,
    times_out, kernels_out, grads_out, windows_out, slope_out,
    down_plane, sems,
):
    loads = start(sems, (0, down_far, times_out), (1, plane_far, down_plane))
    kernels_out[...] = jnp.zeros_like(kernels_out)
    for frame in range(2):
        planes = [acts[4 + frame, par].reshape(COLS, HALF, CH) for par in range(2)]
        fill_windows(windows_out, frame * CELLS, *planes)
    slope_out[...] = silu_slope(pre[...])
    wide = lowered[...].astype(F32)
    for col in range(4):
        for half in range(2):
            grads_out[pl.ds(LOWERED_AT + col * 2 + half, HALF, stride=8), :] = wide[
                col * HALF : (col + 1) * HALF, half * CH : (half + 1) * CH
            ]
    own = [kept[pl.ds(STRIDED_AT + half * DOWN, DOWN), :] for half in range(2)]
    taps = (prior[0], prior[1], jnp.concatenate(own, axis=1))
    grad_pre = sent[pl.ds(0, DOWN), :]
    for k in range(3):
        down = dot_tn(taps[k], grad_pre)
        for half in range(2):
            lanes = slice(half * CH, (half + 1) * CH)
            grads_out[pl.ds((half * 3 + k) * WIDE, WIDE), :] = down[:, lanes]
    last = dot_tn(lowered[...], sent[pl.ds(DOWN, DOWN), :])
    for half in range(2):
        grads_out[pl.ds((6 + half) * WIDE, WIDE), :] = last[:, half * CH : (half + 1) * CH]
    for load in loads:
        load.wait()
    part = dot_nt(grad_pre, times_out[2])
    for half in range(2):
        grads_out[pl.ds(PART_AT + half * DOWN, DOWN), :] = part[:, half * CH : (half + 1) * CH]
    for row_par, col_par, row_off, col_off, row, tap in BACK:
        rows = pl.ds((row_par * 2 + col_par) * CH, CH)
        lanes = pl.ds((row_off * 2 + col_off) * WIDE, WIDE)
        kernels_out[rows, lanes] = down_plane[row, tap]


def back_body(
    core, ahead, further, grads, times, kernels, kept, acts, windows, slope, lowered, time_far,
    mine_out, other_out,
    shifted, mixed, flat, rows_here, first_time, sems,
):
    loads = start(sems, (0, time_far, first_time))
    near, far = ahead[pl.ds(0, DOWN), :], further[pl.ds(0, DOWN), :]
    part = [grads[pl.ds(PART_AT + half * DOWN, DOWN), :] for half in range(2)]
    strided = [
        jnp.concatenate(part, axis=1) + dot_nt(near, times[0]),
        dot_nt(near, times[1]),
        dot_nt(near, times[2]) + dot_nt(far, times[0]),
        dot_nt(far, times[1]),
    ]
    strided = [frame.astype(BF16) for frame in strided]
    for frame in range(4):
        planes = strided[frame].reshape(4, HALF, WIDE)
        for row_off, rows in ((0, planes), (1, row_after(planes))):
            cells = rows.reshape(DOWN, WIDE)
            here = pl.ds((row_off * 2) * WIDE, WIDE)
            after = pl.ds((row_off * 2 + 1) * WIDE, WIDE)
            shifted[pl.ds(frame * DOWN, DOWN), here] = cells
            shifted[pl.ds(frame * DOWN, DOWN - HALF), after] = cells[HALF:]
            shifted[pl.ds(frame * DOWN + DOWN - HALF, HALF), after] = jnp.zeros((HALF, WIDE), BF16)
    product = dot_nt(shifted[...], kernels[...]).astype(BF16)
    for frame in range(4):
        for par in range(2):
            for col_par in range(2):
                lanes = slice((par * 2 + col_par) * CH, (par * 2 + col_par + 1) * CH)
                for col in range(4):
                    rows = slice(frame * DOWN + col * HALF, frame * DOWN + (col + 1) * HALF)
                    plane = (frame * 2 + par) * COLS + 2 * col + col_par
                    mixed[pl.ds(plane * HALF, HALF), :] = product[rows, lanes]

    loads[0].wait()
    taps = jnp.concatenate([first_time[k] for k in range(3)], axis=1)
    cotans = []
    for frame in range(2):
        parts = []
        for par in range(2):
            frames = [
                mixed[pl.ds(((frame + 2 - k) * 2 + par) * CELLS, CELLS), :] for k in range(3)
            ]
            grad_hidden = dot_nt(jnp.concatenate(frames, axis=1), taps)
            parts.append((grad_hidden * slope[frame, par]).astype(BF16))
        cotans.append(jnp.concatenate(parts, axis=1))
    product = dot_tn(windows[...], jnp.concatenate(cotans, axis=0))
    for row in range(3):
        for tap in range(3):
            at = (tap * 4 + row) * CH
            flat[pl.ds((row * 3 + tap) * CH, CH), :] = (
                product[at : at + CH, :CH] + product[at + CH : at + 2 * CH, CH:]
            )
    cotan = mixed[pl.ds(0, 4 * CELLS), :]
    for k in range(3):
        flat[pl.ds((9 + k) * CH, CH), :] = dot_tn(acts[pl.ds(k, 2)].reshape(4 * CELLS, CH), cotan)
    down = dot_tn(cells_of(kept), jnp.concatenate(strided[:2], axis=0))
    last = [dot_tn(lowered[...], sent[pl.ds(DOWN, DOWN), :]) for sent in (further, ahead)]
    flat[pl.ds(30 * CH, 12 * CH), :] = grads[pl.ds(0, 12 * CH), :]
    for half in range(2):
        lanes = slice(half * CH, (half + 1) * CH)
        flat[pl.ds((12 + half * 9) * CH, 9 * CH), :] = down[:, lanes]
        base = (42 + half * 6) * CH
        for k in range(2):
            flat[pl.ds(base + k * WIDE, WIDE), :] = last[k][:, lanes]
        flat[pl.ds(base + 2 * WIDE, WIDE), :] = grads[pl.ds((6 + half) * WIDE, WIDE), :]

    here = core[0]
    half = GRADS // 2
    mine_out[pl.ds(0, half), :] = flat[pl.ds(pl.multiple_of(here * half, 16), half), :]
    other_out[pl.ds(0, half), :] = flat[
        pl.ds(pl.multiple_of((1 - here) * half, 16), half), :
    ].astype(BF16)
    rows_here[...] = grads[pl.ds(LOWERED_AT, 2 * DOWN), :].reshape(HALF // 2, 2, 8, CH)
    mine_out[pl.ds(half, DOWN), :] = rows_here[:, pl.ds(here, 1)].reshape(DOWN, CH)
    away = rows_here[:, pl.ds(1 - here, 1)].reshape(DOWN, CH)
    other_out[pl.ds(half, DOWN), :] = away.astype(BF16)


def halves_body(core, own, other, half_out, frames_out):
    rows = half_out.shape[0]
    half_out[...] = (own[pl.ds(0, rows), :] + other[pl.ds(0, rows), :].astype(F32)).astype(BF16)
    here = core[0]
    chips = HALF // 2
    mine = own[pl.ds(rows, DOWN), :].reshape(chips, 8, CH)
    theirs = other[pl.ds(rows, DOWN), :].astype(F32).reshape(chips, 8, CH)
    frames = [jnp.where(here == 0, mine, theirs), jnp.where(here == 0, theirs, mine)]
    frames_out[...] = jnp.concatenate(frames, axis=1).astype(BF16)


def sum_body(blocks, frames, sent_out, padded):
    rows = blocks.shape[1]
    total = blocks[0].astype(F32)
    for block in range(1, blocks.shape[0]):
        total = total + blocks[block].astype(F32)
    padded[...] = jnp.zeros_like(padded)
    padded[pl.ds(0, rows), :] = total
    chips = frames.shape[0]
    share = padded.shape[0] // chips
    for chip in range(chips):
        sent_out[chip, pl.ds(0, share), :] = padded[pl.ds(chip * share, share), :].astype(BF16)
        sent_out[chip, pl.ds(share, 16), :] = frames[chip]


def piece_body(received, piece_out):
    share = piece_out.shape[1]
    total = received[0, pl.ds(0, share), :].astype(F32)
    for chip in range(1, received.shape[0]):
        total = total + received[chip, pl.ds(0, share), :].astype(F32)
    piece = total.astype(BF16)
    for chip in range(piece_out.shape[0]):
        piece_out[chip] = piece


def spread_body(pieces, part_out):
    flat = pieces[...].reshape(-1, CH).astype(F32)
    part = flat[: part_out.shape[1]].astype(BF16)
    for block in range(part_out.shape[0]):
        part_out[block] = part


def results_body(core, mine, other, *rest):
    outs, whole = rest[:-1], rest[-1]
    here = core[0]
    half = mine.shape[0]
    whole[pl.ds(pl.multiple_of(here * half, 16), half), :] = mine[...]
    whole[pl.ds(pl.multiple_of((1 - here) * half, 16), half), :] = other[...]
    first = 0
    for out in outs:
        rows, lanes = out.shape
        for part in range(lanes // CH):
            out[:, pl.ds(part * CH, CH)] = whole[pl.ds(first, rows), :]
            first += rows


def output_body(received, last_time, output, spread, padded):
    frames = received[:, pl.ds(received.shape[1] - 16, 16), :]
    spread[...] = frames.astype(F32).reshape(HALF * 8, CH)
    padded[pl.ds(0, 8), :] = jnp.zeros((8, WIDE), F32)
    for half in range(2):
        padded[pl.ds(8, DOWN), pl.ds(half * CH, CH)] = spread[pl.ds(half, DOWN, stride=2), :]
    total = padded[pl.ds(8, DOWN), :]
    for k in range(3):
        taps = padded[pl.ds(4 * k, DOWN), :].astype(BF16)
        total = total + dot(taps, last_time[k])
    output[...] = total.astype(BF16)


def from_behind(block, distance):
    devices = range(lax.axis_size("seq"))
    route = [(i - distance, i) for i in devices if i - distance in devices]
    return lax.ppermute(block, "seq", route)


def swap_cores(block):
    count = lax.axis_size("seq")
    return lax.ppermute(block, "seq", [(i, i ^ 1) for i in range(count)])


def exchange_clip(blocks):
    count = lax.axis_size("clip")
    side = round(count**0.5)
    rows = [list(range(first, first + side)) for first in range(0, count, side)]
    path = [clip for at, row in enumerate(rows) for clip in (row if at % 2 == 0 else row[::-1])]
    return lax.all_to_all(
        blocks, "clip", split_axis=0, concat_axis=0, axis_index_groups=[path], tiled=True
    )


def exchange_seq(blocks):
    return lax.all_to_all(blocks, "seq", split_axis=0, concat_axis=0, tiled=True)


def exchange_chips(blocks):
    count = lax.axis_size("seq")
    groups = [list(range(core, count, 2)) for core in range(2)]
    return lax.all_to_all(
        blocks, "seq", split_axis=0, concat_axis=0, axis_index_groups=groups, tiled=True
    )


def local(clip_in, first_plane, first_time, down_plane, down_time, last_time, cotan_out):
    own = clip_in.reshape(4 * CELLS, CH)
    prior = from_behind(own, 1)
    flat_frames = (2, 2, CELLS, CH)
    core = (lax.axis_index("seq") % 2).astype(jnp.int32).reshape(1)
    (sent,) = call(
        rows_body,
        [(V, cotan_out[0].reshape(HALF, 8, CH)), (H, last_time)],
        [(V, (HALF, 16, CH), BF16)],
        [
            ((3, WIDE, WIDE), BF16),
            ((HALF * 8, CH), F32),
            ((DOWN + 8, WIDE), F32),
            ((HALF * 8, CH), F32),
        ],
        copies=1,
    )
    acts, pre_first, both = call(
        own_body,
        [(H, own), (H, first_plane)],
        [
            (P_, (4, 2, CELLS, CH), BF16),
            (P_, flat_frames, F32),
            (P_, (12 * CH, WIDE), BF16),
        ],
        [
            ((4 * CELLS, CH), BF16),
            ((3, 3, CH, CH), BF16),
            ((2 * CELLS, CH), F32),
            ((2 * CELLS, 12 * CH), BF16),
        ],
        copies=2,
    )
    (acts,) = call(
        prior_body,
        [(P_, prior), (P_, acts), (P_, both)],
        [(P_, (6, 2, CELLS, CH), BF16)],
        [((2 * CELLS, CH), F32), ((2 * CELLS, 12 * CH), BF16)],
    )
    times = (P_, (2, WIDE, WIDE), BF16)
    sent, acts = lax.optimization_barrier((sent, acts))
    received = exchange_seq(sent)
    kept, strided, part, near_times = call(
        first_body,
        [
            (P_, acts), (H, first_time), (H, down_plane), (H, down_time),
        ],
        [
            (P_, (KEPT, CH), BF16),
            (P_, (2, DOWN, WIDE), BF16),
            (P_, (DOWN, WIDE), F32),
            times,
        ],
        [
            ((3, CH, CH), BF16),
            ((3, 3, CH, WIDE), BF16),
            ((3, WIDE, WIDE), BF16),
        ],
        copies=3,
    )
    strided_prior = from_behind(strided, 1)
    down = (P_, (DOWN, WIDE), BF16)
    grad_lowered, cot = call(
        cotan_body, [(P_, received)], [down, down], [((HALF * 16, CH), F32)]
    )
    lowered, sent = call(
        middle_body,
        [(P_, strided_prior), (P_, part), (P_, near_times), (P_, grad_lowered), (P_, cot)],
        [down, (P_, (2 * DOWN, WIDE), BF16)],
    )
    ahead = from_behind(sent, -1)
    further = from_behind(sent, -2)
    all_times, kernels, time_grads, windows, slope = call(
        time_grads_body,
        [
            (P_, sent), (P_, lowered), (P_, strided_prior), (P_, kept), (P_, acts),
            (P_, pre_first), (H, down_time), (H, down_plane),
        ],
        [
            (P_, (3, WIDE, WIDE), BF16),
            (P_, (4 * CH, 4 * WIDE), BF16),
            (P_, (PART_AT + 2 * DOWN, CH), F32),
            (P_, (2 * CELLS, 12 * CH), BF16),
            (P_, flat_frames, F32),
        ],
        [((3, 3, CH, WIDE), BF16)],
        copies=2,
    )
    half_rows = GRADS // 2
    mine, other = call(
        back_body,
        [
            (S, core), (P_, ahead), (P_, further), (P_, time_grads), (P_, all_times),
            (P_, kernels), (P_, kept), (P_, acts), (P_, windows), (P_, slope), (P_, lowered),
            (H, first_time),
        ],
        [(P_, (half_rows + DOWN, CH), F32), (P_, (half_rows + DOWN, CH), BF16)],
        [
            ((4 * DOWN, 4 * WIDE), BF16),
            ((8 * CELLS, CH), BF16),
            ((GRADS, CH), F32),
            ((HALF // 2, 2, 8, CH), F32),
            ((3, CH, CH), BF16),
        ],
        copies=1,
        flops=600000000,
        size=2000000,
    )

    clips = lax.axis_size("clip")
    chips = lax.axis_size("seq") // 2
    part_rows = half_rows // clips
    other = swap_cores(other)
    half, frames = call(
        halves_body,
        [(S, core), (P_, mine), (V, other)],
        [(P_, (half_rows, CH), BF16), (V, (chips, 16, CH), BF16)],
    )
    blocks = exchange_clip(half.reshape(clips, part_rows, CH))
    share = 16 * (-(-part_rows // (16 * chips)))
    (sent,) = call(
        sum_body,
        [(V, blocks), (V, frames)],
        [(V, (chips, share + 16, CH), BF16)],
        [((chips * share, CH), F32)],
    )
    received = exchange_chips(sent)
    (pieces,) = call(piece_body, [(V, received)], [(V, (chips, share, CH), BF16)])
    pieces = exchange_chips(pieces)
    (output,) = call(
        output_body,
        [(V, received), (V, last_time)],
        [(V, (DOWN, WIDE), BF16)],
        [((HALF * 8, CH), F32), ((DOWN + 8, WIDE), F32)],
    )
    (parts,) = call(spread_body, [(V, pieces)], [(V, (clips, part_rows, CH), BF16)])
    half = exchange_clip(parts).reshape(half_rows, CH)
    other = swap_cores(half)
    grads = call(
        results_body,
        [(S, core), (V, half), (V, other)],
        [
            (V, (9 * CH, CH), BF16),
            (V, (3 * CH, CH), BF16),
            (V, (9 * CH, WIDE), BF16),
            (V, (3 * WIDE, WIDE), BF16),
            (V, (3 * WIDE, WIDE), BF16),
        ],
        [((GRADS, CH), BF16)],
    )
    shapes = ((3, 3, CH, CH), (3, CH, CH), (3, 3, CH, WIDE), (3, WIDE, WIDE), (3, WIDE, WIDE))
    grads = [grad.reshape(shape) for grad, shape in zip(grads, shapes)]
    return (output.reshape(1, HALF, 1, 4, WIDE), *grads)


def solution(mesh):
    placed = (
        P("clip", "seq", None, None, None),
        P(),
        P(),
        P(),
        P(),
        P(),
        P("clip", None, "seq", None, None),
    )
    return jax.shard_map(
        local,
        mesh=mesh,
        in_specs=placed,
        out_specs=(P("clip", None, "seq", None, None), P(), P(), P(), P(), P()),
        check_vma=False,
    )
```

```python
import jax
import jax.numpy as jnp
from jax import lax
from jax.experimental import pallas as pl
from jax.experimental.pallas import tpu as pltpu
from jax.sharding import PartitionSpec as P


F32 = jnp.float32
BF16 = jnp.bfloat16
COLS = 8
HALF = 32
CELLS = COLS * HALF
DOWN = CELLS // 2
CH = 128
WIDE = 256
STRIDED_AT = 9 * 2 * DOWN
KEPT = STRIDED_AT + 2 * DOWN
LOWERED_AT = 8 * WIDE
PART_AT = LOWERED_AT + 2 * DOWN
GRADS = (9 + 3 + 18 + 12 + 12) * CH


def dot(left, right):
    return lax.dot_general(left, right, (((1,), (0,)), ((), ())), preferred_element_type=F32)


def dot_nt(left, right):
    return lax.dot_general(left, right, (((1,), (1,)), ((), ())), preferred_element_type=F32)


def dot_tn(left, right):
    return lax.dot_general(left, right, (((0,), (0,)), ((), ())), preferred_element_type=F32)


V, P_, H, S = "vmem", "pinned", "hbm", "smem"
SPACES = {V: pltpu.VMEM, P_: pltpu.VMEM, H: pltpu.HBM, S: pltpu.SMEM}


def placed_input(space, array):
    if space in (P_, H):
        return pltpu.with_memory_space_constraint(array, SPACES[space])
    return array


def placed_output(space, shape, kind):
    if space in (P_, H):
        return SPACES[space](shape, kind)
    return jax.ShapeDtypeStruct(shape, kind)


def call(body, ins, outs, scratch=(), copies=0, flops=1000, size=8000000):
    scratch = [pltpu.VMEM(shape, kind) for shape, kind in scratch]
    if copies:
        scratch.append(pltpu.SemaphoreType.DMA((copies,)))
    return pl.pallas_call(
        body,
        out_shape=[placed_output(*out) for out in outs],
        in_specs=[pl.BlockSpec(memory_space=SPACES[space]) for space, _ in ins],
        out_specs=[pl.BlockSpec(memory_space=SPACES[space]) for space, _, _ in outs],
        scratch_shapes=scratch,
        compiler_params=pltpu.CompilerParams(vmem_limit_bytes=24 * 1024 * 1024),
        cost_estimate=pl.CostEstimate(flops=flops, bytes_accessed=size, transcendentals=0),
    )(*[placed_input(*given) for given in ins])


def start(sems, *pairs):
    copies = [
        pltpu.make_async_copy(source, target, sems.at[at]) for at, source, target in pairs
    ]
    for copy in copies:
        copy.start()
    return copies


def row_before(planes):
    wide = planes.astype(F32)
    rolled = pltpu.roll(wide, 1, 1)
    at = lax.broadcasted_iota(jnp.int32, wide.shape, 1)
    return jnp.where(at == 0, 0.0, rolled).astype(BF16)


def row_after(planes):
    wide = planes.astype(F32)
    rolled = pltpu.roll(wide, HALF - 1, 1)
    at = lax.broadcasted_iota(jnp.int32, wide.shape, 1)
    return jnp.where(at == HALF - 1, 0.0, rolled).astype(BF16)


def fill_windows(windows, at, even, odd):
    by_row = (row_before(odd), even, odd, row_after(even))
    edge = jnp.zeros((HALF, CH), BF16)
    for row, planes in enumerate(by_row):
        flat = planes.reshape(CELLS, CH)
        for tap in range(3):
            lanes = pl.ds((tap * 4 + row) * CH, CH)
            if tap == 0:
                windows[pl.ds(at, HALF), lanes] = edge
                windows[pl.ds(at + HALF, CELLS - HALF), lanes] = flat[: CELLS - HALF]
            elif tap == 1:
                windows[pl.ds(at, CELLS), lanes] = flat
            else:
                windows[pl.ds(at, CELLS - HALF), lanes] = flat[HALF:]
                windows[pl.ds(at + CELLS - HALF, HALF), lanes] = edge


def silu_slope(preact):
    sigma = jax.nn.sigmoid(preact)
    return sigma * (1.0 + preact * (1.0 - sigma))


def parity_planes(source, frame, spread):
    spread[...] = source[pl.ds(frame * 2 * CELLS, 2 * CELLS), :].astype(F32)
    planes = []
    for par in range(2):
        cols = [spread[pl.ds(par * COLS + col, HALF, stride=2 * COLS), :] for col in range(COLS)]
        planes.append(jnp.stack(cols, axis=0).astype(BF16))
    return planes


def cells_of(kept):
    return jnp.concatenate([kept[pl.ds(tap * 2 * DOWN, 2 * DOWN), :] for tap in range(9)], axis=1)


def prior_body(prior, own_acts, both, acts_out, spread, windows):
    for frame in range(2):
        fill_windows(windows, frame * CELLS, *parity_planes(prior, frame, spread))
    acts_out[pl.ds(2, 4)] = own_acts[...]
    for frame in range(2):
        pre = dot(windows[pl.ds(frame * CELLS, CELLS), :], both[...])
        hid = (pre * jax.nn.sigmoid(pre)).astype(BF16)
        for par in range(2):
            acts_out[frame, par] = hid[:, par * CH : (par + 1) * CH]


def first_body(
    acts, time_far, plane_far, down_far,
    kept_out, strided_out, times_out,
    first_time, down_plane, down_time, sems,
):
    loads = start(
        sems, (0, time_far, first_time), (1, plane_far, down_plane), (2, down_far, down_time)
    )
    loads[0].wait()
    times = first_time[...].reshape(3 * CH, CH)
    for frame in range(2):
        mixed = []
        for par in range(2):
            taps = jnp.concatenate([acts[frame + k, par] for k in range(3)], axis=1)
            here = acts[4 + frame, par].astype(F32) + dot(taps, times)
            mixed.append(here.astype(BF16).reshape(COLS, HALF, CH))
        by_row = (row_before(mixed[1]), mixed[0], mixed[1])
        for row in range(3):
            for tap in range(3):
                at = (row * 3 + tap) * 2 * DOWN + frame * DOWN
                for col in range(COLS // 2):
                    rows = pl.ds(at + col * HALF, HALF)
                    where = 2 * col + tap - 1
                    if where < 0:
                        kept_out[rows, :] = jnp.zeros((HALF, CH), BF16)
                    else:
                        kept_out[rows, :] = by_row[row][where]
    loads[1].wait()
    kernel = down_plane[...].reshape(9 * CH, WIDE)
    strided = dot(cells_of(kept_out), kernel).astype(BF16).reshape(2, DOWN, WIDE)
    strided_out[...] = strided
    for half in range(2):
        kept_out[pl.ds(STRIDED_AT + half * DOWN, DOWN), :] = strided[
            0, :, half * CH : (half + 1) * CH
        ]
    loads[2].wait()
    times_out[...] = down_time[...]


def rows_body(rows, last_far, sent_out, last_time, spread, padded, turned, sems):
    loads = start(sems, (0, last_far, last_time))
    cotan = rows[...].astype(F32)
    spread[...] = cotan.reshape(HALF * 8, CH)
    for half in range(2):
        padded[pl.ds(0, DOWN), pl.ds(half * CH, CH)] = spread[pl.ds(half, DOWN, stride=2), :]
    padded[pl.ds(DOWN, 8), :] = jnp.zeros((8, WIDE), F32)
    loads[0].wait()
    total = padded[pl.ds(0, DOWN), :]
    for k in range(3):
        taps = padded[pl.ds(4 * (2 - k), DOWN), :].astype(BF16)
        total = total + dot_nt(taps, last_time[k])
    for half in range(2):
        turned[pl.ds(half, DOWN, stride=2), :] = total[:, half * CH : (half + 1) * CH]
    both = jnp.concatenate([turned[...].reshape(HALF, 8, CH), cotan], axis=1)
    sent_out[...] = both.astype(BF16)


def own_body(
    own_far, plane_far,
    acts_out, pre_out, both_out,
    own, first_plane, cells, windows, sems,
):
    loads = start(sems, (0, own_far, own), (1, plane_far, first_plane))
    both_out[...] = jnp.zeros_like(both_out)
    loads[0].wait()
    for frame in range(2):
        planes = parity_planes(own, frame, cells)
        fill_windows(windows, frame * CELLS, *planes)
        for par in range(2):
            acts_out[2 + frame, par] = planes[par].reshape(CELLS, CH)
    loads[1].wait()
    for tap in range(3):
        for row in range(4):
            at = pl.ds((tap * 4 + row) * CH, CH)
            if row < 3:
                both_out[at, pl.ds(0, CH)] = first_plane[row, tap]
            if row > 0:
                both_out[at, pl.ds(CH, CH)] = first_plane[row - 1, tap]
    for frame in range(2):
        pre = dot(windows[pl.ds(frame * CELLS, CELLS), :], both_out[...])
        hid = (pre * jax.nn.sigmoid(pre)).astype(BF16)
        for par in range(2):
            acts_out[frame, par] = hid[:, par * CH : (par + 1) * CH]
            pre_out[frame, par] = pre[:, par * CH : (par + 1) * CH]


def cotan_body(
    received,
    grad_lowered_out, cot_out,
    spread,
):
    spread[...] = received[...].astype(F32).reshape(HALF * 16, CH)
    for at, out in ((0, grad_lowered_out), (8, cot_out)):
        parts = []
        for col in range(4):
            halves = [
                spread[pl.ds(at + col * 2 + half, HALF, stride=16), :] for half in range(2)
            ]
            parts.append(jnp.concatenate(halves, axis=1))
        out[...] = jnp.concatenate(parts, axis=0).astype(BF16)


def middle_body(prior, own, times, grad_lowered, cot, lowered_out, sent_out):
    pre = dot(prior[0], times[0]) + dot(prior[1], times[1]) + dot(own[0], times[2])
    lowered_out[...] = (pre * jax.nn.sigmoid(pre)).astype(BF16)
    sent_out[pl.ds(0, DOWN), :] = (grad_lowered[...].astype(F32) * silu_slope(pre)).astype(BF16)
    sent_out[pl.ds(DOWN, DOWN), :] = cot[...]


BACK = (
    (0, 0, 0, 0, 1, 1),
    (0, 1, 0, 1, 1, 0),
    (0, 1, 0, 0, 1, 2),
    (1, 0, 1, 0, 0, 1),
    (1, 0, 0, 0, 2, 1),
    (1, 1, 1, 1, 0, 0),
    (1, 1, 1, 0, 0, 2),
    (1, 1, 0, 1, 2, 0),
    (1, 1, 0, 0, 2, 2),
)


def time_grads_body(
    sent, lowered, prior, kept, acts, pre, down_far, plane_far,
    times_out, kernels_out, grads_out, windows_out, slope_out,
    down_plane, sems,
):
    loads = start(sems, (0, down_far, times_out), (1, plane_far, down_plane))
    kernels_out[...] = jnp.zeros_like(kernels_out)
    for frame in range(2):
        planes = [acts[4 + frame, par].reshape(COLS, HALF, CH) for par in range(2)]
        fill_windows(windows_out, frame * CELLS, *planes)
    slope_out[...] = silu_slope(pre[...])
    wide = lowered[...].astype(F32)
    for col in range(4):
        for half in range(2):
            grads_out[pl.ds(LOWERED_AT + col * 2 + half, HALF, stride=8), :] = wide[
                col * HALF : (col + 1) * HALF, half * CH : (half + 1) * CH
            ]
    own = [kept[pl.ds(STRIDED_AT + half * DOWN, DOWN), :] for half in range(2)]
    taps = (prior[0], prior[1], jnp.concatenate(own, axis=1))
    grad_pre = sent[pl.ds(0, DOWN), :]
    for k in range(3):
        down = dot_tn(taps[k], grad_pre)
        for half in range(2):
            lanes = slice(half * CH, (half + 1) * CH)
            grads_out[pl.ds((half * 3 + k) * WIDE, WIDE), :] = down[:, lanes]
    last = dot_tn(lowered[...], sent[pl.ds(DOWN, DOWN), :])
    for half in range(2):
        grads_out[pl.ds((6 + half) * WIDE, WIDE), :] = last[:, half * CH : (half + 1) * CH]
    for load in loads:
        load.wait()
    part = dot_nt(grad_pre, times_out[2])
    for half in range(2):
        grads_out[pl.ds(PART_AT + half * DOWN, DOWN), :] = part[:, half * CH : (half + 1) * CH]
    for row_par, col_par, row_off, col_off, row, tap in BACK:
        rows = pl.ds((row_par * 2 + col_par) * CH, CH)
        lanes = pl.ds((row_off * 2 + col_off) * WIDE, WIDE)
        kernels_out[rows, lanes] = down_plane[row, tap]


def back_body(
    core, ahead, further, grads, times, kernels, kept, acts, windows, slope, lowered, time_far,
    mine_out, other_out,
    shifted, mixed, flat, rows_here, first_time, sems,
):
    loads = start(sems, (0, time_far, first_time))
    near, far = ahead[pl.ds(0, DOWN), :], further[pl.ds(0, DOWN), :]
    part = [grads[pl.ds(PART_AT + half * DOWN, DOWN), :] for half in range(2)]
    strided = [
        jnp.concatenate(part, axis=1) + dot_nt(near, times[0]),
        dot_nt(near, times[1]),
        dot_nt(near, times[2]) + dot_nt(far, times[0]),
        dot_nt(far, times[1]),
    ]
    strided = [frame.astype(BF16) for frame in strided]
    for frame in range(4):
        planes = strided[frame].reshape(4, HALF, WIDE)
        for row_off, rows in ((0, planes), (1, row_after(planes))):
            cells = rows.reshape(DOWN, WIDE)
            here = pl.ds((row_off * 2) * WIDE, WIDE)
            after = pl.ds((row_off * 2 + 1) * WIDE, WIDE)
            shifted[pl.ds(frame * DOWN, DOWN), here] = cells
            shifted[pl.ds(frame * DOWN, DOWN - HALF), after] = cells[HALF:]
            shifted[pl.ds(frame * DOWN + DOWN - HALF, HALF), after] = jnp.zeros((HALF, WIDE), BF16)
    product = dot_nt(shifted[...], kernels[...]).astype(BF16)
    for frame in range(4):
        for par in range(2):
            for col_par in range(2):
                lanes = slice((par * 2 + col_par) * CH, (par * 2 + col_par + 1) * CH)
                for col in range(4):
                    rows = slice(frame * DOWN + col * HALF, frame * DOWN + (col + 1) * HALF)
                    plane = (frame * 2 + par) * COLS + 2 * col + col_par
                    mixed[pl.ds(plane * HALF, HALF), :] = product[rows, lanes]

    loads[0].wait()
    taps = jnp.concatenate([first_time[k] for k in range(3)], axis=1)
    cotans = []
    for frame in range(2):
        parts = []
        for par in range(2):
            frames = [
                mixed[pl.ds(((frame + 2 - k) * 2 + par) * CELLS, CELLS), :] for k in range(3)
            ]
            grad_hidden = dot_nt(jnp.concatenate(frames, axis=1), taps)
            parts.append((grad_hidden * slope[frame, par]).astype(BF16))
        cotans.append(jnp.concatenate(parts, axis=1))
    product = dot_tn(windows[...], jnp.concatenate(cotans, axis=0))
    for row in range(3):
        for tap in range(3):
            at = (tap * 4 + row) * CH
            flat[pl.ds((row * 3 + tap) * CH, CH), :] = (
                product[at : at + CH, :CH] + product[at + CH : at + 2 * CH, CH:]
            )
    cotan = mixed[pl.ds(0, 4 * CELLS), :]
    for k in range(3):
        flat[pl.ds((9 + k) * CH, CH), :] = dot_tn(acts[pl.ds(k, 2)].reshape(4 * CELLS, CH), cotan)
    down = dot_tn(cells_of(kept), jnp.concatenate(strided[:2], axis=0))
    last = [dot_tn(lowered[...], sent[pl.ds(DOWN, DOWN), :]) for sent in (further, ahead)]
    flat[pl.ds(30 * CH, 12 * CH), :] = grads[pl.ds(0, 12 * CH), :]
    for half in range(2):
        lanes = slice(half * CH, (half + 1) * CH)
        flat[pl.ds((12 + half * 9) * CH, 9 * CH), :] = down[:, lanes]
        base = (42 + half * 6) * CH
        for k in range(2):
            flat[pl.ds(base + k * WIDE, WIDE), :] = last[k][:, lanes]
        flat[pl.ds(base + 2 * WIDE, WIDE), :] = grads[pl.ds((6 + half) * WIDE, WIDE), :]

    here = core[0]
    half = GRADS // 2
    mine_out[pl.ds(0, half), :] = flat[pl.ds(pl.multiple_of(here * half, 16), half), :]
    other_out[pl.ds(0, half), :] = flat[
        pl.ds(pl.multiple_of((1 - here) * half, 16), half), :
    ].astype(BF16)
    rows_here[...] = grads[pl.ds(LOWERED_AT, 2 * DOWN), :].reshape(HALF // 2, 2, 8, CH)
    mine_out[pl.ds(half, DOWN), :] = rows_here[:, pl.ds(here, 1)].reshape(DOWN, CH)
    away = rows_here[:, pl.ds(1 - here, 1)].reshape(DOWN, CH)
    other_out[pl.ds(half, DOWN), :] = away.astype(BF16)


def halves_body(core, own, other, half_out, frames_out):
    rows = half_out.shape[0]
    half_out[...] = (own[pl.ds(0, rows), :] + other[pl.ds(0, rows), :].astype(F32)).astype(BF16)
    here = core[0]
    chips = HALF // 2
    mine = own[pl.ds(rows, DOWN), :].reshape(chips, 8, CH)
    theirs = other[pl.ds(rows, DOWN), :].astype(F32).reshape(chips, 8, CH)
    frames = [jnp.where(here == 0, mine, theirs), jnp.where(here == 0, theirs, mine)]
    frames_out[...] = jnp.concatenate(frames, axis=1).astype(BF16)


def sum_body(blocks, frames, sent_out, padded):
    rows = blocks.shape[1]
    total = blocks[0].astype(F32)
    for block in range(1, blocks.shape[0]):
        total = total + blocks[block].astype(F32)
    padded[...] = jnp.zeros_like(padded)
    padded[pl.ds(0, rows), :] = total
    chips = frames.shape[0]
    share = padded.shape[0] // chips
    for chip in range(chips):
        sent_out[chip, pl.ds(0, share), :] = padded[pl.ds(chip * share, share), :].astype(BF16)
        sent_out[chip, pl.ds(share, 16), :] = frames[chip]


def piece_body(received, piece_out):
    share = piece_out.shape[1]
    total = received[0, pl.ds(0, share), :].astype(F32)
    for chip in range(1, received.shape[0]):
        total = total + received[chip, pl.ds(0, share), :].astype(F32)
    piece = total.astype(BF16)
    for chip in range(piece_out.shape[0]):
        piece_out[chip] = piece


def spread_body(pieces, part_out):
    flat = pieces[...].reshape(-1, CH).astype(F32)
    part = flat[: part_out.shape[1]].astype(BF16)
    for block in range(part_out.shape[0]):
        part_out[block] = part


def results_body(core, mine, other, *rest):
    outs, whole = rest[:-1], rest[-1]
    here = core[0]
    half = mine.shape[0]
    whole[pl.ds(pl.multiple_of(here * half, 16), half), :] = mine[...]
    whole[pl.ds(pl.multiple_of((1 - here) * half, 16), half), :] = other[...]
    first = 0
    for out in outs:
        rows, lanes = out.shape
        for part in range(lanes // CH):
            out[:, pl.ds(part * CH, CH)] = whole[pl.ds(first, rows), :]
            first += rows


def output_body(received, last_time, output, spread, padded):
    frames = received[:, pl.ds(received.shape[1] - 16, 16), :]
    spread[...] = frames.astype(F32).reshape(HALF * 8, CH)
    padded[pl.ds(0, 8), :] = jnp.zeros((8, WIDE), F32)
    for half in range(2):
        padded[pl.ds(8, DOWN), pl.ds(half * CH, CH)] = spread[pl.ds(half, DOWN, stride=2), :]
    total = padded[pl.ds(8, DOWN), :]
    for k in range(3):
        taps = padded[pl.ds(4 * k, DOWN), :].astype(BF16)
        total = total + dot(taps, last_time[k])
    output[...] = total.astype(BF16)


def from_behind(block, distance):
    devices = range(lax.axis_size("seq"))
    route = [(i - distance, i) for i in devices if i - distance in devices]
    return lax.ppermute(block, "seq", route)


def swap_cores(block):
    count = lax.axis_size("seq")
    return lax.ppermute(block, "seq", [(i, i ^ 1) for i in range(count)])


def exchange_clip(blocks):
    count = lax.axis_size("clip")
    side = round(count**0.5)
    rows = [list(range(first, first + side)) for first in range(0, count, side)]
    path = [clip for at, row in enumerate(rows) for clip in (row if at % 2 == 0 else row[::-1])]
    return lax.all_to_all(
        blocks, "clip", split_axis=0, concat_axis=0, axis_index_groups=[path], tiled=True
    )


def exchange_seq(blocks):
    return lax.all_to_all(blocks, "seq", split_axis=0, concat_axis=0, tiled=True)


def exchange_chips(blocks):
    count = lax.axis_size("seq")
    groups = [list(range(core, count, 2)) for core in range(2)]
    return lax.all_to_all(
        blocks, "seq", split_axis=0, concat_axis=0, axis_index_groups=groups, tiled=True
    )


def local(clip_in, first_plane, first_time, down_plane, down_time, last_time, cotan_out):
    own = clip_in.reshape(4 * CELLS, CH)
    prior = from_behind(own, 1)
    flat_frames = (2, 2, CELLS, CH)
    core = (lax.axis_index("seq") % 2).astype(jnp.int32).reshape(1)
    (sent,) = call(
        rows_body,
        [(V, cotan_out[0].reshape(HALF, 8, CH)), (H, last_time)],
        [(V, (HALF, 16, CH), BF16)],
        [
            ((3, WIDE, WIDE), BF16),
            ((HALF * 8, CH), F32),
            ((DOWN + 8, WIDE), F32),
            ((HALF * 8, CH), F32),
        ],
        copies=1,
    )
    acts, pre_first, both = call(
        own_body,
        [(H, own), (H, first_plane)],
        [
            (P_, (4, 2, CELLS, CH), BF16),
            (P_, flat_frames, F32),
            (P_, (12 * CH, WIDE), BF16),
        ],
        [
            ((4 * CELLS, CH), BF16),
            ((3, 3, CH, CH), BF16),
            ((2 * CELLS, CH), F32),
            ((2 * CELLS, 12 * CH), BF16),
        ],
        copies=2,
    )
    sent, prior, acts = lax.optimization_barrier((sent, prior, acts))
    received = exchange_seq(sent)
    (acts,) = call(
        prior_body,
        [(P_, prior), (P_, acts), (P_, both)],
        [(P_, (6, 2, CELLS, CH), BF16)],
        [((2 * CELLS, CH), F32), ((2 * CELLS, 12 * CH), BF16)],
    )
    times = (P_, (3, WIDE, WIDE), BF16)
    kept, strided, near_times = call(
        first_body,
        [
            (P_, acts), (H, first_time), (H, down_plane), (H, down_time),
        ],
        [
            (P_, (KEPT, CH), BF16),
            (P_, (2, DOWN, WIDE), BF16),
            times,
        ],
        [
            ((3, CH, CH), BF16),
            ((3, 3, CH, WIDE), BF16),
            ((3, WIDE, WIDE), BF16),
        ],
        copies=3,
    )
    strided_prior = from_behind(strided, 1)
    down = (P_, (DOWN, WIDE), BF16)
    grad_lowered, cot = call(
        cotan_body, [(P_, received)], [down, down], [((HALF * 16, CH), F32)]
    )
    lowered, sent = call(
        middle_body,
        [(P_, strided_prior), (P_, strided), (P_, near_times), (P_, grad_lowered), (P_, cot)],
        [down, (P_, (2 * DOWN, WIDE), BF16)],
    )
    ahead = from_behind(sent, -1)
    further = from_behind(sent, -2)
    all_times, kernels, time_grads, windows, slope = call(
        time_grads_body,
        [
            (P_, sent), (P_, lowered), (P_, strided_prior), (P_, kept), (P_, acts),
            (P_, pre_first), (H, down_time), (H, down_plane),
        ],
        [
            (P_, (3, WIDE, WIDE), BF16),
            (P_, (4 * CH, 4 * WIDE), BF16),
            (P_, (PART_AT + 2 * DOWN, CH), F32),
            (P_, (2 * CELLS, 12 * CH), BF16),
            (P_, flat_frames, F32),
        ],
        [((3, 3, CH, WIDE), BF16)],
        copies=2,
    )
    half_rows = GRADS // 2
    mine, other = call(
        back_body,
        [
            (S, core), (P_, ahead), (P_, further), (P_, time_grads), (P_, all_times),
            (P_, kernels), (P_, kept), (P_, acts), (P_, windows), (P_, slope), (P_, lowered),
            (H, first_time),
        ],
        [(P_, (half_rows + DOWN, CH), F32), (P_, (half_rows + DOWN, CH), BF16)],
        [
            ((4 * DOWN, 4 * WIDE), BF16),
            ((8 * CELLS, CH), BF16),
            ((GRADS, CH), F32),
            ((HALF // 2, 2, 8, CH), F32),
            ((3, CH, CH), BF16),
        ],
        copies=1,
        flops=600000000,
        size=2000000,
    )

    clips = lax.axis_size("clip")
    chips = lax.axis_size("seq") // 2
    part_rows = half_rows // clips
    other = swap_cores(other)
    half, frames = call(
        halves_body,
        [(S, core), (P_, mine), (V, other)],
        [(P_, (half_rows, CH), BF16), (V, (chips, 16, CH), BF16)],
    )
    blocks = exchange_clip(half.reshape(clips, part_rows, CH))
    share = 16 * (-(-part_rows // (16 * chips)))
    (sent,) = call(
        sum_body,
        [(V, blocks), (V, frames)],
        [(V, (chips, share + 16, CH), BF16)],
        [((chips * share, CH), F32)],
    )
    received = exchange_chips(sent)
    (pieces,) = call(piece_body, [(V, received)], [(V, (chips, share, CH), BF16)])
    pieces = exchange_chips(pieces)
    (output,) = call(
        output_body,
        [(V, received), (V, last_time)],
        [(V, (DOWN, WIDE), BF16)],
        [((HALF * 8, CH), F32), ((DOWN + 8, WIDE), F32)],
    )
    (parts,) = call(spread_body, [(V, pieces)], [(V, (clips, part_rows, CH), BF16)])
    half = exchange_clip(parts).reshape(half_rows, CH)
    other = swap_cores(half)
    grads = call(
        results_body,
        [(S, core), (V, half), (V, other)],
        [
            (V, (9 * CH, CH), BF16),
            (V, (3 * CH, CH), BF16),
            (V, (9 * CH, WIDE), BF16),
            (V, (3 * WIDE, WIDE), BF16),
            (V, (3 * WIDE, WIDE), BF16),
        ],
        [((GRADS, CH), BF16)],
    )
    shapes = ((3, 3, CH, CH), (3, CH, CH), (3, 3, CH, WIDE), (3, WIDE, WIDE), (3, WIDE, WIDE))
    grads = [grad.reshape(shape) for grad, shape in zip(grads, shapes)]
    return (output.reshape(1, HALF, 1, 4, WIDE), *grads)


def solution(mesh):
    placed = (
        P("clip", "seq", None, None, None),
        P(),
        P(),
        P(),
        P(),
        P(),
        P("clip", None, "seq", None, None),
    )
    return jax.shard_map(
        local,
        mesh=mesh,
        in_specs=placed,
        out_specs=(P("clip", None, "seq", None, None), P(), P(), P(), P(), P()),
        check_vma=False,
    )
```

```python
import jax
import jax.numpy as jnp
from jax import lax
from jax.experimental import pallas as pl
from jax.experimental.pallas import tpu as pltpu
from jax.sharding import PartitionSpec as P


F32 = jnp.float32
BF16 = jnp.bfloat16
COLS = 8
HALF = 32
CELLS = COLS * HALF
DOWN = CELLS // 2
CH = 128
WIDE = 256
STRIDED_AT = 9 * 2 * DOWN
KEPT = STRIDED_AT + 2 * DOWN
LOWERED_AT = 8 * WIDE
PART_AT = LOWERED_AT + 2 * DOWN
GRADS = (9 + 3 + 18 + 12 + 12) * CH


def dot(left, right):
    return lax.dot_general(left, right, (((1,), (0,)), ((), ())), preferred_element_type=F32)


def dot_nt(left, right):
    return lax.dot_general(left, right, (((1,), (1,)), ((), ())), preferred_element_type=F32)


def dot_tn(left, right):
    return lax.dot_general(left, right, (((0,), (0,)), ((), ())), preferred_element_type=F32)


V, P_, H, S = "vmem", "pinned", "hbm", "smem"
SPACES = {V: pltpu.VMEM, P_: pltpu.VMEM, H: pltpu.HBM, S: pltpu.SMEM}


def placed_input(space, array):
    if space in (P_, H):
        return pltpu.with_memory_space_constraint(array, SPACES[space])
    return array


def placed_output(space, shape, kind):
    if space in (P_, H):
        return SPACES[space](shape, kind)
    return jax.ShapeDtypeStruct(shape, kind)


def call(body, ins, outs, scratch=(), copies=0, flops=1000, size=8000000):
    scratch = [pltpu.VMEM(shape, kind) for shape, kind in scratch]
    if copies:
        scratch.append(pltpu.SemaphoreType.DMA((copies,)))
    return pl.pallas_call(
        body,
        out_shape=[placed_output(*out) for out in outs],
        in_specs=[pl.BlockSpec(memory_space=SPACES[space]) for space, _ in ins],
        out_specs=[pl.BlockSpec(memory_space=SPACES[space]) for space, _, _ in outs],
        scratch_shapes=scratch,
        compiler_params=pltpu.CompilerParams(vmem_limit_bytes=24 * 1024 * 1024),
        cost_estimate=pl.CostEstimate(flops=flops, bytes_accessed=size, transcendentals=0),
    )(*[placed_input(*given) for given in ins])


def start(sems, *pairs):
    copies = [
        pltpu.make_async_copy(source, target, sems.at[at]) for at, source, target in pairs
    ]
    for copy in copies:
        copy.start()
    return copies


def row_before(planes):
    wide = planes.astype(F32)
    rolled = pltpu.roll(wide, 1, 1)
    at = lax.broadcasted_iota(jnp.int32, wide.shape, 1)
    return jnp.where(at == 0, 0.0, rolled).astype(BF16)


def row_after(planes):
    wide = planes.astype(F32)
    rolled = pltpu.roll(wide, HALF - 1, 1)
    at = lax.broadcasted_iota(jnp.int32, wide.shape, 1)
    return jnp.where(at == HALF - 1, 0.0, rolled).astype(BF16)


def fill_windows(windows, at, even, odd):
    by_row = (row_before(odd), even, odd, row_after(even))
    edge = jnp.zeros((HALF, CH), BF16)
    for row, planes in enumerate(by_row):
        flat = planes.reshape(CELLS, CH)
        for tap in range(3):
            lanes = pl.ds((tap * 4 + row) * CH, CH)
            if tap == 0:
                windows[pl.ds(at, HALF), lanes] = edge
                windows[pl.ds(at + HALF, CELLS - HALF), lanes] = flat[: CELLS - HALF]
            elif tap == 1:
                windows[pl.ds(at, CELLS), lanes] = flat
            else:
                windows[pl.ds(at, CELLS - HALF), lanes] = flat[HALF:]
                windows[pl.ds(at + CELLS - HALF, HALF), lanes] = edge


def silu_slope(preact):
    sigma = jax.nn.sigmoid(preact)
    return sigma * (1.0 + preact * (1.0 - sigma))


def parity_planes(source, frame, spread):
    spread[...] = source[pl.ds(frame * 2 * CELLS, 2 * CELLS), :].astype(F32)
    planes = []
    for par in range(2):
        cols = [spread[pl.ds(par * COLS + col, HALF, stride=2 * COLS), :] for col in range(COLS)]
        planes.append(jnp.stack(cols, axis=0).astype(BF16))
    return planes


def cells_of(kept):
    return jnp.concatenate([kept[pl.ds(tap * 2 * DOWN, 2 * DOWN), :] for tap in range(9)], axis=1)


def prior_body(prior, own_acts, both, acts_out, spread, windows):
    for frame in range(2):
        fill_windows(windows, frame * CELLS, *parity_planes(prior, frame, spread))
    acts_out[pl.ds(2, 4)] = own_acts[...]
    for frame in range(2):
        pre = dot(windows[pl.ds(frame * CELLS, CELLS), :], both[...])
        hid = (pre * jax.nn.sigmoid(pre)).astype(BF16)
        for par in range(2):
            acts_out[frame, par] = hid[:, par * CH : (par + 1) * CH]


def first_body(
    acts, time_far, plane_far, down_far,
    kept_out, strided_out, times_out,
    first_time, down_plane, down_time, sems,
):
    loads = start(
        sems, (0, time_far, first_time), (1, plane_far, down_plane), (2, down_far, down_time)
    )
    loads[0].wait()
    times = first_time[...].reshape(3 * CH, CH)
    for frame in range(2):
        mixed = []
        for par in range(2):
            taps = jnp.concatenate([acts[frame + k, par] for k in range(3)], axis=1)
            here = acts[4 + frame, par].astype(F32) + dot(taps, times)
            mixed.append(here.astype(BF16).reshape(COLS, HALF, CH))
        by_row = (row_before(mixed[1]), mixed[0], mixed[1])
        for row in range(3):
            for tap in range(3):
                at = (row * 3 + tap) * 2 * DOWN + frame * DOWN
                for col in range(COLS // 2):
                    rows = pl.ds(at + col * HALF, HALF)
                    where = 2 * col + tap - 1
                    if where < 0:
                        kept_out[rows, :] = jnp.zeros((HALF, CH), BF16)
                    else:
                        kept_out[rows, :] = by_row[row][where]
    loads[1].wait()
    kernel = down_plane[...].reshape(9 * CH, WIDE)
    strided = dot(cells_of(kept_out), kernel).astype(BF16).reshape(2, DOWN, WIDE)
    strided_out[...] = strided
    for half in range(2):
        kept_out[pl.ds(STRIDED_AT + half * DOWN, DOWN), :] = strided[
            0, :, half * CH : (half + 1) * CH
        ]
    loads[2].wait()
    times_out[...] = down_time[...]


def rows_body(rows, last_far, sent_out, last_time, spread, padded, turned, sems):
    loads = start(sems, (0, last_far, last_time))
    cotan = rows[...].astype(F32)
    spread[...] = cotan.reshape(HALF * 8, CH)
    for half in range(2):
        padded[pl.ds(0, DOWN), pl.ds(half * CH, CH)] = spread[pl.ds(half, DOWN, stride=2), :]
    padded[pl.ds(DOWN, 8), :] = jnp.zeros((8, WIDE), F32)
    loads[0].wait()
    total = padded[pl.ds(0, DOWN), :]
    for k in range(3):
        taps = padded[pl.ds(4 * (2 - k), DOWN), :].astype(BF16)
        total = total + dot_nt(taps, last_time[k])
    for half in range(2):
        turned[pl.ds(half, DOWN, stride=2), :] = total[:, half * CH : (half + 1) * CH]
    both = jnp.concatenate([turned[...].reshape(HALF, 8, CH), cotan], axis=1)
    sent_out[...] = both.astype(BF16)


def own_body(
    own_far, plane_far,
    acts_out, pre_out, both_out,
    own, first_plane, cells, windows, sems,
):
    loads = start(sems, (0, own_far, own), (1, plane_far, first_plane))
    both_out[...] = jnp.zeros_like(both_out)
    loads[0].wait()
    for frame in range(2):
        planes = parity_planes(own, frame, cells)
        fill_windows(windows, frame * CELLS, *planes)
        for par in range(2):
            acts_out[2 + frame, par] = planes[par].reshape(CELLS, CH)
    loads[1].wait()
    for tap in range(3):
        for row in range(4):
            at = pl.ds((tap * 4 + row) * CH, CH)
            if row < 3:
                both_out[at, pl.ds(0, CH)] = first_plane[row, tap]
            if row > 0:
                both_out[at, pl.ds(CH, CH)] = first_plane[row - 1, tap]
    for frame in range(2):
        pre = dot(windows[pl.ds(frame * CELLS, CELLS), :], both_out[...])
        hid = (pre * jax.nn.sigmoid(pre)).astype(BF16)
        for par in range(2):
            acts_out[frame, par] = hid[:, par * CH : (par + 1) * CH]
            pre_out[frame, par] = pre[:, par * CH : (par + 1) * CH]


def cotan_body(
    received,
    grad_lowered_out, cot_out,
    spread,
):
    spread[...] = received[...].astype(F32).reshape(HALF * 16, CH)
    for at, out in ((0, grad_lowered_out), (8, cot_out)):
        parts = []
        for col in range(4):
            halves = [
                spread[pl.ds(at + col * 2 + half, HALF, stride=16), :] for half in range(2)
            ]
            parts.append(jnp.concatenate(halves, axis=1))
        out[...] = jnp.concatenate(parts, axis=0).astype(BF16)


def middle_body(prior, own, times, grad_lowered, cot, lowered_out, sent_out):
    pre = dot(prior[0], times[0]) + dot(prior[1], times[1]) + dot(own[0], times[2])
    lowered_out[...] = (pre * jax.nn.sigmoid(pre)).astype(BF16)
    sent_out[pl.ds(0, DOWN), :] = (grad_lowered[...].astype(F32) * silu_slope(pre)).astype(BF16)
    sent_out[pl.ds(DOWN, DOWN), :] = cot[...]


BACK = (
    (0, 0, 0, 0, 1, 1),
    (0, 1, 0, 1, 1, 0),
    (0, 1, 0, 0, 1, 2),
    (1, 0, 1, 0, 0, 1),
    (1, 0, 0, 0, 2, 1),
    (1, 1, 1, 1, 0, 0),
    (1, 1, 1, 0, 0, 2),
    (1, 1, 0, 1, 2, 0),
    (1, 1, 0, 0, 2, 2),
)


def time_grads_body(
    sent, lowered, prior, kept, acts, pre, down_far, plane_far,
    times_out, kernels_out, grads_out, windows_out, slope_out,
    down_plane, sems,
):
    loads = start(sems, (0, down_far, times_out), (1, plane_far, down_plane))
    kernels_out[...] = jnp.zeros_like(kernels_out)
    for frame in range(2):
        planes = [acts[4 + frame, par].reshape(COLS, HALF, CH) for par in range(2)]
        fill_windows(windows_out, frame * CELLS, *planes)
    slope_out[...] = silu_slope(pre[...])
    wide = lowered[...].astype(F32)
    for col in range(4):
        for half in range(2):
            grads_out[pl.ds(LOWERED_AT + col * 2 + half, HALF, stride=8), :] = wide[
                col * HALF : (col + 1) * HALF, half * CH : (half + 1) * CH
            ]
    own = [kept[pl.ds(STRIDED_AT + half * DOWN, DOWN), :] for half in range(2)]
    taps = (prior[0], prior[1], jnp.concatenate(own, axis=1))
    grad_pre = sent[pl.ds(0, DOWN), :]
    for k in range(3):
        down = dot_tn(taps[k], grad_pre)
        for half in range(2):
            lanes = slice(half * CH, (half + 1) * CH)
            grads_out[pl.ds((half * 3 + k) * WIDE, WIDE), :] = down[:, lanes]
    last = dot_tn(lowered[...], sent[pl.ds(DOWN, DOWN), :])
    for half in range(2):
        grads_out[pl.ds((6 + half) * WIDE, WIDE), :] = last[:, half * CH : (half + 1) * CH]
    for load in loads:
        load.wait()
    part = dot_nt(grad_pre, times_out[2])
    for half in range(2):
        grads_out[pl.ds(PART_AT + half * DOWN, DOWN), :] = part[:, half * CH : (half + 1) * CH]
    for row_par, col_par, row_off, col_off, row, tap in BACK:
        rows = pl.ds((row_par * 2 + col_par) * CH, CH)
        lanes = pl.ds((row_off * 2 + col_off) * WIDE, WIDE)
        kernels_out[rows, lanes] = down_plane[row, tap]


def back_body(
    core, ahead, further, grads, times, kernels, kept, acts, windows, slope, lowered, time_far,
    mine_out, other_out,
    shifted, mixed, flat, rows_here, first_time, sems,
):
    loads = start(sems, (0, time_far, first_time))
    near, far = ahead[pl.ds(0, DOWN), :], further[pl.ds(0, DOWN), :]
    part = [grads[pl.ds(PART_AT + half * DOWN, DOWN), :] for half in range(2)]
    strided = [
        jnp.concatenate(part, axis=1) + dot_nt(near, times[0]),
        dot_nt(near, times[1]),
        dot_nt(near, times[2]) + dot_nt(far, times[0]),
        dot_nt(far, times[1]),
    ]
    strided = [frame.astype(BF16) for frame in strided]
    for frame in range(4):
        planes = strided[frame].reshape(4, HALF, WIDE)
        for row_off, rows in ((0, planes), (1, row_after(planes))):
            cells = rows.reshape(DOWN, WIDE)
            here = pl.ds((row_off * 2) * WIDE, WIDE)
            after = pl.ds((row_off * 2 + 1) * WIDE, WIDE)
            shifted[pl.ds(frame * DOWN, DOWN), here] = cells
            shifted[pl.ds(frame * DOWN, DOWN - HALF), after] = cells[HALF:]
            shifted[pl.ds(frame * DOWN + DOWN - HALF, HALF), after] = jnp.zeros((HALF, WIDE), BF16)
    product = dot_nt(shifted[...], kernels[...]).astype(BF16)
    for frame in range(4):
        for par in range(2):
            for col_par in range(2):
                lanes = slice((par * 2 + col_par) * CH, (par * 2 + col_par + 1) * CH)
                for col in range(4):
                    rows = slice(frame * DOWN + col * HALF, frame * DOWN + (col + 1) * HALF)
                    plane = (frame * 2 + par) * COLS + 2 * col + col_par
                    mixed[pl.ds(plane * HALF, HALF), :] = product[rows, lanes]

    loads[0].wait()
    taps = jnp.concatenate([first_time[k] for k in range(3)], axis=1)
    cotans = []
    for frame in range(2):
        parts = []
        for par in range(2):
            frames = [
                mixed[pl.ds(((frame + 2 - k) * 2 + par) * CELLS, CELLS), :] for k in range(3)
            ]
            grad_hidden = dot_nt(jnp.concatenate(frames, axis=1), taps)
            parts.append((grad_hidden * slope[frame, par]).astype(BF16))
        cotans.append(jnp.concatenate(parts, axis=1))
    product = dot_tn(windows[...], jnp.concatenate(cotans, axis=0))
    for row in range(3):
        for tap in range(3):
            at = (tap * 4 + row) * CH
            flat[pl.ds((row * 3 + tap) * CH, CH), :] = (
                product[at : at + CH, :CH] + product[at + CH : at + 2 * CH, CH:]
            )
    cotan = mixed[pl.ds(0, 4 * CELLS), :]
    for k in range(3):
        flat[pl.ds((9 + k) * CH, CH), :] = dot_tn(acts[pl.ds(k, 2)].reshape(4 * CELLS, CH), cotan)
    down = dot_tn(cells_of(kept), jnp.concatenate(strided[:2], axis=0))
    last = [dot_tn(lowered[...], sent[pl.ds(DOWN, DOWN), :]) for sent in (further, ahead)]
    flat[pl.ds(30 * CH, 12 * CH), :] = grads[pl.ds(0, 12 * CH), :]
    for half in range(2):
        lanes = slice(half * CH, (half + 1) * CH)
        flat[pl.ds((12 + half * 9) * CH, 9 * CH), :] = down[:, lanes]
        base = (42 + half * 6) * CH
        for k in range(2):
            flat[pl.ds(base + k * WIDE, WIDE), :] = last[k][:, lanes]
        flat[pl.ds(base + 2 * WIDE, WIDE), :] = grads[pl.ds((6 + half) * WIDE, WIDE), :]

    here = core[0]
    half = GRADS // 2
    mine_out[pl.ds(0, half), :] = flat[pl.ds(pl.multiple_of(here * half, 16), half), :]
    other_out[pl.ds(0, half), :] = flat[
        pl.ds(pl.multiple_of((1 - here) * half, 16), half), :
    ].astype(BF16)
    rows_here[...] = grads[pl.ds(LOWERED_AT, 2 * DOWN), :].reshape(HALF // 2, 2, 8, CH)
    mine_out[pl.ds(half, DOWN), :] = rows_here[:, pl.ds(here, 1)].reshape(DOWN, CH)
    away = rows_here[:, pl.ds(1 - here, 1)].reshape(DOWN, CH)
    other_out[pl.ds(half, DOWN), :] = away.astype(BF16)


def halves_body(core, own, other, half_out, frames_out):
    rows = half_out.shape[0]
    half_out[...] = (own[pl.ds(0, rows), :] + other[pl.ds(0, rows), :].astype(F32)).astype(BF16)
    here = core[0]
    chips = HALF // 2
    mine = own[pl.ds(rows, DOWN), :].reshape(chips, 8, CH)
    theirs = other[pl.ds(rows, DOWN), :].astype(F32).reshape(chips, 8, CH)
    frames = [jnp.where(here == 0, mine, theirs), jnp.where(here == 0, theirs, mine)]
    frames_out[...] = jnp.concatenate(frames, axis=1).astype(BF16)


def sum_body(blocks, frames, sent_out, padded):
    rows = blocks.shape[1]
    total = blocks[0].astype(F32)
    for block in range(1, blocks.shape[0]):
        total = total + blocks[block].astype(F32)
    padded[...] = jnp.zeros_like(padded)
    padded[pl.ds(0, rows), :] = total
    chips = frames.shape[0]
    share = padded.shape[0] // chips
    for chip in range(chips):
        sent_out[chip, pl.ds(0, share), :] = padded[pl.ds(chip * share, share), :].astype(BF16)
        sent_out[chip, pl.ds(share, 16), :] = frames[chip]


def piece_body(received, piece_out):
    share = piece_out.shape[1]
    total = received[0, pl.ds(0, share), :].astype(F32)
    for chip in range(1, received.shape[0]):
        total = total + received[chip, pl.ds(0, share), :].astype(F32)
    piece = total.astype(BF16)
    for chip in range(piece_out.shape[0]):
        piece_out[chip] = piece


def spread_body(pieces, part_out):
    flat = pieces[...].reshape(-1, CH).astype(F32)
    part = flat[: part_out.shape[1]].astype(BF16)
    for block in range(part_out.shape[0]):
        part_out[block] = part


def results_body(core, mine, other, *rest):
    outs, whole = rest[:-1], rest[-1]
    here = core[0]
    half = mine.shape[0]
    whole[pl.ds(pl.multiple_of(here * half, 16), half), :] = mine[...]
    whole[pl.ds(pl.multiple_of((1 - here) * half, 16), half), :] = other[...]
    first = 0
    for out in outs:
        rows, lanes = out.shape
        for part in range(lanes // CH):
            out[:, pl.ds(part * CH, CH)] = whole[pl.ds(first, rows), :]
            first += rows


def output_body(received, last_time, output, spread, padded):
    frames = received[:, pl.ds(received.shape[1] - 16, 16), :]
    spread[...] = frames.astype(F32).reshape(HALF * 8, CH)
    padded[pl.ds(0, 8), :] = jnp.zeros((8, WIDE), F32)
    for half in range(2):
        padded[pl.ds(8, DOWN), pl.ds(half * CH, CH)] = spread[pl.ds(half, DOWN, stride=2), :]
    total = padded[pl.ds(8, DOWN), :]
    for k in range(3):
        taps = padded[pl.ds(4 * k, DOWN), :].astype(BF16)
        total = total + dot(taps, last_time[k])
    output[...] = total.astype(BF16)


def from_behind(block, distance):
    devices = range(lax.axis_size("seq"))
    route = [(i - distance, i) for i in devices if i - distance in devices]
    return lax.ppermute(block, "seq", route)


def swap_cores(block):
    count = lax.axis_size("seq")
    return lax.ppermute(block, "seq", [(i, i ^ 1) for i in range(count)])


def exchange_clip(blocks):
    count = lax.axis_size("clip")
    side = round(count**0.5)
    path = [row * side + (row + shift) % side for shift in range(side) for row in range(side)]
    return lax.all_to_all(
        blocks, "clip", split_axis=0, concat_axis=0, axis_index_groups=[path], tiled=True
    )


def exchange_seq(blocks):
    return lax.all_to_all(blocks, "seq", split_axis=0, concat_axis=0, tiled=True)


def exchange_chips(blocks):
    count = lax.axis_size("seq")
    groups = [list(range(core, count, 2)) for core in range(2)]
    return lax.all_to_all(
        blocks, "seq", split_axis=0, concat_axis=0, axis_index_groups=groups, tiled=True
    )


def local(clip_in, first_plane, first_time, down_plane, down_time, last_time, cotan_out):
    own = clip_in.reshape(4 * CELLS, CH)
    prior = from_behind(own, 1)
    flat_frames = (2, 2, CELLS, CH)
    core = (lax.axis_index("seq") % 2).astype(jnp.int32).reshape(1)
    (sent,) = call(
        rows_body,
        [(V, cotan_out[0].reshape(HALF, 8, CH)), (H, last_time)],
        [(V, (HALF, 16, CH), BF16)],
        [
            ((3, WIDE, WIDE), BF16),
            ((HALF * 8, CH), F32),
            ((DOWN + 8, WIDE), F32),
            ((HALF * 8, CH), F32),
        ],
        copies=1,
    )
    acts, pre_first, both = call(
        own_body,
        [(H, own), (H, first_plane)],
        [
            (P_, (4, 2, CELLS, CH), BF16),
            (P_, flat_frames, F32),
            (P_, (12 * CH, WIDE), BF16),
        ],
        [
            ((4 * CELLS, CH), BF16),
            ((3, 3, CH, CH), BF16),
            ((2 * CELLS, CH), F32),
            ((2 * CELLS, 12 * CH), BF16),
        ],
        copies=2,
    )
    sent, prior, acts = lax.optimization_barrier((sent, prior, acts))
    received = exchange_seq(sent)
    (acts,) = call(
        prior_body,
        [(P_, prior), (P_, acts), (P_, both)],
        [(P_, (6, 2, CELLS, CH), BF16)],
        [((2 * CELLS, CH), F32), ((2 * CELLS, 12 * CH), BF16)],
    )
    times = (P_, (3, WIDE, WIDE), BF16)
    kept, strided, near_times = call(
        first_body,
        [
            (P_, acts), (H, first_time), (H, down_plane), (H, down_time),
        ],
        [
            (P_, (KEPT, CH), BF16),
            (P_, (2, DOWN, WIDE), BF16),
            times,
        ],
        [
            ((3, CH, CH), BF16),
            ((3, 3, CH, WIDE), BF16),
            ((3, WIDE, WIDE), BF16),
        ],
        copies=3,
    )
    strided_prior = from_behind(strided, 1)
    down = (P_, (DOWN, WIDE), BF16)
    grad_lowered, cot = call(
        cotan_body, [(P_, received)], [down, down], [((HALF * 16, CH), F32)]
    )
    lowered, sent = call(
        middle_body,
        [(P_, strided_prior), (P_, strided), (P_, near_times), (P_, grad_lowered), (P_, cot)],
        [down, (P_, (2 * DOWN, WIDE), BF16)],
    )
    ahead = from_behind(sent, -1)
    further = from_behind(sent, -2)
    all_times, kernels, time_grads, windows, slope = call(
        time_grads_body,
        [
            (P_, sent), (P_, lowered), (P_, strided_prior), (P_, kept), (P_, acts),
            (P_, pre_first), (H, down_time), (H, down_plane),
        ],
        [
            (P_, (3, WIDE, WIDE), BF16),
            (P_, (4 * CH, 4 * WIDE), BF16),
            (P_, (PART_AT + 2 * DOWN, CH), F32),
            (P_, (2 * CELLS, 12 * CH), BF16),
            (P_, flat_frames, F32),
        ],
        [((3, 3, CH, WIDE), BF16)],
        copies=2,
    )
    half_rows = GRADS // 2
    mine, other = call(
        back_body,
        [
            (S, core), (P_, ahead), (P_, further), (P_, time_grads), (P_, all_times),
            (P_, kernels), (P_, kept), (P_, acts), (P_, windows), (P_, slope), (P_, lowered),
            (H, first_time),
        ],
        [(P_, (half_rows + DOWN, CH), F32), (P_, (half_rows + DOWN, CH), BF16)],
        [
            ((4 * DOWN, 4 * WIDE), BF16),
            ((8 * CELLS, CH), BF16),
            ((GRADS, CH), F32),
            ((HALF // 2, 2, 8, CH), F32),
            ((3, CH, CH), BF16),
        ],
        copies=1,
        flops=600000000,
        size=2000000,
    )

    clips = lax.axis_size("clip")
    chips = lax.axis_size("seq") // 2
    part_rows = half_rows // clips
    other = swap_cores(other)
    half, frames = call(
        halves_body,
        [(S, core), (P_, mine), (V, other)],
        [(P_, (half_rows, CH), BF16), (V, (chips, 16, CH), BF16)],
    )
    blocks = exchange_clip(half.reshape(clips, part_rows, CH))
    share = 16 * (-(-part_rows // (16 * chips)))
    (sent,) = call(
        sum_body,
        [(V, blocks), (V, frames)],
        [(V, (chips, share + 16, CH), BF16)],
        [((chips * share, CH), F32)],
    )
    received = exchange_chips(sent)
    (pieces,) = call(piece_body, [(V, received)], [(V, (chips, share, CH), BF16)])
    pieces = exchange_chips(pieces)
    (output,) = call(
        output_body,
        [(V, received), (V, last_time)],
        [(V, (DOWN, WIDE), BF16)],
        [((HALF * 8, CH), F32), ((DOWN + 8, WIDE), F32)],
    )
    (parts,) = call(spread_body, [(V, pieces)], [(V, (clips, part_rows, CH), BF16)])
    half = exchange_clip(parts).reshape(half_rows, CH)
    other = swap_cores(half)
    grads = call(
        results_body,
        [(S, core), (V, half), (V, other)],
        [
            (V, (9 * CH, CH), BF16),
            (V, (3 * CH, CH), BF16),
            (V, (9 * CH, WIDE), BF16),
            (V, (3 * WIDE, WIDE), BF16),
            (V, (3 * WIDE, WIDE), BF16),
        ],
        [((GRADS, CH), BF16)],
    )
    shapes = ((3, 3, CH, CH), (3, CH, CH), (3, 3, CH, WIDE), (3, WIDE, WIDE), (3, WIDE, WIDE))
    grads = [grad.reshape(shape) for grad, shape in zip(grads, shapes)]
    return (output.reshape(1, HALF, 1, 4, WIDE), *grads)


def solution(mesh):
    placed = (
        P("clip", "seq", None, None, None),
        P(),
        P(),
        P(),
        P(),
        P(),
        P("clip", None, "seq", None, None),
    )
    return jax.shard_map(
        local,
        mesh=mesh,
        in_specs=placed,
        out_specs=(P("clip", None, "seq", None, None), P(), P(), P(), P(), P()),
        check_vma=False,
    )
```
